32 devices in a mesh: groups: 2 (over y), tp: 8 (over z, x), sub: 2 (over core).
Axes of the slice: x: 2, y: 2, z: 4, core: 2. Of those that a mesh axis runs over, the one named last changes fastest.
Arguments:
- queries: bfloat16 [4, 32, 64, 576], P(('groups', 'sub'), 'tp'), parts along dimension 0, may hold values from -48 to 48
- kv_cache: bfloat16 [4, 32, 256, 576], P(('groups', 'sub'), 'tp'), parts along dimension 0, may hold values from -6 to 6
- cache_lengths: int32 [4, 32], P(('groups', 'sub'), 'tp'), parts along dimension 0, may hold values from 1 to 256, as said below
- live_counts: int32 [4, 8], P(('groups', 'sub')), parts along dimension 0, may hold values from 0 to 4, as said below
- stream: bfloat16 [4, 32, 7168], P(('groups', 'sub'), 'tp'), parts along dimension 0, may hold values from -6 to 6
- norm_gain: float32 [7168], replicated, may hold values from 0.1 to 1.9
- w_gate: bfloat16 [9216, 7168], P('tp'), may hold values from -0.0625 to 0.0625
- w_up: bfloat16 [9216, 7168], P('tp'), may hold values from -0.0625 to 0.0625
- w_down: bfloat16 [9216, 7168], P('tp'), may hold values from -0.0625 to 0.0625
Outputs:
- latent_ctx: bfloat16 [4, 32, 64, 512], P(('groups', 'sub'), 'tp'), parts along dimension 0
- layer_out: bfloat16 [4, 8, 7168], P(('groups', 'sub'), 'tp'), parts along dimension 0
The draws below stay inside these ranges and needn't reach their ends.
There are 2 independent parts, one for each index of `groups`. The reference program is written for one: setup_inputs(seed, part) draws one part's arguments, and reference() takes and returns one part's arrays. A program takes and returns all parts, laid end to end along the dimension named above; an argument that names none is the same for every part. Nothing has to cross between parts.
Inputs may be any that keep to these rules, and one draw needn't show every extreme that they name: `live_counts`: in each sub-batch the counts add up to 8; some device holds 4 live slots. `cache_lengths`: every device has a slot of length 256.
All inputs are finite; a program needn't handle non-finite values.
Results may differ from the reference program's by a relative error of at most 0.0051.
Values may be sent and summed in bfloat16 or wider, within the bound.
No kernel may reach another device: no remote copies, remote signals or barrier semaphores. Data moves between devices by JAX's collectives and lax.ppermute only.
A program may use at most 128 MiB of HBM per device.

```python
import jax
import jax.numpy as jnp
from jax import lax

D = 7168
FF = 9216
H = 64
KVL = 512
QKD = 576
SLOTS = 4
POS = 256
N_TP = 8
N_SUB = 2


def first_entries(key):
    return jnp.clip(jax.random.normal(jax.random.fold_in(key, 12), (N_SUB, N_TP * SLOTS, 1, QKD), jnp.float32), -6.0, 6.0)


def draw_kv_cache(key, part):
    leading = first_entries(key)
    key = jax.random.fold_in(key, 2)
    others = jnp.clip(jax.random.normal(key, (N_SUB, N_TP * SLOTS, POS, QKD), jnp.float32), -6.0, 6.0)
    return jnp.concatenate([leading, others[:, :, 1:, :]], axis=2).astype(jnp.bfloat16)


def draw_queries(key, part):
    key = jax.random.fold_in(key, 5)
    key_a = jax.random.fold_in(key, 0)
    fresh = jnp.clip(jax.random.normal(key_a, (N_SUB, N_TP * SLOTS, H, QKD), jnp.float32), -6.0, 6.0)
    return fresh.astype(jnp.bfloat16)


def draw_cache_lengths(key, part):
    key = jax.random.fold_in(key, 4)
    key_a, key_b = jax.random.split(key)
    lengths = jax.random.randint(key_a, (N_SUB, N_TP, SLOTS), 1, POS + 1)
    longest = jax.random.randint(key_b, (N_SUB, N_TP, 1), 0, SLOTS)
    marked = jnp.arange(SLOTS, dtype=jnp.int32)[None, None, :] == longest
    return jnp.where(marked, POS, lengths).reshape(N_SUB, N_TP * SLOTS).astype(jnp.int32)


def draw_live_counts(key, part):
    key = jax.random.fold_in(key, 3)
    ranks = jnp.stack([jax.random.permutation(jax.random.fold_in(key, sub_idx), N_TP) for sub_idx in range(N_SUB)])
    heavy = N_TP // 8
    counts = jnp.where(ranks < heavy, SLOTS, jnp.where(ranks < SLOTS * heavy, 0, 1))
    return counts.astype(jnp.int32)


def shard_levels(key, dims, cuts, least, high):
    loudness = 1.0
    for dim, blocks in cuts:
        draws = jax.random.uniform(jax.random.fold_in(jax.random.fold_in(key, 6), dim), (blocks,), jnp.float32, least / len(cuts), high / len(cuts))
        loudness = loudness * jnp.repeat(jnp.exp(draws), dims[dim] // blocks).reshape((-1,) + (1,) * (len(dims) - 1 - dim))
    return loudness


def normal_values(own_key, dims, spread, limit, pieces=(), kind=jnp.bfloat16):
    result = jax.random.normal(own_key, dims, jnp.float32) * spread
    if len(pieces) > 0:
        result = shard_levels(own_key, dims, pieces, -0.22, 0.18) * result
    return jnp.clip(result, min=-limit, max=limit).astype(kind)


def setup_inputs(seed: int = 0, part: int = 0) -> dict:
    seeds = jax.random.split(jax.random.key(seed), 10)
    part_splits = jax.random.split(jax.random.fold_in(seeds[9], part), 10)
    queries = draw_queries(jax.random.fold_in(jax.random.fold_in(seeds[9], part), 71), part)
    kv_cache = draw_kv_cache(jax.random.fold_in(jax.random.fold_in(seeds[9], part), 71), part)
    cache_lengths = draw_cache_lengths(jax.random.fold_in(jax.random.fold_in(seeds[9], part), 71), part)
    live_counts = draw_live_counts(jax.random.fold_in(jax.random.fold_in(seeds[9], part), 71), part)
    stream = normal_values(part_splits[4], (N_SUB, N_TP * SLOTS, D), 1.0, 6.0, ((0, 2), (1, 8)))
    norm_gain = jnp.clip(1.0 + 0.18 * jax.random.normal(seeds[5], (D,), jnp.float32), 0.1, 1.9)
    w_gate = normal_values(seeds[6], (FF, D), D ** -0.5, 0.0625, ((0, 8),))
    w_up = normal_values(seeds[7], (FF, D), D ** -0.5, 0.0625, ((0, 8),))
    w_down = normal_values(seeds[8], (FF, D), FF ** -0.5, 0.0625, ((0, 8),))
    return dict(queries=queries, kv_cache=kv_cache, cache_lengths=cache_lengths, live_counts=live_counts, stream=stream, norm_gain=norm_gain, w_gate=w_gate, w_up=w_up, w_down=w_down)


score_scale = 192.0 ** (-0.5)
norm_eps = 1e-06

def token_rows(counts_row, slot_count):
    run_ends = jnp.cumsum(counts_row).astype(jnp.int32)
    starts = (run_ends - counts_row).astype(jnp.int32)
    positions = jnp.arange(counts_row.shape[0], dtype=jnp.int32)
    owners = lax.optimization_barrier(jnp.sum((run_ends[None, :] <= positions[:, None]).astype(jnp.int32), axis=1)).astype(jnp.int32)
    places = (positions - starts[owners]).astype(jnp.int32)
    return (owners * slot_count + places).astype(jnp.int32)

def attend(queries_s, cache_s, lengths, in_use):
    scores = jnp.einsum('shd,spd->shp', queries_s.astype(jnp.float32), cache_s.astype(jnp.float32)) * score_scale
    visible = jnp.arange(cache_s.shape[1], dtype=jnp.int32)[None, None, :] < lengths[:, None, None]
    scores = jnp.where(visible, scores, -jnp.inf)
    row_max = lax.optimization_barrier(jnp.max(scores, axis=2, keepdims=True))
    weights = jnp.exp(scores - row_max)
    weights_bf = (weights / lax.optimization_barrier(jnp.sum(weights, axis=2, keepdims=True))).astype(jnp.bfloat16)
    values = cache_s[:, :, :KVL]
    context = jnp.einsum('shp,spd->shd', weights_bf.astype(jnp.float32), values.astype(jnp.float32))
    return jnp.where(in_use[:, None, None], context, 0.0).astype(jnp.bfloat16)

def feed_forward(rows_in, norm_gain, w_gate, w_up, w_down):
    widened = rows_in.astype(jnp.float32)
    inv_rms = lax.rsqrt(lax.optimization_barrier(jnp.mean(widened * widened, axis=1, keepdims=True)) + norm_eps)
    normed = (widened * inv_rms * norm_gain.astype(jnp.float32)).astype(jnp.bfloat16)
    contract = (((1,), (1,)), ((), ()))
    gate_out = lax.dot_general(normed, w_gate, contract, preferred_element_type=jnp.float32)
    up_out = lax.dot_general(normed, w_up, contract, preferred_element_type=jnp.float32)
    hidden = (jax.nn.silu(gate_out) * up_out).astype(jnp.bfloat16)
    down_sum = jnp.dot(hidden, w_down, preferred_element_type=jnp.float32)
    return (down_sum + widened).astype(jnp.bfloat16)

def reference(queries, kv_cache, cache_lengths, live_counts, stream, norm_gain, w_gate, w_up, w_down):
    sub_count = cache_lengths.shape[0]
    slot_rows = cache_lengths.shape[1]
    slot_index = jnp.arange(slot_rows, dtype=jnp.int32) % SLOTS
    in_use = slot_index[None, :] < jnp.repeat(live_counts, SLOTS, axis=1)
    blocks = sub_count * slot_rows // SLOTS

    def per_block(packed):
        return attend(packed[0], packed[1], packed[2], packed[3])
    latent_ctx = lax.map(per_block, (queries.reshape(blocks, SLOTS, H, QKD), kv_cache.reshape(blocks, SLOTS, POS, QKD), cache_lengths.reshape(blocks, SLOTS), in_use.reshape(blocks, SLOTS)))
    latent_ctx = latent_ctx.reshape(sub_count, slot_rows, H, KVL)
    outputs = []
    for sub_idx in range(sub_count):
        picked = token_rows(live_counts[sub_idx], SLOTS)
        rows_in = jnp.take(stream[sub_idx], picked, axis=0)
        outputs.append(feed_forward(rows_in, norm_gain, w_gate, w_up, w_down))
    return (latent_ctx, jnp.stack(outputs))
```

```python
import jax
import jax.numpy as jnp
from jax import lax
from jax.experimental import pallas as pl
from jax.experimental.pallas import tpu as pltpu
from jax.sharding import PartitionSpec as P

KVL = 512
MIB = 1024 * 1024

score_scale = 192.0 ** (-0.5)
norm_eps = 1e-06


def bit_reverse(value, bits):
    out = 0
    for bit in range(bits):
        out |= ((value >> bit) & 1) << (bits - 1 - bit)
    return out


def swap(x, bit, size):
    return lax.ppermute(x, "tp", [(i, i ^ (1 << bit)) for i in range(size)])


def attend(queries_s, cache_s, lengths, in_use):
    scores = (
        jnp.einsum("shd,spd->shp", queries_s, cache_s, preferred_element_type=jnp.float32)
        * score_scale
    )
    visible = jnp.arange(cache_s.shape[1], dtype=jnp.int32)[None, None, :] < lengths[:, None, None]
    scores = jnp.where(visible, scores, -jnp.inf)
    row_max = jnp.max(scores, axis=2, keepdims=True)
    weights = jnp.exp(scores - row_max)
    weights_bf = (weights / jnp.sum(weights, axis=2, keepdims=True)).astype(jnp.bfloat16)
    values = cache_s[:, :, :KVL]
    context = jnp.einsum("shp,spd->shd", weights_bf, values, preferred_element_type=jnp.float32)
    return jnp.where(in_use[:, None, None], context, 0.0).astype(jnp.bfloat16)


def pick_matrix(counts_row, device, size, slots, bits):
    order = jnp.array([bit_reverse(p, bits) for p in range(size)], jnp.int32)
    owner = (order ^ device)[:, None]
    every = jnp.arange(size, dtype=jnp.int32)[None, :]
    start = jnp.sum(jnp.where(every < owner, counts_row[None, :], 0), axis=1)
    count = jnp.sum(jnp.where(every == owner, counts_row[None, :], 0), axis=1)
    place = jnp.arange(slots, dtype=jnp.int32)[None, :]
    request = jnp.where(place < count[:, None], start[:, None] + place, -1)
    return (request[None] == (order ^ device)[:, None, None]).astype(jnp.bfloat16).reshape(size, size * slots)


def load_rows(weight, first, rows, after):
    pieces = 4 if rows % 64 == 0 else 1
    step = rows // pieces

    def body(weight_ref, after_ref, out_ref, sems):
        copies = [
            pltpu.make_async_copy(
                weight_ref.at[pl.ds(first + i * step, step)], out_ref.at[pl.ds(i * step, step)], sems.at[i]
            )
            for i in range(pieces)
        ]
        for copy in copies:
            copy.start()
        for copy in copies:
            copy.wait()

    return pl.pallas_call(
        body,
        out_shape=pltpu.VMEM((rows, weight.shape[1]), weight.dtype),
        in_specs=[pl.BlockSpec(memory_space=pl.ANY)] * 2,
        out_specs=pl.BlockSpec(memory_space=pltpu.VMEM),
        scratch_shapes=[pltpu.SemaphoreType.DMA((pieces,))],
        compiler_params=pltpu.CompilerParams(vmem_limit_bytes=2 * MIB),
        cost_estimate=pl.CostEstimate(
            flops=0, transcendentals=0, bytes_accessed=2 * rows * weight.shape[1] * 2
        ),
        name="load_rows",
    )(pltpu.with_memory_space_constraint(weight, pltpu.HBM), after)


def feed_forward(pick, gain, blocks, gate_parts, up_parts, w_up, w_down):
    requests = pick.shape[0]
    units, width = w_down.shape
    block_count, gate_count, up_count = len(blocks), len(gate_parts), len(up_parts)
    loaded = sum(part.shape[0] for part in up_parts)
    late = units - loaded
    half = requests // 2
    column = 1024
    pieces = 8 if units % 128 == 0 else 1

    def body(*refs):
        pick_ref, gain_ref = refs[:2]
        refs = refs[2:]
        block_refs, refs = refs[:block_count], refs[block_count:]
        gate_refs, refs = refs[:gate_count], refs[gate_count:]
        up_refs, refs = refs[:up_count], refs[up_count:]
        up_hbm, down_hbm, keep_ref, send_ref, rows_ref, normed_ref, up_late, down_ref, up_sems, down_sems = refs

        copies_up = []
        if late:
            up_pieces = 4 if late % 64 == 0 else 1
            step = late // up_pieces
            copies_up = [
                pltpu.make_async_copy(
                    up_hbm.at[pl.ds(loaded + i * step, step)], up_late.at[pl.ds(i * step, step)], up_sems.at[i]
                )
                for i in range(up_pieces)
            ]
        step = units // pieces
        copies_down = [
            pltpu.make_async_copy(
                down_hbm.at[pl.ds(i * step, step)], down_ref.at[pl.ds(i * step, step)], down_sems.at[i]
            )
            for i in range(pieces)
        ]
        for copy in copies_up + copies_down:
            copy.start()

        pick_now = pick_ref[...]
        total = jnp.zeros((requests, 1), jnp.float32)
        for c in range(0, width, column):
            gathered = jnp.concatenate([ref[:, c : c + column].astype(jnp.float32) for ref in block_refs], axis=0)
            rows = jnp.dot(pick_now, gathered.astype(jnp.bfloat16), preferred_element_type=jnp.float32)
            rows_ref[:, c : c + column] = rows
            total += jnp.sum(rows * rows, axis=1, keepdims=True)
        inv_rms = lax.rsqrt(total / width + norm_eps)
        normed_ref[...] = (rows_ref[...] * inv_rms * gain_ref[...]).astype(jnp.bfloat16)
        normed = normed_ref[...]

        def project(ref):
            rows = ref.shape[0]
            chunk = 192 if rows % 192 == 0 else rows
            return [
                lax.dot_general(
                    ref[j : j + chunk, :], normed, (((1,), (1,)), ((), ())), preferred_element_type=jnp.float32
                )
                for j in range(0, rows, chunk)
            ]

        gate_out = jnp.concatenate([g for ref in gate_refs for g in project(ref)], axis=0)
        up_list = [u for ref in up_refs for u in project(ref)]
        if late:
            for copy in copies_up:
                copy.wait()
            up_list += project(up_late)
        up_out = jnp.concatenate(up_list, axis=0)
        hidden = (jax.nn.silu(gate_out) * up_out).T.astype(jnp.bfloat16)
        for copy in copies_down:
            copy.wait()
        for c in range(0, width, column):
            out = jnp.dot(hidden, down_ref[:, c : c + column], preferred_element_type=jnp.float32)
            first = lax.broadcasted_iota(jnp.int32, out.shape, 0) == 0
            out += jnp.where(first, rows_ref[:, c : c + column], 0.0)
            keep_ref[:, c : c + column] = out[:half]
            send_ref[:, c : c + column] = out[half:]

    vmem = pl.BlockSpec(memory_space=pltpu.VMEM)
    anywhere = pl.BlockSpec(memory_space=pl.ANY)
    out = jax.ShapeDtypeStruct((half, width), jnp.float32)
    return pl.pallas_call(
        body,
        out_shape=(out, out),
        in_specs=[vmem] * (2 + block_count + gate_count + up_count) + [anywhere] * 2,
        out_specs=(vmem, vmem),
        scratch_shapes=[
            pltpu.VMEM((requests, width), jnp.float32),
            pltpu.VMEM((requests, width), jnp.bfloat16),
            pltpu.VMEM((max(late, 16), width), jnp.bfloat16),
            pltpu.VMEM((units, width), jnp.bfloat16),
            pltpu.SemaphoreType.DMA((4,)),
            pltpu.SemaphoreType.DMA((pieces,)),
        ],
        compiler_params=pltpu.CompilerParams(vmem_limit_bytes=27 * MIB),
        cost_estimate=pl.CostEstimate(
            flops=6 * requests * units * width, transcendentals=requests * units, bytes_accessed=4 * units * width
        ),
        name="feed_forward",
    )(
        pick,
        gain[None],
        *blocks,
        *gate_parts,
        *up_parts,
        pltpu.with_memory_space_constraint(w_up, pltpu.HBM),
        pltpu.with_memory_space_constraint(w_down, pltpu.HBM),
    )


def make_shards(size):
    bits = size.bit_length() - 1

    def shards(queries, kv_cache, cache_lengths, live_counts, stream, norm_gain, w_gate, w_up, w_down):
        slots = queries.shape[1]
        units = w_gate.shape[0]
        device = lax.axis_index("tp")
        counts_row = live_counts[0]
        pick = pick_matrix(counts_row, device, size, slots, bits)

        part = units // 2 if units % 32 == 0 else units
        jobs = [(w_gate, first) for first in range(0, units, part)] + [(w_up, 0)]
        loaded = []
        blocks = [stream[0]]
        for step in range(bits):
            for weight, first in jobs[:1]:
                loaded.append(load_rows(weight, first, part, blocks[-1]))
            jobs = jobs[1:]
            if len(blocks) > 4:
                blocks = [jnp.concatenate(blocks, axis=0)]
            blocks = blocks + [swap(block, bits - 1 - step, size) for block in blocks]
        keep, send = feed_forward(
            pick, norm_gain, blocks, loaded[: units // part], loaded[units // part :], w_up, w_down
        )

        queries, send = lax.optimization_barrier((queries, send))
        own_count = jnp.sum(jnp.where(jnp.arange(size, dtype=jnp.int32) == device, counts_row, 0))
        in_use = jnp.arange(slots, dtype=jnp.int32) < own_count
        latent_ctx = attend(queries[0], kv_cache[0], cache_lengths[0], in_use)[None]

        for bit in range(bits):
            arrived = swap(send, bit, size)
            if bit == bits - 1:
                return (latent_ctx, (keep + arrived).astype(jnp.bfloat16)[None])
            half = keep.shape[0] // 2
            send = keep[half:] + arrived[half:]
            keep = keep[:half] + arrived[:half]

    return shards


def solution(mesh):
    in_specs = (
        P(("groups", "sub"), "tp", None, None),
        P(("groups", "sub"), "tp", None, None),
        P(("groups", "sub"), "tp"),
        P(("groups", "sub"), None),
        P(("groups", "sub"), "tp", None),
        P(),
        P("tp", None),
        P("tp", None),
        P("tp", None),
    )
    out_specs = (P(("groups", "sub"), "tp", None, None), P(("groups", "sub"), "tp", None))
    return jax.shard_map(
        make_shards(mesh.shape["tp"]), mesh=mesh, in_specs=in_specs, out_specs=out_specs, check_vma=False
    )
```

```python
import jax
import jax.numpy as jnp
from jax import lax
from jax.experimental import pallas as pl
from jax.experimental.pallas import tpu as pltpu
from jax.sharding import PartitionSpec as P

KVL = 512
MIB = 1024 * 1024

score_scale = 192.0 ** (-0.5)
norm_eps = 1e-06

VMEM = pl.BlockSpec(memory_space=pltpu.VMEM)
SMEM = pl.BlockSpec(memory_space=pltpu.SMEM)
ANY = pl.BlockSpec(memory_space=pl.ANY)


def bit_reverse(value, bits):
    out = 0
    for bit in range(bits):
        out = out | (((value >> bit) & 1) << (bits - 1 - bit))
    return out


def swap(x, axis, bit, size):
    return lax.ppermute(x, axis, [(i, i ^ (1 << bit)) for i in range(size)])


def pinned(weight):
    return pltpu.with_memory_space_constraint(weight, pltpu.HBM)


def row_copies(source, first, target, sems):
    rows = target.shape[0]
    pieces = sems.shape[0]
    step = rows // pieces
    return [
        pltpu.make_async_copy(
            source.at[pl.ds(first + i * step, step)], target.at[pl.ds(i * step, step)], sems.at[i]
        )
        for i in range(pieces)
    ]


def pieces_of(rows, most):
    return most if rows % (16 * most) == 0 else 1


def share_start(units, share):
    if share == units:
        return 0
    return pl.multiple_of(lax.axis_index("sub") * share, 16)


def pick_matrix(counts, device, size, slots, bits):
    slot = lax.broadcasted_iota(jnp.int32, (size, size // 2 * slots), 1)
    every = lax.broadcasted_iota(jnp.int32, (size, size // 2 * slots), 0)
    owner = bit_reverse(slot // slots, bits) ^ device
    known = jnp.broadcast_to(counts, (8, size)).astype(jnp.bfloat16)
    start = jnp.dot(known, (every < owner).astype(jnp.bfloat16), preferred_element_type=jnp.float32)[:1]
    count = jnp.dot(known, (every == owner).astype(jnp.bfloat16), preferred_element_type=jnp.float32)[:1]
    place = (slot % slots)[:1].astype(jnp.float32)
    request = jnp.where(place < count, start + place, -1.0)
    row = lax.broadcasted_iota(jnp.int32, (2 * size, size // 2 * slots), 0)
    wanted = bit_reverse(row % size, bits) ^ device ^ (row // size)
    return (request == wanted.astype(jnp.float32)).astype(jnp.bfloat16)


def load_rows(jobs, share, after, counts=None, slots=0):
    pieces = [pieces_of(rows, 4) for _, _, rows in jobs]
    size = 0 if counts is None else counts.shape[1]
    bits = max(size.bit_length() - 1, 0)

    def body(*refs):
        sources = refs[: len(jobs)]
        refs = refs[len(jobs) + 1 :]
        if counts is not None:
            counts_ref, refs = refs[0], refs[1:]
        targets, refs = refs[: len(jobs)], refs[len(jobs) :]
        copies = []
        for (weight, first, _), source, target, sems in zip(jobs, sources, targets, refs[-len(jobs) :]):
            copies += row_copies(source, share_start(weight.shape[0], share) + first, target, sems)
        for copy in copies:
            copy.start()
        if counts is not None:
            refs[0][...] = pick_matrix(counts_ref[...], lax.axis_index("tp"), size, slots, bits)
        for copy in copies:
            copy.wait()

    out_shape = [pltpu.VMEM((rows, weight.shape[1]), weight.dtype) for weight, _, rows in jobs]
    if counts is not None:
        out_shape.append(jax.ShapeDtypeStruct((2 * size, size // 2 * slots), jnp.bfloat16))
    return pl.pallas_call(
        body,
        out_shape=out_shape,
        in_specs=[ANY] * (len(jobs) + 1) + [VMEM] * (counts is not None),
        out_specs=[VMEM] * len(out_shape),
        scratch_shapes=[pltpu.SemaphoreType.DMA((count,)) for count in pieces],
        compiler_params=pltpu.CompilerParams(vmem_limit_bytes=2 * MIB),
        cost_estimate=pl.CostEstimate(
            flops=0, transcendentals=0, bytes_accessed=sum(4 * rows * weight.shape[1] for weight, _, rows in jobs)
        ),
        name="load_rows",
    )(*[pinned(weight) for weight, _, _ in jobs], after, *([counts] if counts is not None else []))


def compact(pick, blocks, after):
    size = pick.shape[0] // 2
    width = blocks[0].shape[1]
    column = 1024
    count = len(blocks)

    def body(*refs):
        pick_ref, block_refs, (_, own_ref, send_ref) = refs[0], refs[1 : 1 + count], refs[1 + count :]
        pick_now = pick_ref[...]
        for c in range(0, width, column):
            rows = [ref[:, c : c + column].astype(jnp.float32) for ref in block_refs]
            rows = rows[0] if count == 1 else jnp.concatenate(rows, axis=0)
            out = jnp.dot(pick_now, rows.astype(jnp.bfloat16), preferred_element_type=jnp.float32)
            out = out.astype(jnp.bfloat16)
            own_ref[:, c : c + column] = out[:size]
            send_ref[:, c : c + column] = out[size:]

    out = jax.ShapeDtypeStruct((size, width), jnp.bfloat16)
    return pl.pallas_call(
        body,
        out_shape=(out, out),
        in_specs=[VMEM] * (1 + count) + [ANY],
        out_specs=(VMEM, VMEM),
        compiler_params=pltpu.CompilerParams(vmem_limit_bytes=16 * MIB),
        name="compact",
    )(pick, *blocks, after)


def feed_forward(gain, row_sets, gate_parts, up_parts, w_down, share):
    requests, width = row_sets[0].shape
    units = w_down.shape[0]
    set_count, gate_count, up_count = len(row_sets), len(gate_parts), len(up_parts)
    column = 1024
    pieces = pieces_of(share, 4)

    def body(*refs):
        gain_ref, refs = refs[0], refs[1:]
        set_refs, refs = refs[:set_count], refs[set_count:]
        gate_refs, refs = refs[:gate_count], refs[gate_count:]
        up_refs, refs = refs[:up_count], refs[up_count:]
        down_hbm, refs = refs[0], refs[1:]
        out_refs, refs = refs[:set_count], refs[set_count:]
        down_ref, down_sems = refs

        copies = row_copies(down_hbm, share_start(units, share), down_ref, down_sems)
        for copy in copies:
            copy.start()

        rows = [ref[...].astype(jnp.float32) for ref in set_refs]
        rows = rows[0] if set_count == 1 else jnp.concatenate(rows, axis=0)
        inv_rms = lax.rsqrt(jnp.mean(rows * rows, axis=1, keepdims=True) + norm_eps)
        normed = (rows * inv_rms * gain_ref[...]).astype(jnp.bfloat16)

        def project(part_refs):
            out = []
            for ref in part_refs:
                count = ref.shape[0]
                chunk = 192 if count % 192 == 0 else count
                for j in range(0, count, chunk):
                    out.append(
                        lax.dot_general(
                            ref[j : j + chunk, :], normed, (((1,), (1,)), ((), ())), preferred_element_type=jnp.float32
                        )
                    )
            return out[0] if len(out) == 1 else jnp.concatenate(out, axis=0)

        gate_out = project(gate_refs)
        up_out = project(up_refs)
        hidden = (jax.nn.silu(gate_out) * up_out).T.astype(jnp.bfloat16)
        for copy in copies:
            copy.wait()
        for c in range(0, width, column):
            out = jnp.dot(hidden, down_ref[:, c : c + column], preferred_element_type=jnp.float32)
            own = out[:requests]
            first = lax.broadcasted_iota(jnp.int32, own.shape, 0) == 0
            own += jnp.where(first, set_refs[0][:, c : c + column].astype(jnp.float32), 0.0)
            out_refs[0][:, c : c + column] = own
            if set_count == 2:
                out_refs[1][:, c : c + column] = out[requests:].astype(jnp.bfloat16)

    outs = [
        jax.ShapeDtypeStruct((requests, width), jnp.float32),
        jax.ShapeDtypeStruct((requests, width), jnp.bfloat16),
    ][:set_count]
    return pl.pallas_call(
        body,
        out_shape=outs,
        in_specs=[VMEM] * (1 + set_count + gate_count + up_count) + [ANY],
        out_specs=[VMEM] * set_count,
        scratch_shapes=[pltpu.VMEM((share, width), jnp.bfloat16), pltpu.SemaphoreType.DMA((pieces,))],
        compiler_params=pltpu.CompilerParams(vmem_limit_bytes=20 * MIB),
        cost_estimate=pl.CostEstimate(
            flops=6 * requests * set_count * share * width,
            transcendentals=requests * share,
            bytes_accessed=6 * share * width,
        ),
        name="feed_forward",
    )(gain[None], *row_sets, *gate_parts, *up_parts, pinned(w_down))


def attend(queries, cache, lengths, counts, after):
    slots, heads, _ = queries.shape
    positions = cache.shape[2]

    def body(lengths_ref, counts_ref, queries_ref, cache_ref, after_ref, out_ref):
        live = counts_ref[0, lax.axis_index("tp")]
        spot = lax.broadcasted_iota(jnp.int32, (heads, positions), 1)
        for s in range(slots):
            scores = (
                jnp.dot(queries_ref[s], cache_ref[s], preferred_element_type=jnp.float32)
                * score_scale
            )
            scores = jnp.where(spot < lengths_ref[0, s], scores, -jnp.inf)
            weights = jnp.exp(scores - jnp.max(scores, axis=1, keepdims=True))
            probs = (weights / jnp.sum(weights, axis=1, keepdims=True)).astype(jnp.bfloat16)
            context = lax.dot_general(
                probs, cache_ref[s, :KVL, :], (((1,), (1,)), ((), ())), preferred_element_type=jnp.float32
            )
            out_ref[s] = jnp.where(s < live, context, 0.0).astype(jnp.bfloat16)

    return pl.pallas_call(
        body,
        out_shape=jax.ShapeDtypeStruct((slots, heads, KVL), jnp.bfloat16),
        in_specs=[SMEM, SMEM, VMEM, VMEM, ANY],
        out_specs=VMEM,
        compiler_params=pltpu.CompilerParams(vmem_limit_bytes=8 * MIB),
        cost_estimate=pl.CostEstimate(
            flops=4 * slots * heads * positions * KVL,
            transcendentals=slots * heads * positions,
            bytes_accessed=2 * (queries.size + cache.size),
        ),
        name="attend",
    )(lengths, counts, queries, cache, after)


def load_plan(gate, up, share):
    if share % 48 == 0 and share // 3 % 16 == 0:
        third = share // 3
        return [
            [(gate, 0, 2 * third)],
            [(gate, 2 * third, third), (up, 0, third)],
            [(up, third, 2 * third)],
        ]
    return [[(gate, 0, share)], [(up, 0, share)], []]


def make_shards(size, cores):
    bits = size.bit_length() - 1

    def shards(queries, kv_cache, cache_lengths, live_counts, stream, norm_gain, w_gate, w_up, w_down):
        slots = queries.shape[1]
        units = w_gate.shape[0]
        split = cores == 2 and units % 32 == 0
        share = units // 2 if split else units
        plan = load_plan(w_gate, w_up, share)
        gate_parts, up_parts = [], []

        def load(jobs, after, counts=None):
            *parts, last = [*load_rows(jobs, share, after, counts, slots), *[None] * (counts is None)]
            for (weight, _, _), part in zip(jobs, parts):
                (gate_parts if weight is w_gate else up_parts).append(part)
            return last

        blocks = [stream[0]]
        for step in range(bits - 1):
            if len(blocks) > 4:
                blocks = [jnp.concatenate(blocks, axis=0)]
            arrived = [swap(block, "tp", bits - 1 - step, size) for block in blocks]
            if step == 0:
                pick = load(plan[0], blocks[0], live_counts)
                arrived[0], gate_parts[0] = lax.optimization_barrier((arrived[0], gate_parts[0]))
            elif step == 1:
                load(plan[1], blocks[1])
            blocks = blocks + arrived

        own, send = compact(pick, blocks, up_parts[0])
        arrived = swap(send, "tp", 0, size)
        if plan[2]:
            load(plan[2], send)
            arrived, up_parts[-1] = lax.optimization_barrier((arrived, up_parts[-1]))
        rows = own + arrived
        row_sets = [rows, swap(rows, "sub", 0, cores)] if split else [rows]
        total, *other = feed_forward(norm_gain, row_sets, gate_parts, up_parts, w_down, share)

        if split:
            total = total + swap(other[0], "sub", 0, cores).astype(jnp.float32)
        for bit in range(bits):
            half = total.shape[0] // 2
            send = total[half:].astype(jnp.bfloat16 if bit < 2 else jnp.float32)
            if bit == 0:
                latent_ctx = attend(queries[0], jnp.swapaxes(kv_cache[0], 1, 2), cache_lengths, live_counts, send)[None]
            total = total[:half] + swap(send, "tp", bit, size).astype(jnp.float32)
        return (latent_ctx, total.astype(jnp.bfloat16)[None])

    return shards


def solution(mesh):
    in_specs = (
        P(("groups", "sub"), "tp", None, None),
        P(("groups", "sub"), "tp", None, None),
        P(("groups", "sub"), "tp"),
        P(("groups", "sub"), None),
        P(("groups", "sub"), "tp", None),
        P(),
        P("tp", None),
        P("tp", None),
        P("tp", None),
    )
    out_specs = (P(("groups", "sub"), "tp", None, None), P(("groups", "sub"), "tp", None))
    return jax.shard_map(
        make_shards(mesh.shape["tp"], mesh.shape["sub"]),
        mesh=mesh,
        in_specs=in_specs,
        out_specs=out_specs,
        check_vma=False,
    )
```

```python
import jax
import jax.numpy as jnp
from jax import lax
from jax.experimental import pallas as pl
from jax.experimental.pallas import tpu as pltpu
from jax.sharding import PartitionSpec as P

KVL = 512
MIB = 1024 * 1024

score_scale = 192.0 ** (-0.5)
norm_eps = 1e-06

VMEM = pl.BlockSpec(memory_space=pltpu.VMEM)
SMEM = pl.BlockSpec(memory_space=pltpu.SMEM)
ANY = pl.BlockSpec(memory_space=pl.ANY)


def gather_stages(bits):
    stages, top = [], bits
    while top > 1:
        width = 1 if top % 2 == 0 else 2
        top -= width
        stages.append((top, width))
    return stages


def sum_stages(bits):
    return [(low, min(2, bits - low)) for low in range(0, bits, 2)]


def block_offset(position, stages):
    out = position * 0
    for low, width in stages:
        out = out | ((position & ((1 << width) - 1)) << low)
        position = position >> width
    return out


def row_offset(position, stages):
    return block_offset(position, stages[::-1])


def swap(x, axis, distance, size):
    return lax.ppermute(x, axis, [(i, i ^ distance) for i in range(size)])


def pinned(weight):
    return pltpu.with_memory_space_constraint(weight, pltpu.HBM)


def row_copies(source, first, target, sems):
    rows = target.shape[0]
    pieces = sems.shape[0]
    step = rows // pieces
    return [
        pltpu.make_async_copy(
            source.at[pl.ds(first + i * step, step)], target.at[pl.ds(i * step, step)], sems.at[i]
        )
        for i in range(pieces)
    ]


def pieces_of(rows, most):
    return most if rows % (16 * most) == 0 else 1


def share_start(units, share):
    if share == units:
        return 0
    return pl.multiple_of(lax.axis_index("sub") * share, 16)


def pick_matrix(counts, device, size, slots):
    stages = gather_stages(size.bit_length() - 1)
    shape = (size, size // 2 * slots)
    slot = lax.broadcasted_iota(jnp.int32, shape, 1)
    every = lax.broadcasted_iota(jnp.int32, shape, 0)
    owner = block_offset(slot // slots, stages) ^ device
    known = jnp.broadcast_to(counts, (8, size)).astype(jnp.bfloat16)
    start = jnp.dot(known, (every < owner).astype(jnp.bfloat16), preferred_element_type=jnp.float32)[:1]
    count = jnp.dot(known, (every == owner).astype(jnp.bfloat16), preferred_element_type=jnp.float32)[:1]
    place = (slot % slots)[:1].astype(jnp.float32)
    request = jnp.where(place < count, start + place, -1.0)
    return (request == every.astype(jnp.float32)).astype(jnp.bfloat16)


def load_rows(jobs, share, after=None, counts=None, slots=0):
    pieces = [pieces_of(rows, 4) for _, _, rows in jobs]
    size = 0 if counts is None else counts.shape[1]
    operands = [pinned(weight) for weight, _, _ in jobs]
    out_shape = [pltpu.VMEM((rows, weight.shape[1]), weight.dtype) for weight, _, rows in jobs]
    scratch = [pltpu.SemaphoreType.DMA((count,)) for count in pieces]
    if counts is not None:
        operands.append(pinned(counts))
        out_shape.append(jax.ShapeDtypeStruct((size, size // 2 * slots), jnp.bfloat16))
        scratch += [pltpu.VMEM((1, size), jnp.int32), pltpu.SemaphoreType.DMA]
    if after is not None:
        operands.append(after)

    def body(*refs):
        sources, refs = refs[: len(operands)], refs[len(operands) :]
        targets, refs = refs[: len(out_shape)], refs[len(out_shape) :]
        if counts is not None:
            small = pltpu.make_async_copy(sources[len(jobs)], refs[-2], refs[-1])
            small.start()
        copies = []
        for (weight, first, _), source, target, sems in zip(jobs, sources, targets, refs):
            copies += row_copies(source, share_start(weight.shape[0], share) + first, target, sems)
        for copy in copies:
            copy.start()
        if counts is not None:
            small.wait()
            targets[-1][...] = pick_matrix(refs[-2][...], lax.axis_index("tp"), size, slots)
        for copy in copies:
            copy.wait()

    return pl.pallas_call(
        body,
        out_shape=out_shape,
        in_specs=[ANY] * len(operands),
        out_specs=[VMEM] * len(out_shape),
        scratch_shapes=scratch,
        compiler_params=pltpu.CompilerParams(vmem_limit_bytes=2 * MIB),
        cost_estimate=pl.CostEstimate(
            flops=0, transcendentals=0, bytes_accessed=sum(4 * rows * weight.shape[1] for weight, _, rows in jobs)
        ),
        name="load_rows",
    )(*operands)


def compact(pick, blocks):
    size = pick.shape[0]
    width = blocks[0].shape[1]
    column = 1024
    count = len(blocks)

    def body(*refs):
        pick_ref, block_refs, out_ref = refs[0], refs[1 : 1 + count], refs[1 + count]
        pick_now = pick_ref[...]
        for c in range(0, width, column):
            rows = [ref[:, c : c + column].astype(jnp.float32) for ref in block_refs]
            rows = rows[0] if count == 1 else jnp.concatenate(rows, axis=0)
            out = jnp.dot(pick_now, rows.astype(jnp.bfloat16), preferred_element_type=jnp.float32)
            out_ref[:, c : c + column] = out.astype(jnp.bfloat16)

    return pl.pallas_call(
        body,
        out_shape=jax.ShapeDtypeStruct((size, width), jnp.bfloat16),
        in_specs=[VMEM] * (1 + count),
        out_specs=VMEM,
        compiler_params=pltpu.CompilerParams(vmem_limit_bytes=16 * MIB),
        name="compact",
    )(pick, *blocks)


def feed_forward(gain, row_sets, loaded, late, w_down, share, split):
    requests, width = row_sets[0].shape
    units = w_down.shape[0]
    set_count = len(row_sets)
    every = requests * set_count
    stages = sum_stages(requests.bit_length() - 1)
    column = 1024
    late_pieces = [pieces_of(rows, 4) for _, _, _, rows in late]
    pieces = pieces_of(share, 4)
    parts = [part for _, part in loaded]

    def body(*refs):
        gain_ref, refs = refs[0], refs[1:]
        set_refs, refs = refs[:set_count], refs[set_count:]
        part_refs, refs = refs[: len(parts)], refs[len(parts) :]
        late_hbm, refs = refs[: len(late)], refs[len(late) :]
        down_hbm, refs = refs[0], refs[1:]
        out_refs, refs = refs[:set_count], refs[set_count:]
        rows_ref, down_ref, down_sems, refs = refs[0], refs[1], refs[2], refs[3:]
        late_refs, late_sems = refs[: len(late)], refs[len(late) :]
        device = lax.axis_index("tp")

        late_copies = [
            row_copies(source, share_start(units, share) + first, target, sems)
            for (_, _, first, _), source, target, sems in zip(late, late_hbm, late_refs, late_sems)
        ]
        down_copies = row_copies(down_hbm, share_start(units, share), down_ref, down_sems)

        @pl.when(device >= 0)
        def _():
            for copies in late_copies:
                for copy in copies:
                    copy.start()
            for copy in down_copies:
                copy.start()

        place = lax.broadcasted_iota(jnp.int32, (every, every), 0)
        source_row = lax.broadcasted_iota(jnp.int32, (every, every), 1)
        wanted = (row_offset(place % requests, stages) ^ device) + place // requests * requests
        order = (source_row == wanted).astype(jnp.bfloat16)
        for c in range(0, width, column):
            rows = [ref[:, c : c + column].astype(jnp.float32) for ref in set_refs]
            rows = rows[0] if set_count == 1 else jnp.concatenate(rows, axis=0)
            rows_ref[:, c : c + column] = jnp.dot(
                order, rows.astype(jnp.bfloat16), preferred_element_type=jnp.float32
            )
        rows = rows_ref[...]
        inv_rms = lax.rsqrt(jnp.mean(rows * rows, axis=1, keepdims=True) + norm_eps)
        normed = (rows * inv_rms * gain_ref[...]).astype(jnp.bfloat16)

        results = [[], []]

        def project(which, ref):
            rows = ref.shape[0]
            chunk = next((c for c in (192, 160, 128, 64) if rows % c == 0), rows)
            for j in range(0, rows, chunk):
                results[which].append(
                    lax.dot_general(
                        ref[j : j + chunk, :], normed, (((1,), (1,)), ((), ())), preferred_element_type=jnp.float32
                    )
                )

        for (which, _), ref in zip(loaded, part_refs):
            project(which, ref)
        for (which, _, _, _), ref, copies in zip(late, late_refs, late_copies):
            for copy in copies:
                copy.wait()
            project(which, ref)
        gate_out, up_out = [out[0] if len(out) == 1 else jnp.concatenate(out, axis=0) for out in results]
        hidden = (jax.nn.silu(gate_out) * up_out).T.astype(jnp.bfloat16)
        for copy in down_copies:
            copy.wait()
        for c in range(0, width, column):
            out = jnp.dot(hidden, down_ref[:, c : c + column], preferred_element_type=jnp.float32)
            own = out[:requests]
            first = lax.broadcasted_iota(jnp.int32, own.shape, 0) == 0
            own += jnp.where(first, rows_ref[:requests, c : c + column], 0.0)
            out_refs[0][:, c : c + column] = own
            if set_count == 2:
                out_refs[1][:, c : c + column] = out[requests:].astype(jnp.bfloat16)

    outs = [
        jax.ShapeDtypeStruct((requests, width), jnp.float32),
        jax.ShapeDtypeStruct((requests, width), jnp.bfloat16),
    ][:set_count]
    return pl.pallas_call(
        body,
        out_shape=outs,
        in_specs=[VMEM] * (1 + set_count + len(parts)) + [ANY] * (len(late) + 1),
        out_specs=[VMEM] * set_count,
        scratch_shapes=[
            pltpu.VMEM((every, width), jnp.float32),
            pltpu.VMEM((share, width), jnp.bfloat16),
            pltpu.SemaphoreType.DMA((pieces,)),
            *[pltpu.VMEM((rows, width), jnp.bfloat16) for _, _, _, rows in late],
            *[pltpu.SemaphoreType.DMA((count,)) for count in late_pieces],
        ],
        compiler_params=pltpu.CompilerParams(vmem_limit_bytes=28 * MIB),
        cost_estimate=pl.CostEstimate(
            flops=6 * every * share * width,
            transcendentals=every * share,
            bytes_accessed=6 * share * width,
        ),
        name="feed_forward",
    )(gain[None], *row_sets, *parts, *[pinned(weight) for _, weight, _, _ in late], pinned(w_down))


def attend(queries, cache, lengths, counts, after):
    slots, heads, _ = queries.shape
    positions = cache.shape[2]

    def body(lengths_ref, counts_ref, queries_ref, cache_ref, after_ref, out_ref):
        live = counts_ref[0, lax.axis_index("tp")]
        spot = lax.broadcasted_iota(jnp.int32, (heads, positions), 1)
        for s in range(slots):
            scores = (
                jnp.dot(queries_ref[s], cache_ref[s], preferred_element_type=jnp.float32)
                * score_scale
            )
            scores = jnp.where(spot < lengths_ref[0, s], scores, -jnp.inf)
            weights = jnp.exp(scores - jnp.max(scores, axis=1, keepdims=True))
            probs = (weights / jnp.sum(weights, axis=1, keepdims=True)).astype(jnp.bfloat16)
            context = lax.dot_general(
                probs, cache_ref[s, :KVL, :], (((1,), (1,)), ((), ())), preferred_element_type=jnp.float32
            )
            out_ref[s] = jnp.where(s < live, context, 0.0).astype(jnp.bfloat16)

    return pl.pallas_call(
        body,
        out_shape=jax.ShapeDtypeStruct((slots, heads, KVL), jnp.bfloat16),
        in_specs=[SMEM, SMEM, VMEM, VMEM, ANY],
        out_specs=VMEM,
        compiler_params=pltpu.CompilerParams(vmem_limit_bytes=8 * MIB),
        cost_estimate=pl.CostEstimate(
            flops=4 * slots * heads * positions * KVL,
            transcendentals=slots * heads * positions,
            bytes_accessed=2 * (queries.size + cache.size),
        ),
        name="attend",
    )(lengths, counts, queries, cache, after)


def load_plan(share):
    if share % 192:
        return [(0, 0, share)], [(1, 0, share)], []
    early = share // 9 * 5
    return (
        [(0, 0, early)],
        [(0, early, share - early), (1, 0, 2 * early - share)],
        [(1, 2 * early - share, 2 * share - 2 * early)],
    )


def make_shards(size, cores):
    bits = size.bit_length() - 1

    def shards(queries, kv_cache, cache_lengths, live_counts, stream, norm_gain, w_gate, w_up, w_down):
        slots = queries.shape[1]
        units = w_gate.shape[0]
        split = cores == 2 and units % 32 == 0
        share = units // 2 if split else units
        weights = (w_gate, w_up)
        plan = load_plan(share)
        loaded = []

        def load(jobs, **more):
            parts = load_rows([(weights[which], first, rows) for which, first, rows in jobs], share, **more)
            loaded.extend((which, part) for (which, _, _), part in zip(jobs, parts))
            return parts

        block = stream[0]
        for step, (low, width) in enumerate(gather_stages(bits)):
            blocks = [block] + [swap(block, "tp", digit << low, size) for digit in range(1, 1 << width)]
            if step == 0:
                pick = load(plan[0], counts=live_counts, slots=slots)[-1]
            if low > 1:
                block = jnp.concatenate(blocks, axis=0)

        own = compact(pick, blocks)
        arrived = swap(own, "tp", 1, size)
        load(plan[1], after=own)
        last = loaded[-1]
        arrived, part = lax.optimization_barrier((arrived, last[1]))
        loaded[-1] = (last[0], part)
        rows = own + arrived
        row_sets = [rows, swap(rows, "sub", 1, cores)] if split else [rows]
        late = [(which, weights[which], first, count) for which, first, count in plan[2]]
        total, *other = feed_forward(norm_gain, row_sets, loaded, late, w_down, share, split)

        if split:
            total = total + swap(other[0], "sub", 1, cores).astype(jnp.float32)
        for step, (low, width) in enumerate(sum_stages(bits)):
            part = total.shape[0] >> width
            sends = [total[digit * part : (digit + 1) * part] for digit in range(1, 1 << width)]
            total = total[:part]
            if step == 0:
                sends = [send.astype(jnp.bfloat16) for send in sends]
                latent_ctx = attend(
                    queries[0], jnp.swapaxes(kv_cache[0], 1, 2), cache_lengths, live_counts, sends[0]
                )[None]
            for digit, send in enumerate(sends, 1):
                total = total + swap(send, "tp", digit << low, size).astype(jnp.float32)
        return (latent_ctx, total.astype(jnp.bfloat16)[None])

    return shards


def solution(mesh):
    in_specs = (
        P(("groups", "sub"), "tp", None, None),
        P(("groups", "sub"), "tp", None, None),
        P(("groups", "sub"), "tp"),
        P(("groups", "sub"), None),
        P(("groups", "sub"), "tp", None),
        P(),
        P("tp", None),
        P("tp", None),
        P("tp", None),
    )
    out_specs = (P(("groups", "sub"), "tp", None, None), P(("groups", "sub"), "tp", None))
    return jax.shard_map(
        make_shards(mesh.shape["tp"], mesh.shape["sub"]),
        mesh=mesh,
        in_specs=in_specs,
        out_specs=out_specs,
        check_vma=False,
    )
```

```python
import jax
import jax.numpy as jnp
from jax import lax
from jax.experimental import pallas as pl
from jax.experimental.pallas import tpu as pltpu
from jax.sharding import PartitionSpec as P

KVL = 512
MIB = 1024 * 1024

score_scale = 192.0 ** (-0.5)
norm_eps = 1e-06

VMEM = pl.BlockSpec(memory_space=pltpu.VMEM)
SMEM = pl.BlockSpec(memory_space=pltpu.SMEM)
ANY = pl.BlockSpec(memory_space=pl.ANY)


def gather_stages(bits):
    stages, top = [], bits
    while top > 1:
        width = 1 if top % 2 == 0 else 2
        top -= width
        stages.append((top, width))
    return stages


def sum_stages(bits):
    return [(low, min(2, bits - low)) for low in range(0, bits, 2)]


def block_offset(position, stages):
    out = position * 0
    for low, width in stages:
        out = out | ((position & ((1 << width) - 1)) << low)
        position = position >> width
    return out


def row_offset(position, stages):
    return block_offset(position, stages[::-1])


def swap(x, axis, distance, size):
    return lax.ppermute(x, axis, [(i, i ^ distance) for i in range(size)])


def pinned(weight):
    return pltpu.with_memory_space_constraint(weight, pltpu.HBM)


def row_copy(source, first, target, sems, i):
    step = target.shape[0] // sems.shape[0]
    here = pl.multiple_of(i * step, step)
    return pltpu.make_async_copy(
        source.at[pl.ds(first + here, step)], target.at[pl.ds(here, step)], sems.at[i]
    )


def start_rows(source, first, target, sems, pieces=None):
    @pl.loop(*(pieces or (0, sems.shape[0])))
    def _(i):
        row_copy(source, first, target, sems, i).start()


def wait_rows(source, first, target, sems):
    @pl.loop(0, sems.shape[0])
    def _(i):
        row_copy(source, first, target, sems, i).wait()


def pieces_of(rows, most):
    return most if rows % (16 * most) == 0 else 1


def share_start(units, share):
    if share == units:
        return 0
    return pl.multiple_of(lax.axis_index("sub") * share, 16)


def pick_matrix(counts, device, size, slots):
    stages = gather_stages(size.bit_length() - 1)
    shape = (size, size // 2 * slots)
    slot = lax.broadcasted_iota(jnp.int32, shape, 1)
    every = lax.broadcasted_iota(jnp.int32, shape, 0)
    owner = block_offset(slot // slots, stages) ^ device
    known = jnp.broadcast_to(counts, (8, size)).astype(jnp.bfloat16)
    start = jnp.dot(known, (every < owner).astype(jnp.bfloat16), preferred_element_type=jnp.float32)[:1]
    count = jnp.dot(known, (every == owner).astype(jnp.bfloat16), preferred_element_type=jnp.float32)[:1]
    place = (slot % slots)[:1].astype(jnp.float32)
    request = jnp.where(place < count, start + place, -1.0)
    return (request == every.astype(jnp.float32)).astype(jnp.bfloat16)


def load_rows(jobs, share, after=None, counts=None, slots=0):
    pieces = [pieces_of(rows, 4) for _, _, rows in jobs]
    size = 0 if counts is None else counts.shape[1]
    operands = [pinned(weight) for weight, _, _ in jobs]
    out_shape = [pltpu.VMEM((rows, weight.shape[1]), weight.dtype) for weight, _, rows in jobs]
    scratch = [pltpu.SemaphoreType.DMA((count,)) for count in pieces]
    if counts is not None:
        operands.append(pinned(counts))
        out_shape.append(jax.ShapeDtypeStruct((size, size // 2 * slots), jnp.bfloat16))
        scratch += [pltpu.VMEM((1, size), jnp.int32), pltpu.SemaphoreType.DMA]
    if after is not None:
        operands.append(after)

    def body(*refs):
        sources, refs = refs[: len(operands)], refs[len(operands) :]
        targets, refs = refs[: len(out_shape)], refs[len(out_shape) :]
        if counts is not None:
            small = pltpu.make_async_copy(sources[len(jobs)], refs[-2], refs[-1])
            small.start()
        copies = [
            (source, share_start(weight.shape[0], share) + first, target, sems)
            for (weight, first, _), source, target, sems in zip(jobs, sources, targets, refs)
        ]
        for copy in copies:
            start_rows(*copy)
        if counts is not None:
            small.wait()
            targets[-1][...] = pick_matrix(refs[-2][...], lax.axis_index("tp"), size, slots)
        for copy in copies:
            wait_rows(*copy)

    return pl.pallas_call(
        body,
        out_shape=out_shape,
        in_specs=[ANY] * len(operands),
        out_specs=[VMEM] * len(out_shape),
        scratch_shapes=scratch,
        compiler_params=pltpu.CompilerParams(vmem_limit_bytes=2 * MIB),
        cost_estimate=pl.CostEstimate(
            flops=0, transcendentals=0, bytes_accessed=sum(4 * rows * weight.shape[1] for weight, _, rows in jobs)
        ),
        name="load_rows",
    )(*operands)


def compact(pick, blocks):
    size = pick.shape[0]
    width = blocks[0].shape[1]
    column = 1024
    count = len(blocks)

    def body(*refs):
        pick_ref, block_refs, out_ref = refs[0], refs[1 : 1 + count], refs[1 + count]
        pick_now = pick_ref[...]
        for c in range(0, width, column):
            rows = [ref[:, c : c + column].astype(jnp.float32) for ref in block_refs]
            rows = rows[0] if count == 1 else jnp.concatenate(rows, axis=0)
            out = jnp.dot(pick_now, rows.astype(jnp.bfloat16), preferred_element_type=jnp.float32)
            out_ref[:, c : c + column] = out.astype(jnp.bfloat16)

    return pl.pallas_call(
        body,
        out_shape=jax.ShapeDtypeStruct((size, width), jnp.bfloat16),
        in_specs=[VMEM] * (1 + count),
        out_specs=VMEM,
        compiler_params=pltpu.CompilerParams(vmem_limit_bytes=16 * MIB),
        name="compact",
    )(pick, *blocks)


def feed_forward(gain, row_sets, loaded, late, w_down, share, split):
    requests, width = row_sets[0].shape
    units = w_down.shape[0]
    set_count = len(row_sets)
    every = requests * set_count
    stages = sum_stages(requests.bit_length() - 1)
    column = 1024
    late_pieces = [pieces_of(rows, 4) for _, _, _, rows in late]
    pieces = pieces_of(share, 4)
    parts = [part for _, _, part in loaded]

    def body(*refs):
        gain_ref, refs = refs[0], refs[1:]
        set_refs, refs = refs[:set_count], refs[set_count:]
        part_refs, refs = refs[: len(parts)], refs[len(parts) :]
        late_hbm, refs = refs[: len(late)], refs[len(late) :]
        down_hbm, refs = refs[0], refs[1:]
        out_refs, refs = refs[:set_count], refs[set_count:]
        rows_ref, normed_ref, down_ref, down_sems = refs[:4]
        projected_refs, refs = refs[4:6], refs[6:]
        late_refs, late_sems = refs[: len(late)], refs[len(late) :]
        device = lax.axis_index("tp")

        start = share_start(units, share)
        late_copies = [
            (source, start + first, target, sems)
            for (_, _, first, _), source, target, sems in zip(late, late_hbm, late_refs, late_sems)
        ]
        down_copy = (down_hbm, start, down_ref, down_sems)
        for copy in late_copies:
            start_rows(*copy)

        def project(which, ref, at):
            rows = ref.shape[0]
            chunk = next((c for c in (192, 160, 128, 64) if rows % c == 0), rows)
            for j in range(0, rows, chunk):
                projected_refs[which][at + j : at + j + chunk, :] = lax.dot_general(
                    ref[j : j + chunk, :], normed_ref[...], (((1,), (1,)), ((), ())), preferred_element_type=jnp.float32
                )

        place = lax.broadcasted_iota(jnp.int32, (every, every), 0)
        source_row = lax.broadcasted_iota(jnp.int32, (every, every), 1)
        wanted = (row_offset(place % requests, stages) ^ device) + place // requests * requests
        order = (source_row == wanted).astype(jnp.bfloat16)
        for c in range(0, width, column):
            rows = [ref[:, c : c + column].astype(jnp.float32) for ref in set_refs]
            rows = rows[0] if set_count == 1 else jnp.concatenate(rows, axis=0)
            rows_ref[:, c : c + column] = jnp.dot(
                order, rows.astype(jnp.bfloat16), preferred_element_type=jnp.float32
            )
        rows = rows_ref[...]
        inv_rms = lax.rsqrt(jnp.mean(rows * rows, axis=1, keepdims=True) + norm_eps)
        normed_ref[...] = (rows * inv_rms * gain_ref[...]).astype(jnp.bfloat16)

        for part, ((which, first, _), ref) in enumerate(zip(loaded, part_refs)):
            project(which, ref, first)
            if part == 0:
                start_rows(*down_copy, pieces=(0, pieces // 2))
        for copy in late_copies:
            wait_rows(*copy)
        start_rows(*down_copy, pieces=(pieces // 2, pieces))
        for (which, _, first, _), ref in zip(late, late_refs):
            project(which, ref, first)
        hidden = (jax.nn.silu(projected_refs[0][...]) * projected_refs[1][...]).T.astype(jnp.bfloat16)
        wait_rows(*down_copy)
        for c in range(0, width, column):
            out = jnp.dot(hidden, down_ref[:, c : c + column], preferred_element_type=jnp.float32)
            own = out[:requests]
            first = lax.broadcasted_iota(jnp.int32, own.shape, 0) == 0
            own += jnp.where(first, rows_ref[:requests, c : c + column], 0.0)
            out_refs[0][:, c : c + column] = own
            if set_count == 2:
                out_refs[1][:, c : c + column] = out[requests:].astype(jnp.bfloat16)

    outs = [
        jax.ShapeDtypeStruct((requests, width), jnp.float32),
        jax.ShapeDtypeStruct((requests, width), jnp.bfloat16),
    ][:set_count]
    return pl.pallas_call(
        body,
        out_shape=outs,
        in_specs=[VMEM] * (1 + set_count + len(parts)) + [ANY] * (len(late) + 1),
        out_specs=[VMEM] * set_count,
        scratch_shapes=[
            pltpu.VMEM((every, width), jnp.float32),
            pltpu.VMEM((every, width), jnp.bfloat16),
            pltpu.VMEM((share, width), jnp.bfloat16),
            pltpu.SemaphoreType.DMA((pieces,)),
            *[pltpu.VMEM((share, every), jnp.float32)] * 2,
            *[pltpu.VMEM((rows, width), jnp.bfloat16) for _, _, _, rows in late],
            *[pltpu.SemaphoreType.DMA((count,)) for count in late_pieces],
        ],
        compiler_params=pltpu.CompilerParams(vmem_limit_bytes=28 * MIB),
        cost_estimate=pl.CostEstimate(
            flops=6 * every * share * width,
            transcendentals=every * share,
            bytes_accessed=6 * share * width,
        ),
        name="feed_forward",
    )(gain[None], *row_sets, *parts, *[pinned(weight) for _, weight, _, _ in late], pinned(w_down))


def attend(queries, cache, lengths, counts, after):
    slots, heads, _ = queries.shape
    positions = cache.shape[2]

    def body(lengths_ref, counts_ref, queries_ref, cache_ref, after_ref, out_ref):
        live = counts_ref[0, lax.axis_index("tp")]
        spot = lax.broadcasted_iota(jnp.int32, (heads, positions), 1)
        for s in range(slots):
            scores = (
                jnp.dot(queries_ref[s], cache_ref[s], preferred_element_type=jnp.float32)
                * score_scale
            )
            scores = jnp.where(spot < lengths_ref[0, s], scores, -jnp.inf)
            weights = jnp.exp(scores - jnp.max(scores, axis=1, keepdims=True))
            probs = (weights / jnp.sum(weights, axis=1, keepdims=True)).astype(jnp.bfloat16)
            context = lax.dot_general(
                probs, cache_ref[s, :KVL, :], (((1,), (1,)), ((), ())), preferred_element_type=jnp.float32
            )
            out_ref[s] = jnp.where(s < live, context, 0.0).astype(jnp.bfloat16)

    return pl.pallas_call(
        body,
        out_shape=jax.ShapeDtypeStruct((slots, heads, KVL), jnp.bfloat16),
        in_specs=[SMEM, SMEM, VMEM, VMEM, ANY],
        out_specs=VMEM,
        compiler_params=pltpu.CompilerParams(vmem_limit_bytes=8 * MIB),
        cost_estimate=pl.CostEstimate(
            flops=4 * slots * heads * positions * KVL,
            transcendentals=slots * heads * positions,
            bytes_accessed=2 * (queries.size + cache.size),
        ),
        name="attend",
    )(lengths, counts, queries, cache, after)


def load_plan(share):
    if share % 192:
        return [(0, 0, share)], [(1, 0, share)], []
    early = share // 9 * 5
    return (
        [(0, 0, early)],
        [(0, early, share - early), (1, 0, 2 * early - share)],
        [(1, 2 * early - share, 2 * share - 2 * early)],
    )


def make_shards(size, cores):
    bits = size.bit_length() - 1

    def shards(queries, kv_cache, cache_lengths, live_counts, stream, norm_gain, w_gate, w_up, w_down):
        slots = queries.shape[1]
        units = w_gate.shape[0]
        split = cores == 2 and units % 32 == 0
        share = units // 2 if split else units
        weights = (w_gate, w_up)
        plan = load_plan(share)
        loaded = []

        def load(jobs, **more):
            parts = load_rows([(weights[which], first, rows) for which, first, rows in jobs], share, **more)
            loaded.extend((which, first, part) for (which, first, _), part in zip(jobs, parts))
            return parts

        block = stream[0]
        for step, (low, width) in enumerate(gather_stages(bits)):
            blocks = [block] + [swap(block, "tp", digit << low, size) for digit in range(1, 1 << width)]
            if step == 0:
                pick = load(plan[0], counts=live_counts, slots=slots)[-1]
            if low > 1:
                block = jnp.concatenate(blocks, axis=0)

        own = compact(pick, blocks)
        arrived = swap(own, "tp", 1, size)
        load(plan[1], after=own)
        *last, part = loaded[-1]
        arrived, part = lax.optimization_barrier((arrived, part))
        loaded[-1] = (*last, part)
        rows = own + arrived
        row_sets = [rows, swap(rows, "sub", 1, cores)] if split else [rows]
        late = [(which, weights[which], first, count) for which, first, count in plan[2]]
        total, *other = feed_forward(norm_gain, row_sets, loaded, late, w_down, share, split)

        if split:
            total = total + swap(other[0], "sub", 1, cores).astype(jnp.float32)
        for step, (low, width) in enumerate(sum_stages(bits)):
            part = total.shape[0] >> width
            sends = [total[digit * part : (digit + 1) * part] for digit in range(1, 1 << width)]
            total = total[:part]
            if step == 0:
                sends = [send.astype(jnp.bfloat16) for send in sends]
                latent_ctx = attend(
                    queries[0], jnp.swapaxes(kv_cache[0], 1, 2), cache_lengths, live_counts, sends[0]
                )[None]
            for digit, send in enumerate(sends, 1):
                total = total + swap(send, "tp", digit << low, size).astype(jnp.float32)
        return (latent_ctx, total.astype(jnp.bfloat16)[None])

    return shards


def solution(mesh):
    in_specs = (
        P(("groups", "sub"), "tp", None, None),
        P(("groups", "sub"), "tp", None, None),
        P(("groups", "sub"), "tp"),
        P(("groups", "sub"), None),
        P(("groups", "sub"), "tp", None),
        P(),
        P("tp", None),
        P("tp", None),
        P("tp", None),
    )
    out_specs = (P(("groups", "sub"), "tp", None, None), P(("groups", "sub"), "tp", None))
    return jax.shard_map(
        make_shards(mesh.shape["tp"], mesh.shape["sub"]),
        mesh=mesh,
        in_specs=in_specs,
        out_specs=out_specs,
        check_vma=False,
    )
```

```python
import jax
import jax.numpy as jnp
from jax import lax
from jax.experimental import pallas as pl
from jax.experimental.pallas import tpu as pltpu
from jax.sharding import PartitionSpec as P

KVL = 512
MIB = 1024 * 1024

score_scale = 192.0 ** (-0.5)
norm_eps = 1e-06

VMEM = pl.BlockSpec(memory_space=pltpu.VMEM)
SMEM = pl.BlockSpec(memory_space=pltpu.SMEM)
ANY = pl.BlockSpec(memory_space=pl.ANY)


def gather_stages(bits):
    stages, top = [], bits
    while top > 1:
        width = 1 if top % 2 == 0 else 2
        top -= width
        stages.append((top, width))
    return stages


def sum_stages(bits):
    return [(low, min(2, bits - low)) for low in range(0, bits, 2)]


def block_offset(position, stages):
    out = position * 0
    for low, width in stages:
        out = out | ((position & ((1 << width) - 1)) << low)
        position = position >> width
    return out


def row_offset(position, stages):
    return block_offset(position, stages[::-1])


def swap(x, axis, distance, size):
    return lax.ppermute(x, axis, [(i, i ^ distance) for i in range(size)])


def pinned(weight):
    return pltpu.with_memory_space_constraint(weight, pltpu.HBM)


def row_copy(source, first, target, sems, i):
    step = target.shape[0] // sems.shape[0]
    here = pl.multiple_of(i * step, step)
    return pltpu.make_async_copy(source.at[pl.ds(first + here, step)], target.at[pl.ds(here, step)], sems.at[i])


def column_copy(source, first, target, sems, i):
    rows, width = target.shape
    step = width // sems.shape[0]
    here = pl.ds(pl.multiple_of(i * step, step), step)
    return pltpu.make_async_copy(source.at[pl.ds(first, rows), here], target.at[:, here], sems.at[i])


def start_pieces(piece, copy, first=0, count=None):
    @pl.loop(first, first + (count or copy[-1].shape[0]))
    def _(i):
        piece(*copy, i).start()


def wait_pieces(piece, copy):
    @pl.loop(0, copy[-1].shape[0])
    def _(i):
        piece(*copy, i).wait()


def pieces_of(rows, most):
    return most if rows % (16 * most) == 0 else 1


def share_start(units, share):
    if share == units:
        return 0
    return pl.multiple_of(lax.axis_index("sub") * share, 16)


def pick_matrix(counts, device, size, slots):
    bits = size.bit_length() - 1
    shape = (size, size // 2 * slots)
    slot = lax.broadcasted_iota(jnp.int32, shape, 1)
    every = lax.broadcasted_iota(jnp.int32, shape, 0)
    owner = block_offset(slot // slots, gather_stages(bits)) ^ device
    known = jnp.broadcast_to(counts, (8, size)).astype(jnp.bfloat16)
    start = jnp.dot(known, (every < owner).astype(jnp.bfloat16), preferred_element_type=jnp.float32)[:1]
    count = jnp.dot(known, (every == owner).astype(jnp.bfloat16), preferred_element_type=jnp.float32)[:1]
    place = (slot % slots)[:1].astype(jnp.float32)
    request = jnp.where(place < count, start + place, -1.0)
    row = lax.broadcasted_iota(jnp.int32, (2 * size, shape[1]), 0)
    wanted = row_offset(row % size, sum_stages(bits)) ^ device ^ (row // size)
    return (request == wanted.astype(jnp.float32)).astype(jnp.bfloat16)


def load_rows(jobs, share, after=None, counts=None, slots=0):
    pieces = [pieces_of(rows, 4) for _, _, rows in jobs]
    size = 0 if counts is None else counts.shape[1]
    operands = [pinned(weight) for weight, _, _ in jobs]
    out_shape = [pltpu.VMEM((rows, weight.shape[1]), weight.dtype) for weight, _, rows in jobs]
    scratch = [pltpu.SemaphoreType.DMA((count,)) for count in pieces]
    if counts is not None:
        operands.append(pinned(counts))
        out_shape.append(jax.ShapeDtypeStruct((2 * size, size // 2 * slots), jnp.bfloat16))
        scratch += [pltpu.VMEM((1, size), jnp.int32), pltpu.SemaphoreType.DMA]
    if after is not None:
        operands.append(after)

    def body(*refs):
        sources, refs = refs[: len(operands)], refs[len(operands) :]
        targets, refs = refs[: len(out_shape)], refs[len(out_shape) :]
        if counts is not None:
            small = pltpu.make_async_copy(sources[len(jobs)], refs[-2], refs[-1])
            small.start()
        copies = [
            (source, share_start(weight.shape[0], share) + first, target, sems)
            for (weight, first, _), source, target, sems in zip(jobs, sources, targets, refs)
        ]
        for copy in copies:
            start_pieces(row_copy, copy)
        if counts is not None:
            small.wait()
            targets[-1][...] = pick_matrix(refs[-2][...], lax.axis_index("tp"), size, slots)
        for copy in copies:
            wait_pieces(row_copy, copy)

    return pl.pallas_call(
        body,
        out_shape=out_shape,
        in_specs=[ANY] * len(operands),
        out_specs=[VMEM] * len(out_shape),
        scratch_shapes=scratch,
        compiler_params=pltpu.CompilerParams(vmem_limit_bytes=2 * MIB),
        cost_estimate=pl.CostEstimate(
            flops=0, transcendentals=0, bytes_accessed=sum(4 * rows * weight.shape[1] for weight, _, rows in jobs)
        ),
        name="load_rows",
    )(*operands)


def compact(pick, blocks):
    size = pick.shape[0] // 2
    width = blocks[0].shape[1]
    column = 1024
    count = len(blocks)

    def body(*refs):
        pick_ref, block_refs, (own_ref, send_ref) = refs[0], refs[1 : 1 + count], refs[1 + count :]
        pick_now = pick_ref[...]
        for c in range(0, width, column):
            rows = [ref[:, c : c + column].astype(jnp.float32) for ref in block_refs]
            rows = rows[0] if count == 1 else jnp.concatenate(rows, axis=0)
            out = jnp.dot(pick_now, rows.astype(jnp.bfloat16), preferred_element_type=jnp.float32)
            own_ref[:, c : c + column] = out[:size].astype(jnp.bfloat16)
            send_ref[:, c : c + column] = out[size:].astype(jnp.bfloat16)

    out = jax.ShapeDtypeStruct((size, width), jnp.bfloat16)
    return pl.pallas_call(
        body,
        out_shape=(out, out),
        in_specs=[VMEM] * (1 + count),
        out_specs=(VMEM, VMEM),
        compiler_params=pltpu.CompilerParams(vmem_limit_bytes=16 * MIB),
        name="compact",
    )(pick, *blocks)


def feed_forward(gain, row_sets, loaded, late, w_down, share):
    requests, width = row_sets[0].shape
    units = w_down.shape[0]
    set_count = len(row_sets)
    every = requests * set_count
    late_pieces = [pieces_of(rows, 4) for _, _, _, rows in late]
    pieces = 4
    column = width // pieces
    parts = [part for _, _, part in loaded]

    def body(*refs):
        gain_ref, refs = refs[0], refs[1:]
        set_refs, refs = refs[:set_count], refs[set_count:]
        part_refs, refs = refs[: len(parts)], refs[len(parts) :]
        late_hbm, refs = refs[: len(late)], refs[len(late) :]
        down_hbm, refs = refs[0], refs[1:]
        out_refs, refs = refs[:set_count], refs[set_count:]
        normed_ref, hidden_ref, down_ref, down_sems = refs[:4]
        projected_refs, refs = refs[4:6], refs[6:]
        late_refs, late_sems = refs[: len(late)], refs[len(late) :]

        start = share_start(units, share)
        late_copies = [
            (source, start + first, target, sems)
            for (_, _, first, _), source, target, sems in zip(late, late_hbm, late_refs, late_sems)
        ]
        down_copy = (down_hbm, start, down_ref, down_sems)
        for copy in late_copies:
            start_pieces(row_copy, copy)

        def project(which, ref, at):
            rows = ref.shape[0]
            chunk = next((c for c in (192, 160, 128, 64) if rows % c == 0), rows)
            for j in range(0, rows, chunk):
                projected_refs[which][at + j : at + j + chunk, :] = lax.dot_general(
                    ref[j : j + chunk, :], normed_ref[...], (((1,), (1,)), ((), ())), preferred_element_type=jnp.float32
                )

        rows = [ref[...].astype(jnp.float32) for ref in set_refs]
        rows = rows[0] if set_count == 1 else jnp.concatenate(rows, axis=0)
        inv_rms = lax.rsqrt(jnp.mean(rows * rows, axis=1, keepdims=True) + norm_eps)
        normed_ref[...] = (rows * inv_rms * gain_ref[...]).astype(jnp.bfloat16)

        for part, ((which, first, _), ref) in enumerate(zip(loaded, part_refs)):
            project(which, ref, first)
            if part == 0:
                start_pieces(column_copy, down_copy, 0, pieces - 1)
        for copy in late_copies:
            wait_pieces(row_copy, copy)
        start_pieces(column_copy, down_copy, pieces - 1, 1)
        for (which, _, first, _), ref in zip(late, late_refs):
            project(which, ref, first)
        hidden_ref[...] = (jax.nn.silu(projected_refs[0][...]) * projected_refs[1][...]).T.astype(jnp.bfloat16)

        @pl.loop(0, pieces)
        def _(i):
            column_copy(*down_copy, i).wait()
            here = pl.ds(pl.multiple_of(i * column, column), column)
            out = jnp.dot(hidden_ref[...], down_ref[:, here], preferred_element_type=jnp.float32)
            own = out[:requests]
            first = lax.broadcasted_iota(jnp.int32, own.shape, 0) == 0
            own += jnp.where(first, set_refs[0][:, here].astype(jnp.float32), 0.0)
            out_refs[0][:, here] = own
            if set_count == 2:
                out_refs[1][:, here] = out[requests:].astype(jnp.bfloat16)

    outs = [
        jax.ShapeDtypeStruct((requests, width), jnp.float32),
        jax.ShapeDtypeStruct((requests, width), jnp.bfloat16),
    ][:set_count]
    return pl.pallas_call(
        body,
        out_shape=outs,
        in_specs=[VMEM] * (1 + set_count + len(parts)) + [ANY] * (len(late) + 1),
        out_specs=[VMEM] * set_count,
        scratch_shapes=[
            pltpu.VMEM((every, width), jnp.bfloat16),
            pltpu.VMEM((every, share), jnp.bfloat16),
            pltpu.VMEM((share, width), jnp.bfloat16),
            pltpu.SemaphoreType.DMA((pieces,)),
            *[pltpu.VMEM((share, every), jnp.float32)] * 2,
            *[pltpu.VMEM((rows, width), jnp.bfloat16) for _, _, _, rows in late],
            *[pltpu.SemaphoreType.DMA((count,)) for count in late_pieces],
        ],
        compiler_params=pltpu.CompilerParams(vmem_limit_bytes=28 * MIB),
        cost_estimate=pl.CostEstimate(
            flops=6 * every * share * width,
            transcendentals=every * share,
            bytes_accessed=6 * share * width,
        ),
        name="feed_forward",
    )(gain[None], *row_sets, *parts, *[pinned(weight) for _, weight, _, _ in late], pinned(w_down))


def attend(queries, cache, lengths, counts, after):
    slots, heads, _ = queries.shape
    positions = cache.shape[2]

    def body(lengths_ref, counts_ref, queries_ref, cache_ref, after_ref, out_ref):
        live = counts_ref[0, lax.axis_index("tp")]
        spot = lax.broadcasted_iota(jnp.int32, (heads, positions), 1)
        every = []
        for s in range(slots):
            scores = (
                jnp.dot(queries_ref[s], cache_ref[s], preferred_element_type=jnp.float32)
                * score_scale
            )
            every.append(jnp.where(spot < lengths_ref[0, s], scores, -jnp.inf))
        scores = jnp.concatenate(every, axis=0)
        weights = jnp.exp(scores - jnp.max(scores, axis=1, keepdims=True))
        probs = (weights / jnp.sum(weights, axis=1, keepdims=True)).astype(jnp.bfloat16)
        for s in range(slots):
            context = lax.dot_general(
                probs[s * heads : (s + 1) * heads],
                cache_ref[s, :KVL, :],
                (((1,), (1,)), ((), ())),
                preferred_element_type=jnp.float32,
            )
            out_ref[s] = jnp.where(s < live, context, 0.0).astype(jnp.bfloat16)

    return pl.pallas_call(
        body,
        out_shape=jax.ShapeDtypeStruct((slots, heads, KVL), jnp.bfloat16),
        in_specs=[SMEM, SMEM, VMEM, VMEM, ANY],
        out_specs=VMEM,
        compiler_params=pltpu.CompilerParams(vmem_limit_bytes=8 * MIB),
        cost_estimate=pl.CostEstimate(
            flops=4 * slots * heads * positions * KVL,
            transcendentals=slots * heads * positions,
            bytes_accessed=2 * (queries.size + cache.size),
        ),
        name="attend",
    )(lengths, counts, queries, cache, after)


def load_plan(share):
    if share % 192:
        return [(0, 0, share)], [(1, 0, share)], []
    early = share // 3 * 2
    return (
        [(0, 0, early)],
        [(0, early, share - early), (1, 0, 2 * early - share)],
        [(1, 2 * early - share, 2 * share - 2 * early)],
    )


def make_shards(size, cores):
    bits = size.bit_length() - 1

    def shards(queries, kv_cache, cache_lengths, live_counts, stream, norm_gain, w_gate, w_up, w_down):
        slots = queries.shape[1]
        units = w_gate.shape[0]
        split = cores == 2 and units % 32 == 0
        share = units // 2 if split else units
        weights = (w_gate, w_up)
        plan = load_plan(share)
        loaded = []

        def load(jobs, **more):
            parts = load_rows([(weights[which], first, rows) for which, first, rows in jobs], share, **more)
            loaded.extend((which, first, part) for (which, first, _), part in zip(jobs, parts))
            return parts

        block = stream[0]
        for step, (low, width) in enumerate(gather_stages(bits)):
            blocks = [block] + [swap(block, "tp", digit << low, size) for digit in range(1, 1 << width)]
            if step == 0:
                pick = load(plan[0], counts=live_counts, slots=slots)[-1]
            if low > 1:
                block = jnp.concatenate(blocks, axis=0)

        own, send = compact(pick, blocks)
        arrived = swap(send, "tp", 1, size)
        load(plan[1], after=send)
        *last, part = loaded[-1]
        arrived, part = lax.optimization_barrier((arrived, part))
        loaded[-1] = (*last, part)
        rows = own + arrived
        row_sets = [rows, swap(rows, "sub", 1, cores)] if split else [rows]
        late = [(which, weights[which], first, count) for which, first, count in plan[2]]
        total, *other = feed_forward(norm_gain, row_sets, loaded, late, w_down, share)

        if split:
            total = total + swap(other[0], "sub", 1, cores).astype(jnp.float32)
        for step, (low, width) in enumerate(sum_stages(bits)):
            part = total.shape[0] >> width
            sends = [total[digit * part : (digit + 1) * part] for digit in range(1, 1 << width)]
            total = total[:part]
            if step == 0:
                sends = [send.astype(jnp.bfloat16) for send in sends]
                latent_ctx = attend(
                    queries[0], jnp.swapaxes(kv_cache[0], 1, 2), cache_lengths, live_counts, sends[0]
                )[None]
            for digit, send in enumerate(sends, 1):
                total = total + swap(send, "tp", digit << low, size).astype(jnp.float32)
        return (latent_ctx, total.astype(jnp.bfloat16)[None])

    return shards


def solution(mesh):
    in_specs = (
        P(("groups", "sub"), "tp", None, None),
        P(("groups", "sub"), "tp", None, None),
        P(("groups", "sub"), "tp"),
        P(("groups", "sub"), None),
        P(("groups", "sub"), "tp", None),
        P(),
        P("tp", None),
        P("tp", None),
        P("tp", None),
    )
    out_specs = (P(("groups", "sub"), "tp", None, None), P(("groups", "sub"), "tp", None))
    return jax.shard_map(
        make_shards(mesh.shape["tp"], mesh.shape["sub"]),
        mesh=mesh,
        in_specs=in_specs,
        out_specs=out_specs,
        check_vma=False,
    )
```

```python
import jax
import jax.numpy as jnp
from jax import lax
from jax.experimental import pallas as pl
from jax.experimental.pallas import tpu as pltpu
from jax.sharding import PartitionSpec as P

KVL = 512
MIB = 1024 * 1024

score_scale = 192.0 ** (-0.5)
norm_eps = 1e-06

VMEM = pl.BlockSpec(memory_space=pltpu.VMEM)
SMEM = pl.BlockSpec(memory_space=pltpu.SMEM)
ANY = pl.BlockSpec(memory_space=pl.ANY)


def gather_stages(bits):
    stages, top = [], bits
    while top > 1:
        width = 1 if top % 2 == 0 else 2
        top -= width
        stages.append((top, width))
    return stages


def sum_stages(bits):
    return [(low, min(2, bits - low)) for low in range(0, bits, 2)]


def direct_offset(place, core):
    return ((-place) & 3) | (core * 4)


def block_offset(position, stages):
    out = position * 0
    for low, width in stages:
        out = out | ((-position & ((1 << width) - 1)) << low)
        position = position >> width
    return out


def row_offset(position, stages):
    out = position * 0
    for low, width in stages[::-1]:
        out = out | ((position & ((1 << width) - 1)) << low)
        position = position >> width
    return out


def swap(x, axis, distance, size):
    return lax.ppermute(x, axis, [(i, i ^ distance) for i in range(size)])


def direct_swap(x, place, size):
    pairs = []
    for core in range(2):
        distance = direct_offset(place, core) or 2
        pairs += [(2 * i + core, 2 * (i ^ distance) + core) for i in range(size)]
    return lax.ppermute(x, ("tp", "sub"), pairs)


def pinned(weight):
    return pltpu.with_memory_space_constraint(weight, pltpu.HBM)


def row_copy(source, first, target, sems, i):
    step = target.shape[0] // sems.shape[0]
    here = pl.multiple_of(i * step, step)
    return pltpu.make_async_copy(source.at[pl.ds(first + here, step)], target.at[pl.ds(here, step)], sems.at[i])


def column_copy(source, first, target, sems, i):
    rows, width = target.shape
    step = width // sems.shape[0]
    here = pl.ds(pl.multiple_of(i * step, step), step)
    return pltpu.make_async_copy(source.at[pl.ds(first, rows), here], target.at[:, here], sems.at[i])


def start_pieces(piece, copy, first=0, count=None):
    @pl.loop(first, first + (count or copy[-1].shape[0]))
    def _(i):
        piece(*copy, i).start()


def wait_pieces(piece, copy):
    @pl.loop(0, copy[-1].shape[0])
    def _(i):
        piece(*copy, i).wait()


def pieces_of(rows, most):
    return most if rows % (16 * most) == 0 else 1


def share_start(units, share):
    if share == units:
        return 0
    return pl.multiple_of(lax.axis_index("sub") * share, 16)


def pick_matrix(counts, device, size, slots, stages):
    bits = size.bit_length() - 1
    shape = (size, size // 2 * slots)
    slot = lax.broadcasted_iota(jnp.int32, shape, 1)
    every = lax.broadcasted_iota(jnp.int32, shape, 0)
    owner = block_offset(slot // slots, gather_stages(bits)) ^ device
    known = jnp.broadcast_to(counts, (8, size)).astype(jnp.bfloat16)
    start = jnp.dot(known, (every < owner).astype(jnp.bfloat16), preferred_element_type=jnp.float32)[:1]
    count = jnp.dot(known, (every == owner).astype(jnp.bfloat16), preferred_element_type=jnp.float32)[:1]
    place = (slot % slots)[:1].astype(jnp.float32)
    request = jnp.where(place < count, start + place, -1.0)
    row = lax.broadcasted_iota(jnp.int32, (2 * size, shape[1]), 0)
    wanted = row_offset(row % size, stages) ^ device ^ (row // size)
    return (request == wanted.astype(jnp.float32)).astype(jnp.bfloat16)


def load_rows(jobs, share, after=None, counts=None, slots=0, stages=()):
    pieces = [pieces_of(rows, 4) for _, _, rows in jobs]
    size = 0 if counts is None else counts.shape[1]
    operands = [pinned(weight) for weight, _, _ in jobs]
    out_shape = [pltpu.VMEM((rows, weight.shape[1]), weight.dtype) for weight, _, rows in jobs]
    scratch = [pltpu.SemaphoreType.DMA((count,)) for count in pieces]
    if counts is not None:
        operands.append(pinned(counts))
        out_shape.append(jax.ShapeDtypeStruct((2 * size, size // 2 * slots), jnp.bfloat16))
        scratch += [pltpu.VMEM((1, size), jnp.int32), pltpu.SemaphoreType.DMA]
    if after is not None:
        operands.append(after)

    def body(*refs):
        sources, refs = refs[: len(operands)], refs[len(operands) :]
        targets, refs = refs[: len(out_shape)], refs[len(out_shape) :]
        if counts is not None:
            small = pltpu.make_async_copy(sources[len(jobs)], refs[-2], refs[-1])
            small.start()
        copies = [
            (source, share_start(weight.shape[0], share) + first, target, sems)
            for (weight, first, _), source, target, sems in zip(jobs, sources, targets, refs)
        ]
        for copy in copies:
            start_pieces(row_copy, copy)
        if counts is not None:
            small.wait()
            targets[-1][...] = pick_matrix(refs[-2][...], lax.axis_index("tp"), size, slots, stages)
        for copy in copies:
            wait_pieces(row_copy, copy)

    return pl.pallas_call(
        body,
        out_shape=out_shape,
        in_specs=[ANY] * len(operands),
        out_specs=[VMEM] * len(out_shape),
        scratch_shapes=scratch,
        compiler_params=pltpu.CompilerParams(vmem_limit_bytes=2 * MIB),
        cost_estimate=pl.CostEstimate(
            flops=0, transcendentals=0, bytes_accessed=sum(4 * rows * weight.shape[1] for weight, _, rows in jobs)
        ),
        name="load_rows",
    )(*operands)


def compact(pick, blocks):
    size = pick.shape[0] // 2
    width = blocks[0].shape[1]
    column = 1024
    count = len(blocks)

    def body(*refs):
        pick_ref, block_refs, (own_ref, send_ref) = refs[0], refs[1 : 1 + count], refs[1 + count :]
        pick_now = pick_ref[...]
        for c in range(0, width, column):
            rows = [ref[:, c : c + column].astype(jnp.float32) for ref in block_refs]
            rows = rows[0] if count == 1 else jnp.concatenate(rows, axis=0)
            out = jnp.dot(pick_now, rows.astype(jnp.bfloat16), preferred_element_type=jnp.float32)
            own_ref[:, c : c + column] = out[:size].astype(jnp.bfloat16)
            send_ref[:, c : c + column] = out[size:].astype(jnp.bfloat16)

    out = jax.ShapeDtypeStruct((size, width), jnp.bfloat16)
    return pl.pallas_call(
        body,
        out_shape=(out, out),
        in_specs=[VMEM] * (1 + count),
        out_specs=(VMEM, VMEM),
        compiler_params=pltpu.CompilerParams(vmem_limit_bytes=16 * MIB),
        name="compact",
    )(pick, *blocks)


def feed_forward(gain, row_sets, loaded, late, w_down, share):
    requests, width = row_sets[0].shape
    units = w_down.shape[0]
    set_count = len(row_sets)
    every = requests * set_count
    late_pieces = [pieces_of(rows, 4) for _, _, _, rows in late]
    pieces = 4
    column = width // pieces
    parts = [part for _, _, part in loaded]

    def body(*refs):
        gain_ref, refs = refs[0], refs[1:]
        set_refs, refs = refs[:set_count], refs[set_count:]
        part_refs, refs = refs[: len(parts)], refs[len(parts) :]
        late_hbm, refs = refs[: len(late)], refs[len(late) :]
        down_hbm, refs = refs[0], refs[1:]
        out_refs, refs = refs[:set_count], refs[set_count:]
        normed_ref, hidden_ref, down_ref, down_sems = refs[:4]
        projected_refs, refs = refs[4:6], refs[6:]
        late_refs, late_sems = refs[: len(late)], refs[len(late) :]

        start = share_start(units, share)
        late_copies = [
            (source, start + first, target, sems)
            for (_, _, first, _), source, target, sems in zip(late, late_hbm, late_refs, late_sems)
        ]
        down_copy = (down_hbm, start, down_ref, down_sems)
        for copy in late_copies:
            start_pieces(row_copy, copy)

        def project(which, ref, at):
            rows = ref.shape[0]
            chunk = next((c for c in (192, 160, 128, 64) if rows % c == 0), rows)
            for j in range(0, rows, chunk):
                projected_refs[which][at + j : at + j + chunk, :] = lax.dot_general(
                    ref[j : j + chunk, :], normed_ref[...], (((1,), (1,)), ((), ())), preferred_element_type=jnp.float32
                )

        rows = [ref[...].astype(jnp.float32) for ref in set_refs]
        rows = rows[0] if set_count == 1 else jnp.concatenate(rows, axis=0)
        inv_rms = lax.rsqrt(jnp.mean(rows * rows, axis=1, keepdims=True) + norm_eps)
        normed_ref[...] = (rows * inv_rms * gain_ref[...]).astype(jnp.bfloat16)

        for part, ((which, first, _), ref) in enumerate(zip(loaded, part_refs)):
            project(which, ref, first)
            if part == 0:
                start_pieces(column_copy, down_copy, 0, pieces - 1)
        for copy in late_copies:
            wait_pieces(row_copy, copy)
        start_pieces(column_copy, down_copy, pieces - 1, 1)
        for (which, _, first, _), ref in zip(late, late_refs):
            project(which, ref, first)
        hidden = (jax.nn.silu(projected_refs[0][...]) * projected_refs[1][...]).astype(jnp.bfloat16)
        place = lax.broadcasted_iota(jnp.int32, (every, every), 0)
        if set_count == 2:
            core = lax.axis_index("sub")
            other = place // requests
            distance = direct_offset(place % requests // 2, core ^ other)
            place = distance + ((place % 2) ^ other) * requests
        order = (lax.broadcasted_iota(jnp.int32, (every, every), 1) == place).astype(jnp.bfloat16)
        hidden_ref[...] = lax.dot_general(
            order, hidden, (((1,), (1,)), ((), ())), preferred_element_type=jnp.float32
        ).astype(jnp.bfloat16)

        @pl.loop(0, pieces)
        def _(i):
            column_copy(*down_copy, i).wait()
            here = pl.ds(pl.multiple_of(i * column, column), column)
            out = jnp.dot(hidden_ref[...], down_ref[:, here], preferred_element_type=jnp.float32)
            out_refs[0][:, here] = out[:requests]
            if set_count == 2:
                out_refs[1][:, here] = out[requests:].astype(jnp.bfloat16)

    outs = [
        jax.ShapeDtypeStruct((requests, width), jnp.float32),
        jax.ShapeDtypeStruct((requests, width), jnp.bfloat16),
    ][:set_count]
    return pl.pallas_call(
        body,
        out_shape=outs,
        in_specs=[VMEM] * (1 + set_count + len(parts)) + [ANY] * (len(late) + 1),
        out_specs=[VMEM] * set_count,
        scratch_shapes=[
            pltpu.VMEM((every, width), jnp.bfloat16),
            pltpu.VMEM((every, share), jnp.bfloat16),
            pltpu.VMEM((share, width), jnp.bfloat16),
            pltpu.SemaphoreType.DMA((pieces,)),
            *[pltpu.VMEM((share, every), jnp.float32)] * 2,
            *[pltpu.VMEM((rows, width), jnp.bfloat16) for _, _, _, rows in late],
            *[pltpu.SemaphoreType.DMA((count,)) for count in late_pieces],
        ],
        compiler_params=pltpu.CompilerParams(vmem_limit_bytes=28 * MIB),
        cost_estimate=pl.CostEstimate(
            flops=6 * every * share * width,
            transcendentals=every * share,
            bytes_accessed=6 * share * width,
        ),
        name="feed_forward",
    )(gain[None], *row_sets, *parts, *[pinned(weight) for _, weight, _, _ in late], pinned(w_down))


def attend(queries, cache, lengths, counts, after):
    slots, heads, _ = queries.shape
    positions = cache.shape[2]

    def body(lengths_ref, counts_ref, queries_ref, cache_ref, after_ref, out_ref):
        live = counts_ref[0, lax.axis_index("tp")]
        spot = lax.broadcasted_iota(jnp.int32, (heads, positions), 1)
        every = []
        for s in range(slots):
            scores = (
                jnp.dot(queries_ref[s], cache_ref[s], preferred_element_type=jnp.float32)
                * score_scale
            )
            every.append(jnp.where(spot < lengths_ref[0, s], scores, -jnp.inf))
        scores = jnp.concatenate(every, axis=0)
        weights = jnp.exp(scores - jnp.max(scores, axis=1, keepdims=True))
        probs = (weights / jnp.sum(weights, axis=1, keepdims=True)).astype(jnp.bfloat16)
        for s in range(slots):
            context = lax.dot_general(
                probs[s * heads : (s + 1) * heads],
                cache_ref[s, :KVL, :],
                (((1,), (1,)), ((), ())),
                preferred_element_type=jnp.float32,
            )
            out_ref[s] = jnp.where(s < live, context, 0.0).astype(jnp.bfloat16)

    return pl.pallas_call(
        body,
        out_shape=jax.ShapeDtypeStruct((slots, heads, KVL), jnp.bfloat16),
        in_specs=[SMEM, SMEM, VMEM, VMEM, ANY],
        out_specs=VMEM,
        compiler_params=pltpu.CompilerParams(vmem_limit_bytes=8 * MIB),
        cost_estimate=pl.CostEstimate(
            flops=4 * slots * heads * positions * KVL,
            transcendentals=slots * heads * positions,
            bytes_accessed=2 * (queries.size + cache.size),
        ),
        name="attend",
    )(lengths, counts, queries, cache, after)


def load_plan(share):
    if share % 192:
        return [(0, 0, share)], [(1, 0, share)], []
    early = share // 3 * 2
    return (
        [(0, 0, early)],
        [(0, early, share - early), (1, 0, 2 * early - share)],
        [(1, 2 * early - share, 2 * share - 2 * early)],
    )


def make_shards(size, cores):
    bits = size.bit_length() - 1

    def shards(queries, kv_cache, cache_lengths, live_counts, stream, norm_gain, w_gate, w_up, w_down):
        slots = queries.shape[1]
        units = w_gate.shape[0]
        split = cores == 2 and size == 8 and units % 32 == 0
        share = units // 2 if split else units
        weights = (w_gate, w_up)
        stages = [(0, bits)] if split else sum_stages(bits)
        plan = load_plan(share)
        loaded = []

        def load(jobs, **more):
            parts = load_rows([(weights[which], first, rows) for which, first, rows in jobs], share, **more)
            loaded.extend((which, first, part) for (which, first, _), part in zip(jobs, parts))
            return parts

        block = stream[0]
        for step, (low, width) in enumerate(gather_stages(bits)):
            blocks = [block] + [swap(block, "tp", digit << low, size) for digit in range((1 << width) - 1, 0, -1)]
            if step == 0:
                pick = load(plan[0], counts=live_counts, slots=slots, stages=stages)[-1]
            if low > 1:
                block = jnp.concatenate(blocks, axis=0)

        own, send = compact(pick, blocks)
        arrived = swap(send, "tp", 1, size)
        load(plan[1], after=send)
        *last, part = loaded[-1]
        arrived, part = lax.optimization_barrier((arrived, part))
        loaded[-1] = (*last, part)
        rows = own + arrived
        row_sets = [rows, swap(rows, "sub", 1, cores)] if split else [rows]
        late = [(which, weights[which], first, count) for which, first, count in plan[2]]
        total, *other = feed_forward(norm_gain, row_sets, loaded, late, w_down, share)

        after = other[0] if split else total
        latent_ctx = attend(queries[0], jnp.swapaxes(kv_cache[0], 1, 2), cache_lengths, live_counts, after)[None]
        own_row = rows[:1].astype(jnp.float32)
        if split:
            total = total + swap(other[0], "sub", 1, cores).astype(jnp.float32)
            places = [total[2 * place : 2 * place + 2] for place in range(4)]
            sums = [
                direct_swap(places[place].astype(jnp.bfloat16), place, size).astype(jnp.float32)
                for place in (1, 2, 3, 0)
            ]
            total = jnp.where(lax.axis_index("sub") == 0, places[0], sums[3]) + sums[0] + sums[2] + sums[1]
            total, latent_ctx = lax.optimization_barrier((total, latent_ctx))
            total = total[:1] + swap(total[1:], "sub", 1, cores)
        else:
            for step, (low, width) in enumerate(stages):
                part = total.shape[0] >> width
                sends = [total[digit * part : (digit + 1) * part] for digit in range(1, 1 << width)]
                total = total[:part]
                for digit, send in enumerate(sends, 1):
                    total = total + swap(send, "tp", digit << low, size)
        return (latent_ctx, (total + own_row).astype(jnp.bfloat16)[None])

    return shards


def solution(mesh):
    in_specs = (
        P(("groups", "sub"), "tp", None, None),
        P(("groups", "sub"), "tp", None, None),
        P(("groups", "sub"), "tp"),
        P(("groups", "sub"), None),
        P(("groups", "sub"), "tp", None),
        P(),
        P("tp", None),
        P("tp", None),
        P("tp", None),
    )
    out_specs = (P(("groups", "sub"), "tp", None, None), P(("groups", "sub"), "tp", None))
    return jax.shard_map(
        make_shards(mesh.shape["tp"], mesh.shape["sub"]),
        mesh=mesh,
        in_specs=in_specs,
        out_specs=out_specs,
        check_vma=False,
    )
```

```python
import jax
import jax.numpy as jnp
from jax import lax
from jax.experimental import pallas as pl
from jax.experimental.pallas import tpu as pltpu
from jax.sharding import PartitionSpec as P

KVL = 512
MIB = 1024 * 1024

score_scale = 192.0 ** (-0.5)
norm_eps = 1e-06

VMEM = pl.BlockSpec(memory_space=pltpu.VMEM)
SMEM = pl.BlockSpec(memory_space=pltpu.SMEM)
ANY = pl.BlockSpec(memory_space=pl.ANY)


def gather_stages(bits):
    stages, top = [], bits
    while top > 1:
        width = 1 if top % 2 == 0 else 2
        top -= width
        stages.append((top, width))
    return stages


def sum_stages(bits):
    return [(low, min(2, bits - low)) for low in range(0, bits, 2)]


def direct_offset(place, core):
    return ((-place) & 3) | (core * 4)


def block_offset(position, stages):
    out = position * 0
    for low, width in stages:
        out = out | ((-position & ((1 << width) - 1)) << low)
        position = position >> width
    return out


def row_offset(position, stages):
    out = position * 0
    for low, width in stages[::-1]:
        out = out | ((position & ((1 << width) - 1)) << low)
        position = position >> width
    return out


def swap(x, axis, distance, size):
    return lax.ppermute(x, axis, [(i, i ^ distance) for i in range(size)])


def direct_swap(x, place, size):
    pairs = []
    for core in range(2):
        distance = direct_offset(place, core) or 2
        pairs += [(2 * i + core, 2 * (i ^ distance) + core) for i in range(size)]
    return lax.ppermute(x, ("tp", "sub"), pairs)


def pinned(weight):
    return pltpu.with_memory_space_constraint(weight, pltpu.HBM)


def row_copy(source, first, target, sems, i):
    step = target.shape[0] // sems.shape[0]
    here = pl.multiple_of(i * step, step)
    return pltpu.make_async_copy(source.at[pl.ds(first + here, step)], target.at[pl.ds(here, step)], sems.at[i])


def start_pieces(copy):
    @pl.loop(0, copy[-1].shape[0])
    def _(i):
        row_copy(*copy, i).start()


def wait_pieces(copy):
    @pl.loop(0, copy[-1].shape[0])
    def _(i):
        row_copy(*copy, i).wait()


def pieces_of(rows, most):
    return most if rows % (16 * most) == 0 else 1


def share_start(units, share):
    if share == units:
        return 0
    return pl.multiple_of(lax.axis_index("sub") * share, 16)


def pick_matrix(counts, device, size, slots, stages):
    bits = size.bit_length() - 1
    shape = (size, size // 2 * slots)
    slot = lax.broadcasted_iota(jnp.int32, shape, 1)
    every = lax.broadcasted_iota(jnp.int32, shape, 0)
    owner = block_offset(slot // slots, gather_stages(bits)) ^ device
    known = jnp.broadcast_to(counts, (8, size)).astype(jnp.bfloat16)
    start = jnp.dot(known, (every < owner).astype(jnp.bfloat16), preferred_element_type=jnp.float32)[:1]
    count = jnp.dot(known, (every == owner).astype(jnp.bfloat16), preferred_element_type=jnp.float32)[:1]
    place = (slot % slots)[:1].astype(jnp.float32)
    request = jnp.where(place < count, start + place, -1.0)
    row = lax.broadcasted_iota(jnp.int32, (2 * size, shape[1]), 0)
    wanted = row_offset(row % size, stages) ^ device ^ (row // size)
    return (request == wanted.astype(jnp.float32)).astype(jnp.bfloat16)


def attend(lengths_ref, counts_ref, queries_ref, cache_ref, out_ref):
    slots, heads, _ = queries_ref.shape
    positions = cache_ref.shape[2]
    live = counts_ref[0, lax.axis_index("tp")]
    spot = lax.broadcasted_iota(jnp.int32, (heads, positions), 1)
    every = []
    for s in range(slots):
        scores = jnp.dot(queries_ref[s], cache_ref[s], preferred_element_type=jnp.float32) * score_scale
        every.append(jnp.where(spot < lengths_ref[0, s], scores, -jnp.inf))
    scores = jnp.concatenate(every, axis=0)
    weights = jnp.exp(scores - jnp.max(scores, axis=1, keepdims=True))
    probs = (weights / jnp.sum(weights, axis=1, keepdims=True)).astype(jnp.bfloat16)
    for s in range(slots):
        context = lax.dot_general(
            probs[s * heads : (s + 1) * heads],
            cache_ref[s, :KVL, :],
            (((1,), (1,)), ((), ())),
            preferred_element_type=jnp.float32,
        )
        out_ref[s] = jnp.where(s < live, context, 0.0).astype(jnp.bfloat16)


def load_kernel(body, jobs, share, operands, specs, out_shape, out_specs, scratch, name):
    pieces = [pieces_of(rows, 4) for _, _, rows in jobs]
    count = len(jobs)

    def kernel(*refs):
        sources, refs = refs[:count], refs[count:]
        inputs, refs = refs[: len(operands)], refs[len(operands) :]
        targets, refs = refs[:count], refs[count:]
        copies = [
            (source, share_start(weight.shape[0], share) + first, target, sems)
            for (weight, first, _), source, target, sems in zip(jobs, sources, targets, refs[-count:])
        ]
        body([lambda copy=copy: start_pieces(copy) for copy in copies], *inputs, *refs[:-count])
        for copy in copies:
            wait_pieces(copy)

    return pl.pallas_call(
        kernel,
        out_shape=[pltpu.VMEM((rows, weight.shape[1]), weight.dtype) for weight, _, rows in jobs] + out_shape,
        in_specs=[ANY] * count + specs,
        out_specs=[VMEM] * count + out_specs,
        scratch_shapes=scratch + [pltpu.SemaphoreType.DMA((piece_count,)) for piece_count in pieces],
        compiler_params=pltpu.CompilerParams(vmem_limit_bytes=8 * MIB),
        cost_estimate=pl.CostEstimate(
            flops=0, transcendentals=0, bytes_accessed=sum(4 * rows * weight.shape[1] for weight, _, rows in jobs)
        ),
        name=name,
    )(*[pinned(weight) for weight, _, _ in jobs], *operands)


def load_and_pick(jobs, share, counts, slots, stages):
    size = counts.shape[1]

    def body(starts, counts_hbm, pick_ref, counts_ref, counts_sem):
        small = pltpu.make_async_copy(counts_hbm, counts_ref, counts_sem)
        small.start()
        for start in starts:
            start()
        small.wait()
        pick_ref[...] = pick_matrix(counts_ref[...], lax.axis_index("tp"), size, slots, stages)

    pick = jax.ShapeDtypeStruct((2 * size, size // 2 * slots), jnp.bfloat16)
    scratch = [pltpu.VMEM((1, size), jnp.int32), pltpu.SemaphoreType.DMA]
    return load_kernel(body, jobs, share, [pinned(counts)], [ANY], [pick], [VMEM], scratch, "load_and_pick")


def load_and_attend(jobs, share, queries, cache, lengths, counts, after):
    slots, heads, _ = queries.shape

    def body(starts, lengths_ref, counts_ref, queries_hbm, cache_hbm, _, out_hbm, queries_ref, cache_ref, out_ref, sems):
        copies = [
            pltpu.make_async_copy(queries_hbm, queries_ref, sems.at[0]),
            pltpu.make_async_copy(cache_hbm, cache_ref, sems.at[1]),
        ]
        for copy in copies:
            copy.start()
        starts[0]()
        for copy in copies:
            copy.wait()
        for start in starts[1:]:
            start()
        attend(lengths_ref, counts_ref, queries_ref, cache_ref, out_ref)
        out = pltpu.make_async_copy(out_ref, out_hbm, sems.at[2])
        out.start()
        out.wait()

    context = jax.ShapeDtypeStruct((slots, heads, KVL), jnp.bfloat16)
    scratch = [
        pltpu.VMEM(queries.shape, queries.dtype),
        pltpu.VMEM(cache.shape, cache.dtype),
        pltpu.VMEM(context.shape, context.dtype),
        pltpu.SemaphoreType.DMA((3,)),
    ]
    operands = [lengths, counts, pinned(queries), pinned(cache), after]
    specs = [SMEM, SMEM, ANY, ANY, ANY]
    return load_kernel(body, jobs, share, operands, specs, [context], [ANY], scratch, "load_and_attend")


def compact(pick, blocks):
    size = pick.shape[0] // 2
    width = blocks[0].shape[1]
    column = 1024
    count = len(blocks)

    def body(*refs):
        pick_ref, block_refs, (own_ref, send_ref) = refs[0], refs[1 : 1 + count], refs[1 + count :]
        pick_now = pick_ref[...]
        for c in range(0, width, column):
            rows = [ref[:, c : c + column].astype(jnp.float32) for ref in block_refs]
            rows = rows[0] if count == 1 else jnp.concatenate(rows, axis=0)
            out = jnp.dot(pick_now, rows.astype(jnp.bfloat16), preferred_element_type=jnp.float32)
            own_ref[:, c : c + column] = out[:size].astype(jnp.bfloat16)
            send_ref[:, c : c + column] = out[size:].astype(jnp.bfloat16)

    out = jax.ShapeDtypeStruct((size, width), jnp.bfloat16)
    return pl.pallas_call(
        body,
        out_shape=(out, out),
        in_specs=[VMEM] * (1 + count),
        out_specs=(VMEM, VMEM),
        compiler_params=pltpu.CompilerParams(vmem_limit_bytes=16 * MIB),
        name="compact",
    )(pick, *blocks)


def feed_forward(gain, row_sets, loaded, w_down, share):
    requests, width = row_sets[0].shape
    units = w_down.shape[0]
    set_count = len(row_sets)
    every = requests * set_count
    column = 512
    pieces = pieces_of(share, 4)
    parts = [part for _, _, part in loaded]

    def body(*refs):
        gain_ref, refs = refs[0], refs[1:]
        set_refs, refs = refs[:set_count], refs[set_count:]
        part_refs, refs = refs[: len(parts)], refs[len(parts) :]
        down_hbm, refs = refs[0], refs[1:]
        out_refs, refs = refs[:set_count], refs[set_count:]
        normed_ref, gate_ref, up_ref, hidden_ref, down_ref, down_sems = refs

        down_copy = (down_hbm, share_start(units, share), down_ref, down_sems)
        start_pieces(down_copy)

        rows = [ref[...].astype(jnp.float32) for ref in set_refs]
        rows = rows[0] if set_count == 1 else jnp.concatenate(rows, axis=0)
        inv_rms = lax.rsqrt(jnp.mean(rows * rows, axis=1, keepdims=True) + norm_eps)
        normed_ref[...] = (rows * inv_rms * gain_ref[...]).astype(jnp.bfloat16)

        for (which, first, _), ref in zip(loaded, part_refs):
            count = ref.shape[0]
            chunk = next((c for c in (192, 160, 128, 64) if count % c == 0), count)
            for j in range(0, count, chunk):
                (gate_ref, up_ref)[which][first + j : first + j + chunk, :] = lax.dot_general(
                    ref[j : j + chunk, :], normed_ref[...], (((1,), (1,)), ((), ())), preferred_element_type=jnp.float32
                )
        hidden = (jax.nn.silu(gate_ref[...]) * up_ref[...]).astype(jnp.bfloat16)
        place = lax.broadcasted_iota(jnp.int32, (every, every), 0)
        if set_count == 2:
            core = lax.axis_index("sub")
            other = place // requests
            distance = direct_offset(place % requests // 2, core ^ other)
            place = distance + ((place % 2) ^ other) * requests
        order = (lax.broadcasted_iota(jnp.int32, (every, every), 1) == place).astype(jnp.bfloat16)
        hidden_ref[...] = lax.dot_general(
            order, hidden, (((1,), (1,)), ((), ())), preferred_element_type=jnp.float32
        ).astype(jnp.bfloat16)

        wait_pieces(down_copy)
        for c in range(0, width, column):
            out = jnp.dot(hidden_ref[...], down_ref[:, c : c + column], preferred_element_type=jnp.float32)
            out_refs[0][:, c : c + column] = out[:requests]
            if set_count == 2:
                out_refs[1][:, c : c + column] = out[requests:].astype(jnp.bfloat16)

    outs = [
        jax.ShapeDtypeStruct((requests, width), jnp.float32),
        jax.ShapeDtypeStruct((requests, width), jnp.bfloat16),
    ][:set_count]
    return pl.pallas_call(
        body,
        out_shape=outs,
        in_specs=[VMEM] * (1 + set_count + len(parts)) + [ANY],
        out_specs=[VMEM] * set_count,
        scratch_shapes=[
            pltpu.VMEM((every, width), jnp.bfloat16),
            pltpu.VMEM((share, every), jnp.float32),
            pltpu.VMEM((share, every), jnp.float32),
            pltpu.VMEM((every, share), jnp.bfloat16),
            pltpu.VMEM((share, width), jnp.bfloat16),
            pltpu.SemaphoreType.DMA((pieces,)),
        ],
        compiler_params=pltpu.CompilerParams(vmem_limit_bytes=24 * MIB),
        cost_estimate=pl.CostEstimate(
            flops=6 * every * share * width,
            transcendentals=every * share,
            bytes_accessed=6 * share * width,
        ),
        name="feed_forward",
    )(gain[None], *row_sets, *parts, pinned(w_down))


def load_plan(share):
    if share % 192:
        return [(0, 0, share)], [(1, 0, share)]
    early = share // 3 * 2
    return [(0, 0, early)], [(0, early, share - early), (1, 0, share)]


def make_shards(size, cores):
    bits = size.bit_length() - 1

    def shards(queries, kv_cache, cache_lengths, live_counts, stream, norm_gain, w_gate, w_up, w_down):
        slots = queries.shape[1]
        units = w_gate.shape[0]
        split = cores == 2 and size == 8 and units % 32 == 0
        share = units // 2 if split else units
        weights = (w_gate, w_up)
        stages = [(0, bits)] if split else sum_stages(bits)
        plan = load_plan(share)
        loaded = []

        def load(kernel, jobs, *more):
            *parts, extra = kernel([(weights[which], first, rows) for which, first, rows in jobs], share, *more)
            loaded.extend((which, first, part) for (which, first, _), part in zip(jobs, parts))
            return extra

        block = stream[0]
        for step, (low, width) in enumerate(gather_stages(bits)):
            blocks = [block] + [swap(block, "tp", digit << low, size) for digit in range((1 << width) - 1, 0, -1)]
            if step == 0:
                pick = load(load_and_pick, plan[0], live_counts, slots, stages)
            if low > 1:
                block = jnp.concatenate(blocks, axis=0)

        own, send = compact(pick, blocks)
        arrived = swap(send, "tp", 1, size)
        cache = jnp.swapaxes(kv_cache[0], 1, 2)
        latent_ctx = load(load_and_attend, plan[1], queries[0], cache, cache_lengths, live_counts, send)[None]
        *last, part = loaded[-1]
        arrived, part = lax.optimization_barrier((arrived, part))
        loaded[-1] = (*last, part)
        rows = own + arrived
        row_sets = [rows, swap(rows, "sub", 1, cores)] if split else [rows]
        total, *other = feed_forward(norm_gain, row_sets, loaded, w_down, share)

        own_row = rows[:1].astype(jnp.float32)
        if split:
            total = total + swap(other[0], "sub", 1, cores).astype(jnp.float32)
            places = [total[2 * place : 2 * place + 2] for place in range(4)]
            sums = [
                direct_swap(places[place].astype(jnp.bfloat16), place, size).astype(jnp.float32)
                for place in (1, 2, 3, 0)
            ]
            total = jnp.where(lax.axis_index("sub") == 0, places[0], sums[3]) + sums[1] + sums[2] + sums[0]
            total = total[:1] + swap(total[1:], "sub", 1, cores)
        else:
            for step, (low, width) in enumerate(stages):
                part = total.shape[0] >> width
                sends = [total[digit * part : (digit + 1) * part] for digit in range(1, 1 << width)]
                total = total[:part]
                for digit, send in enumerate(sends, 1):
                    total = total + swap(send, "tp", digit << low, size)
        return (latent_ctx, (total + own_row).astype(jnp.bfloat16)[None])

    return shards


def solution(mesh):
    in_specs = (
        P(("groups", "sub"), "tp", None, None),
        P(("groups", "sub"), "tp", None, None),
        P(("groups", "sub"), "tp"),
        P(("groups", "sub"), None),
        P(("groups", "sub"), "tp", None),
        P(),
        P("tp", None),
        P("tp", None),
        P("tp", None),
    )
    out_specs = (P(("groups", "sub"), "tp", None, None), P(("groups", "sub"), "tp", None))
    return jax.shard_map(
        make_shards(mesh.shape["tp"], mesh.shape["sub"]),
        mesh=mesh,
        in_specs=in_specs,
        out_specs=out_specs,
        check_vma=False,
    )
```

```python
import jax
import jax.numpy as jnp
from jax import lax
from jax.experimental import pallas as pl
from jax.experimental.pallas import tpu as pltpu
from jax.sharding import PartitionSpec as P

KVL = 512
MIB = 1024 * 1024

score_scale = 192.0 ** (-0.5)
norm_eps = 1e-06

VMEM = pl.BlockSpec(memory_space=pltpu.VMEM)
ANY = pl.BlockSpec(memory_space=pl.ANY)


def gather_stages(bits):
    stages, top = [], bits
    while top > 1:
        width = 1 if top % 2 == 0 else 2
        top -= width
        stages.append((top, width))
    return stages


def sum_stages(bits):
    return [(low, min(2, bits - low)) for low in range(0, bits, 2)]


def direct_offset(place, core):
    return ((-place) & 3) | (core * 4)


def block_offset(position, stages):
    out = position * 0
    for low, width in stages:
        out = out | ((-position & ((1 << width) - 1)) << low)
        position = position >> width
    return out


def row_offset(position, stages):
    out = position * 0
    for low, width in stages[::-1]:
        out = out | ((position & ((1 << width) - 1)) << low)
        position = position >> width
    return out


def swap(x, axis, distance, size):
    return lax.ppermute(x, axis, [(i, i ^ distance) for i in range(size)])


def direct_swap(x, place, size):
    pairs = []
    for core in range(2):
        distance = direct_offset(place, core) or 2
        pairs += [(2 * i + core, 2 * (i ^ distance) + core) for i in range(size)]
    return lax.ppermute(x, ("tp", "sub"), pairs)


def pinned(weight):
    return pltpu.with_memory_space_constraint(weight, pltpu.HBM)


def row_copy(source, first, target, sems, i):
    step = target.shape[0] // sems.shape[0]
    here = pl.multiple_of(i * step, step)
    return pltpu.make_async_copy(source.at[pl.ds(first + here, step)], target.at[pl.ds(here, step)], sems.at[i])


def start_pieces(copy):
    @pl.loop(0, copy[-1].shape[0])
    def _(i):
        row_copy(*copy, i).start()


def wait_pieces(copy):
    @pl.loop(0, copy[-1].shape[0])
    def _(i):
        row_copy(*copy, i).wait()


def pieces_of(rows, most):
    return most if rows % (16 * most) == 0 else 1


def share_start(units, share):
    if share == units:
        return 0
    return pl.multiple_of(lax.axis_index("sub") * share, 16)


def pick_matrix(counts, device, size, slots, stages):
    bits = size.bit_length() - 1
    shape = (size, size // 2 * slots)
    slot = lax.broadcasted_iota(jnp.int32, shape, 1)
    every = lax.broadcasted_iota(jnp.int32, shape, 0)
    owner = block_offset(slot // slots, gather_stages(bits)) ^ device
    known = jnp.broadcast_to(counts, (8, size)).astype(jnp.bfloat16)
    start = jnp.dot(known, (every < owner).astype(jnp.bfloat16), preferred_element_type=jnp.float32)[:1]
    count = jnp.dot(known, (every == owner).astype(jnp.bfloat16), preferred_element_type=jnp.float32)[:1]
    place = (slot % slots)[:1].astype(jnp.float32)
    request = jnp.where(place < count, start + place, -1.0)
    row = lax.broadcasted_iota(jnp.int32, (2 * size, shape[1]), 0)
    wanted = row_offset(row % size, stages) ^ device ^ (row // size)
    return (request == wanted.astype(jnp.float32)).astype(jnp.bfloat16)


def attend(queries, cache, lengths, counts, after):
    slots, heads, _ = queries.shape
    positions = cache.shape[2]

    def body(lengths_ref, counts_ref, queries_ref, cache_ref, _, out_ref):
        lengths = lengths_ref[...]
        counts = counts_ref[...]
        here = lax.broadcasted_iota(jnp.int32, counts.shape, 1) == lax.axis_index("tp")
        live = jnp.sum(jnp.where(here, counts, 0), axis=1, keepdims=True)
        spot = lax.broadcasted_iota(jnp.int32, (heads, positions), 1)
        every = []
        for s in range(slots):
            scores = jnp.dot(queries_ref[s], cache_ref[s], preferred_element_type=jnp.float32) * score_scale
            every.append(jnp.where(spot < lengths[:, s : s + 1], scores, -jnp.inf))
        scores = jnp.concatenate(every, axis=0)
        weights = jnp.exp(scores - jnp.max(scores, axis=1, keepdims=True))
        probs = (weights / jnp.sum(weights, axis=1, keepdims=True)).astype(jnp.bfloat16)
        for s in range(slots):
            context = lax.dot_general(
                probs[s * heads : (s + 1) * heads],
                cache_ref[s, :KVL, :],
                (((1,), (1,)), ((), ())),
                preferred_element_type=jnp.float32,
            )
            out_ref[s] = jnp.where(s < live, context, 0.0).astype(jnp.bfloat16)

    return pl.pallas_call(
        body,
        out_shape=jax.ShapeDtypeStruct((slots, heads, KVL), jnp.bfloat16),
        in_specs=[VMEM] * 4 + [ANY],
        out_specs=VMEM,
        compiler_params=pltpu.CompilerParams(vmem_limit_bytes=8 * MIB),
        cost_estimate=pl.CostEstimate(
            flops=4 * slots * heads * positions * KVL,
            transcendentals=slots * heads * positions,
            bytes_accessed=2 * (queries.size + cache.size),
        ),
        name="attend",
    )(lengths, counts, queries, cache, after)


def load_rows(jobs, share, after=None, counts=None, slots=0, stages=()):
    size = 0 if counts is None else counts.shape[1]
    pieces = [pieces_of(rows, 2) for _, _, rows in jobs]
    operands = [pinned(weight) for weight, _, _ in jobs]
    out_shape = [pltpu.VMEM((rows, weight.shape[1]), weight.dtype) for weight, _, rows in jobs]
    scratch = [pltpu.SemaphoreType.DMA((count,)) for count in pieces]
    if counts is not None:
        operands.append(pinned(counts))
        out_shape.append(jax.ShapeDtypeStruct((2 * size, size // 2 * slots), jnp.bfloat16))
        scratch += [pltpu.VMEM((1, size), jnp.int32), pltpu.SemaphoreType.DMA]
    if after is not None:
        operands.append(after)

    def body(*refs):
        sources, refs = refs[: len(operands)], refs[len(operands) :]
        targets, refs = refs[: len(out_shape)], refs[len(out_shape) :]
        if counts is not None:
            small = pltpu.make_async_copy(sources[len(jobs)], refs[-2], refs[-1])
            small.start()
        copies = [
            (source, share_start(weight.shape[0], share) + first, target, sems)
            for (weight, first, _), source, target, sems in zip(jobs, sources, targets, refs)
        ]
        for copy in copies:
            start_pieces(copy)
        if counts is not None:
            small.wait()
            targets[-1][...] = pick_matrix(refs[-2][...], lax.axis_index("tp"), size, slots, stages)
        for copy in copies:
            wait_pieces(copy)

    return pl.pallas_call(
        body,
        out_shape=out_shape,
        in_specs=[ANY] * len(operands),
        out_specs=[VMEM] * len(out_shape),
        scratch_shapes=scratch,
        compiler_params=pltpu.CompilerParams(vmem_limit_bytes=2 * MIB),
        cost_estimate=pl.CostEstimate(
            flops=0, transcendentals=0, bytes_accessed=sum(4 * rows * weight.shape[1] for weight, _, rows in jobs)
        ),
        name="load_rows",
    )(*operands)


def compact(pick, blocks):
    size = pick.shape[0] // 2
    width = blocks[0].shape[1]
    column = 1024
    count = len(blocks)

    def body(*refs):
        pick_ref, block_refs, (own_ref, send_ref) = refs[0], refs[1 : 1 + count], refs[1 + count :]
        pick_now = pick_ref[...]
        for c in range(0, width, column):
            rows = [ref[:, c : c + column].astype(jnp.float32) for ref in block_refs]
            rows = rows[0] if count == 1 else jnp.concatenate(rows, axis=0)
            out = jnp.dot(pick_now, rows.astype(jnp.bfloat16), preferred_element_type=jnp.float32)
            own_ref[:, c : c + column] = out[:size].astype(jnp.bfloat16)
            send_ref[:, c : c + column] = out[size:].astype(jnp.bfloat16)

    out = jax.ShapeDtypeStruct((size, width), jnp.bfloat16)
    return pl.pallas_call(
        body,
        out_shape=(out, out),
        in_specs=[VMEM] * (1 + count),
        out_specs=(VMEM, VMEM),
        compiler_params=pltpu.CompilerParams(vmem_limit_bytes=16 * MIB),
        name="compact",
    )(pick, *blocks)


def feed_forward(gain, row_sets, loaded, w_down, share):
    requests, width = row_sets[0].shape
    units = w_down.shape[0]
    set_count = len(row_sets)
    every = requests * set_count
    column = 512
    pieces = pieces_of(share, 4)
    parts = [part for _, _, part in loaded]

    def body(*refs):
        gain_ref, refs = refs[0], refs[1:]
        set_refs, refs = refs[:set_count], refs[set_count:]
        part_refs, refs = refs[: len(parts)], refs[len(parts) :]
        down_hbm, refs = refs[0], refs[1:]
        out_refs, refs = refs[:set_count], refs[set_count:]
        normed_ref, gate_ref, up_ref, hidden_ref, down_ref, down_sems = refs

        down_copy = (down_hbm, share_start(units, share), down_ref, down_sems)
        start_pieces(down_copy)

        rows = [ref[...].astype(jnp.float32) for ref in set_refs]
        rows = rows[0] if set_count == 1 else jnp.concatenate(rows, axis=0)
        inv_rms = lax.rsqrt(jnp.mean(rows * rows, axis=1, keepdims=True) + norm_eps)
        normed_ref[...] = (rows * inv_rms * gain_ref[...]).astype(jnp.bfloat16)

        for (which, first, _), ref in zip(loaded, part_refs):
            count = ref.shape[0]
            chunk = next((c for c in (192, 160, 128, 64) if count % c == 0), count)
            for j in range(0, count, chunk):
                (gate_ref, up_ref)[which][first + j : first + j + chunk, :] = lax.dot_general(
                    ref[j : j + chunk, :], normed_ref[...], (((1,), (1,)), ((), ())), preferred_element_type=jnp.float32
                )
        hidden = (jax.nn.silu(gate_ref[...]) * up_ref[...]).astype(jnp.bfloat16)
        place = lax.broadcasted_iota(jnp.int32, (every, every), 0)
        if set_count == 2:
            core = lax.axis_index("sub")
            other = place // requests
            distance = direct_offset(place % requests // 2, core ^ other)
            place = distance + ((place % 2) ^ other) * requests
        order = (lax.broadcasted_iota(jnp.int32, (every, every), 1) == place).astype(jnp.bfloat16)
        hidden_ref[...] = lax.dot_general(
            order, hidden, (((1,), (1,)), ((), ())), preferred_element_type=jnp.float32
        ).astype(jnp.bfloat16)

        wait_pieces(down_copy)
        for c in range(0, width, column):
            out = jnp.dot(hidden_ref[...], down_ref[:, c : c + column], preferred_element_type=jnp.float32)
            out_refs[0][:, c : c + column] = out[:requests]
            if set_count == 2:
                out_refs[1][:, c : c + column] = out[requests:].astype(jnp.bfloat16)

    outs = [
        jax.ShapeDtypeStruct((requests, width), jnp.float32),
        jax.ShapeDtypeStruct((requests, width), jnp.bfloat16),
    ][:set_count]
    return pl.pallas_call(
        body,
        out_shape=outs,
        in_specs=[VMEM] * (1 + set_count + len(parts)) + [ANY],
        out_specs=[VMEM] * set_count,
        scratch_shapes=[
            pltpu.VMEM((every, width), jnp.bfloat16),
            pltpu.VMEM((share, every), jnp.float32),
            pltpu.VMEM((share, every), jnp.float32),
            pltpu.VMEM((every, share), jnp.bfloat16),
            pltpu.VMEM((share, width), jnp.bfloat16),
            pltpu.SemaphoreType.DMA((pieces,)),
        ],
        compiler_params=pltpu.CompilerParams(vmem_limit_bytes=24 * MIB),
        cost_estimate=pl.CostEstimate(
            flops=6 * every * share * width,
            transcendentals=every * share,
            bytes_accessed=6 * share * width,
        ),
        name="feed_forward",
    )(gain[None], *row_sets, *parts, pinned(w_down))


def load_plan(share):
    if share % 192:
        return [(0, 0, share)], [(1, 0, share)]
    early = share // 3 * 2
    return [(0, 0, early)], [(0, early, share - early), (1, 0, share)]


def make_shards(size, cores):
    bits = size.bit_length() - 1

    def shards(queries, kv_cache, cache_lengths, live_counts, stream, norm_gain, w_gate, w_up, w_down):
        slots = queries.shape[1]
        units = w_gate.shape[0]
        split = cores == 2 and size == 8 and units % 32 == 0
        share = units // 2 if split else units
        weights = (w_gate, w_up)
        stages = [(0, bits)] if split else sum_stages(bits)
        plan = load_plan(share)
        loaded = []

        def load(jobs, **more):
            parts = load_rows([(weights[which], first, rows) for which, first, rows in jobs], share, **more)
            loaded.extend((which, first, part) for (which, first, _), part in zip(jobs, parts))
            return parts[-1]

        block = stream[0]
        for step, (low, width) in enumerate(gather_stages(bits)):
            blocks = [block] + [swap(block, "tp", digit << low, size) for digit in range((1 << width) - 1, 0, -1)]
            if step == 0:
                pick = load(plan[0], counts=live_counts, slots=slots, stages=stages)
            if low > 1:
                block = jnp.concatenate(blocks, axis=0)

        own, send = compact(pick, blocks)
        arrived = swap(send, "tp", 1, size)
        load(plan[1], after=send)
        *last, part = loaded[-1]
        arrived, part = lax.optimization_barrier((arrived, part))
        loaded[-1] = (*last, part)
        rows = own + arrived
        row_sets = [rows, swap(rows, "sub", 1, cores)] if split else [rows]
        total, *other = feed_forward(norm_gain, row_sets, loaded, w_down, share)

        cache = jnp.swapaxes(kv_cache[0], 1, 2)
        after = other[0] if split else total
        latent_ctx = attend(queries[0], cache, cache_lengths, live_counts, after)
        own_row = rows[:1].astype(jnp.float32)
        if split:
            total = total + swap(other[0], "sub", 1, cores).astype(jnp.float32)
            places = [total[2 * place : 2 * place + 2] for place in range(4)]
            sums = [
                direct_swap(places[place].astype(jnp.bfloat16), place, size).astype(jnp.float32)
                for place in (1, 2, 3, 0)
            ]
            total = jnp.where(lax.axis_index("sub") == 0, places[0], sums[3]) + sums[0] + sums[2] + sums[1]
            total, latent_ctx = lax.optimization_barrier((total, latent_ctx))
            total = total[:1] + swap(total[1:], "sub", 1, cores)
        else:
            for step, (low, width) in enumerate(stages):
                part = total.shape[0] >> width
                sends = [total[digit * part : (digit + 1) * part] for digit in range(1, 1 << width)]
                total = total[:part]
                for digit, send in enumerate(sends, 1):
                    total = total + swap(send, "tp", digit << low, size)
        return (latent_ctx[None], (total + own_row).astype(jnp.bfloat16)[None])

    return shards


def solution(mesh):
    in_specs = (
        P(("groups", "sub"), "tp", None, None),
        P(("groups", "sub"), "tp", None, None),
        P(("groups", "sub"), "tp"),
        P(("groups", "sub"), None),
        P(("groups", "sub"), "tp", None),
        P(),
        P("tp", None),
        P("tp", None),
        P("tp", None),
    )
    out_specs = (P(("groups", "sub"), "tp", None, None), P(("groups", "sub"), "tp", None))
    return jax.shard_map(
        make_shards(mesh.shape["tp"], mesh.shape["sub"]),
        mesh=mesh,
        in_specs=in_specs,
        out_specs=out_specs,
        check_vma=False,
    )
```

```python
import jax
import jax.numpy as jnp
from jax import lax
from jax.experimental import pallas as pl
from jax.experimental.pallas import tpu as pltpu
from jax.sharding import PartitionSpec as P

KVL = 512
MIB = 1024 * 1024

score_scale = 192.0 ** (-0.5)
norm_eps = 1e-06

VMEM = pl.BlockSpec(memory_space=pltpu.VMEM)
ANY = pl.BlockSpec(memory_space=pl.ANY)


def gather_stages(bits):
    stages, top = [], bits
    while top > 1:
        width = 1 if top % 2 == 0 else 2
        top -= width
        stages.append((top, width))
    return stages


def sum_stages(bits):
    return [(low, min(2, bits - low)) for low in range(0, bits, 2)]


def direct_offset(place, core):
    return ((-place) & 3) | (core * 4)


def block_offset(position, stages):
    out = position * 0
    for low, width in stages:
        out = out | ((-position & ((1 << width) - 1)) << low)
        position = position >> width
    return out


def row_offset(position, stages):
    out = position * 0
    for low, width in stages[::-1]:
        out = out | ((position & ((1 << width) - 1)) << low)
        position = position >> width
    return out


def swap(x, axis, distance, size):
    return lax.ppermute(x, axis, [(i, i ^ distance) for i in range(size)])


def direct_swap(x, place, size):
    pairs = []
    for core in range(2):
        distance = direct_offset(place, core) or 2
        pairs += [(2 * i + core, 2 * (i ^ distance) + core) for i in range(size)]
    return lax.ppermute(x, ("tp", "sub"), pairs)


def pinned(weight):
    return pltpu.with_memory_space_constraint(weight, pltpu.HBM)


def row_copy(source, first, target, sems, i):
    step = target.shape[0] // sems.shape[0]
    here = pl.multiple_of(i * step, step)
    return pltpu.make_async_copy(source.at[pl.ds(first + here, step)], target.at[pl.ds(here, step)], sems.at[i])


def start_pieces(copy):
    @pl.loop(0, copy[-1].shape[0])
    def _(i):
        row_copy(*copy, i).start()


def wait_pieces(copy):
    @pl.loop(0, copy[-1].shape[0])
    def _(i):
        row_copy(*copy, i).wait()


def pieces_of(rows):
    return 2 if rows % 32 == 0 else 1


def share_start(units, share):
    if share == units:
        return 0
    return pl.multiple_of(lax.axis_index("sub") * share, 16)


def pick_matrix(counts, device, size, slots, stages):
    bits = size.bit_length() - 1
    shape = (size, size // 2 * slots)
    slot = lax.broadcasted_iota(jnp.int32, shape, 1)
    every = lax.broadcasted_iota(jnp.int32, shape, 0)
    owner = block_offset(slot // slots, gather_stages(bits)) ^ device
    known = jnp.broadcast_to(counts, (8, size)).astype(jnp.bfloat16)
    start = jnp.dot(known, (every < owner).astype(jnp.bfloat16), preferred_element_type=jnp.float32)[:1]
    count = jnp.dot(known, (every == owner).astype(jnp.bfloat16), preferred_element_type=jnp.float32)[:1]
    place = (slot % slots)[:1].astype(jnp.float32)
    request = jnp.where(place < count, start + place, -1.0)
    row = lax.broadcasted_iota(jnp.int32, (2 * size, shape[1]), 0)
    wanted = row_offset(row % size, stages) ^ device ^ (row // size)
    return (request == wanted.astype(jnp.float32)).astype(jnp.bfloat16)


def attend(queries, cache, lengths, counts, after):
    slots, heads, _ = queries.shape
    positions = cache.shape[2]

    def body(lengths_ref, counts_ref, queries_ref, cache_ref, _, out_ref):
        lengths = lengths_ref[...]
        counts = counts_ref[...]
        here = lax.broadcasted_iota(jnp.int32, counts.shape, 1) == lax.axis_index("tp")
        live = jnp.sum(jnp.where(here, counts, 0), axis=1, keepdims=True)
        spot = lax.broadcasted_iota(jnp.int32, (heads, positions), 1)
        every = []
        for s in range(slots):
            scores = jnp.dot(queries_ref[s], cache_ref[s], preferred_element_type=jnp.float32) * score_scale
            every.append(jnp.where(spot < lengths[:, s : s + 1], scores, -jnp.inf))
        scores = jnp.concatenate(every, axis=0)
        weights = jnp.exp(scores - jnp.max(scores, axis=1, keepdims=True))
        probs = (weights / jnp.sum(weights, axis=1, keepdims=True)).astype(jnp.bfloat16)
        for s in range(slots):
            context = lax.dot_general(
                probs[s * heads : (s + 1) * heads],
                cache_ref[s, :KVL, :],
                (((1,), (1,)), ((), ())),
                preferred_element_type=jnp.float32,
            )
            out_ref[s] = jnp.where(s < live, context, 0.0).astype(jnp.bfloat16)

    return pl.pallas_call(
        body,
        out_shape=jax.ShapeDtypeStruct((slots, heads, KVL), jnp.bfloat16),
        in_specs=[VMEM] * 4 + [ANY],
        out_specs=VMEM,
        compiler_params=pltpu.CompilerParams(vmem_limit_bytes=8 * MIB),
        cost_estimate=pl.CostEstimate(
            flops=4 * slots * heads * positions * KVL,
            transcendentals=slots * heads * positions,
            bytes_accessed=2 * (queries.size + cache.size),
        ),
        name="attend",
    )(lengths, counts, queries, cache, after)


def load_rows(weight, share, after=None, counts=None, slots=0, stages=()):
    size = 0 if counts is None else counts.shape[1]
    units, width = weight.shape
    operands = [pinned(weight)]
    out_shape = [pltpu.VMEM((share, width), weight.dtype)]
    scratch = [pltpu.SemaphoreType.DMA((pieces_of(share),))]
    if counts is not None:
        operands.append(pinned(counts))
        out_shape.append(jax.ShapeDtypeStruct((2 * size, size // 2 * slots), jnp.bfloat16))
        scratch += [pltpu.VMEM((1, size), jnp.int32), pltpu.SemaphoreType.DMA]
    if after is not None:
        operands.append(after)

    def body(*refs):
        sources, refs = refs[: len(operands)], refs[len(operands) :]
        targets, (sems, *small_refs) = refs[: len(out_shape)], refs[len(out_shape) :]
        if counts is not None:
            small = pltpu.make_async_copy(sources[1], *small_refs)
            small.start()
        copy = (sources[0], share_start(units, share), targets[0], sems)
        start_pieces(copy)
        if counts is not None:
            small.wait()
            targets[1][...] = pick_matrix(small_refs[0][...], lax.axis_index("tp"), size, slots, stages)
        wait_pieces(copy)

    return pl.pallas_call(
        body,
        out_shape=out_shape,
        in_specs=[ANY] * len(operands),
        out_specs=[VMEM] * len(out_shape),
        scratch_shapes=scratch,
        compiler_params=pltpu.CompilerParams(vmem_limit_bytes=2 * MIB),
        cost_estimate=pl.CostEstimate(flops=0, transcendentals=0, bytes_accessed=4 * share * width),
        name="load_rows",
    )(*operands)


def compact(pick, blocks):
    size = pick.shape[0] // 2
    width = blocks[0].shape[1]
    column = 1024
    count = len(blocks)

    def body(*refs):
        pick_ref, block_refs, (own_ref, send_ref) = refs[0], refs[1 : 1 + count], refs[1 + count :]
        pick_now = pick_ref[...]
        for c in range(0, width, column):
            rows = [ref[:, c : c + column].astype(jnp.float32) for ref in block_refs]
            rows = rows[0] if count == 1 else jnp.concatenate(rows, axis=0)
            out = jnp.dot(pick_now, rows.astype(jnp.bfloat16), preferred_element_type=jnp.float32)
            own_ref[:, c : c + column] = out[:size].astype(jnp.bfloat16)
            send_ref[:, c : c + column] = out[size:].astype(jnp.bfloat16)

    out = jax.ShapeDtypeStruct((size, width), jnp.bfloat16)
    return pl.pallas_call(
        body,
        out_shape=(out, out),
        in_specs=[VMEM] * (1 + count),
        out_specs=(VMEM, VMEM),
        compiler_params=pltpu.CompilerParams(vmem_limit_bytes=16 * MIB),
        name="compact",
    )(pick, *blocks)


def feed_forward(gain, row_sets, gate, up, w_down):
    requests, width = row_sets[0].shape
    units = w_down.shape[0]
    share = gate.shape[0]
    set_count = len(row_sets)
    every = requests * set_count
    column = 512
    chunk = 192 if share % 192 == 0 else share

    def body(*refs):
        gain_ref, refs = refs[0], refs[1:]
        set_refs, refs = refs[:set_count], refs[set_count:]
        gate_weight, up_weight, down_hbm, *refs = refs
        out_refs, refs = refs[:set_count], refs[set_count:]
        normed_ref, gate_ref, up_ref, hidden_ref, down_ref, down_sems = refs

        down_copy = (down_hbm, share_start(units, share), down_ref, down_sems)
        start_pieces(down_copy)

        rows = [ref[...].astype(jnp.float32) for ref in set_refs]
        rows = rows[0] if set_count == 1 else jnp.concatenate(rows, axis=0)
        inv_rms = lax.rsqrt(jnp.mean(rows * rows, axis=1, keepdims=True) + norm_eps)
        normed_ref[...] = (rows * inv_rms * gain_ref[...]).astype(jnp.bfloat16)

        for weight_ref, out_ref in ((gate_weight, gate_ref), (up_weight, up_ref)):
            for j in range(0, share, chunk):
                out_ref[j : j + chunk, :] = lax.dot_general(
                    weight_ref[j : j + chunk, :], normed_ref[...], (((1,), (1,)), ((), ())), preferred_element_type=jnp.float32
                )
        hidden = (jax.nn.silu(gate_ref[...]) * up_ref[...]).astype(jnp.bfloat16)
        place = lax.broadcasted_iota(jnp.int32, (every, every), 0)
        if set_count == 2:
            core = lax.axis_index("sub")
            other = place // requests
            distance = direct_offset(place % requests // 2, core ^ other)
            place = distance + ((place % 2) ^ other) * requests
        order = (lax.broadcasted_iota(jnp.int32, (every, every), 1) == place).astype(jnp.bfloat16)
        hidden_ref[...] = lax.dot_general(
            order, hidden, (((1,), (1,)), ((), ())), preferred_element_type=jnp.float32
        ).astype(jnp.bfloat16)

        wait_pieces(down_copy)
        for c in range(0, width, column):
            out = jnp.dot(hidden_ref[...], down_ref[:, c : c + column], preferred_element_type=jnp.float32)
            out_refs[0][:, c : c + column] = out[:requests]
            if set_count == 2:
                out_refs[1][:, c : c + column] = out[requests:].astype(jnp.bfloat16)

    outs = [
        jax.ShapeDtypeStruct((requests, width), jnp.float32),
        jax.ShapeDtypeStruct((requests, width), jnp.bfloat16),
    ][:set_count]
    return pl.pallas_call(
        body,
        out_shape=outs,
        in_specs=[VMEM] * (3 + set_count) + [ANY],
        out_specs=[VMEM] * set_count,
        scratch_shapes=[
            pltpu.VMEM((every, width), jnp.bfloat16),
            pltpu.VMEM((share, every), jnp.float32),
            pltpu.VMEM((share, every), jnp.float32),
            pltpu.VMEM((every, share), jnp.bfloat16),
            pltpu.VMEM((share, width), jnp.bfloat16),
            pltpu.SemaphoreType.DMA((pieces_of(share),)),
        ],
        compiler_params=pltpu.CompilerParams(vmem_limit_bytes=24 * MIB),
        cost_estimate=pl.CostEstimate(
            flops=6 * every * share * width,
            transcendentals=every * share,
            bytes_accessed=6 * share * width,
        ),
        name="feed_forward",
    )(gain[None], *row_sets, gate, up, pinned(w_down))


def make_shards(size, cores):
    bits = size.bit_length() - 1

    def shards(queries, kv_cache, cache_lengths, live_counts, stream, norm_gain, w_gate, w_up, w_down):
        slots = queries.shape[1]
        units = w_gate.shape[0]
        split = cores == 2 and size == 8 and units % 32 == 0
        share = units // 2 if split else units
        stages = [(0, bits)] if split else sum_stages(bits)
        block = stream[0]
        for step, (low, width) in enumerate(gather_stages(bits)):
            blocks = [block] + [swap(block, "tp", digit << low, size) for digit in range((1 << width) - 1, 0, -1)]
            if step == 0:
                gate, pick = load_rows(w_gate, share, counts=live_counts, slots=slots, stages=stages)
            if low > 1:
                block = jnp.concatenate(blocks, axis=0)

        own, send = compact(pick, blocks)
        arrived = swap(send, "tp", 1, size)
        (up,) = load_rows(w_up, share, after=send)
        arrived, up = lax.optimization_barrier((arrived, up))
        rows = own + arrived
        row_sets = [rows, swap(rows, "sub", 1, cores)] if split else [rows]
        total, *other = feed_forward(norm_gain, row_sets, gate, up, w_down)

        cache = jnp.swapaxes(kv_cache[0], 1, 2)
        after = other[0] if split else total
        latent_ctx = attend(queries[0], cache, cache_lengths, live_counts, after)
        own_row = rows[:1].astype(jnp.float32)
        if split:
            total = total + swap(other[0], "sub", 1, cores).astype(jnp.float32)
            places = [total[2 * place : 2 * place + 2] for place in range(4)]
            sums = [
                direct_swap(places[place].astype(jnp.bfloat16), place, size).astype(jnp.float32)
                for place in (1, 2, 3, 0)
            ]
            total = jnp.where(lax.axis_index("sub") == 0, places[0], sums[3]) + sums[0] + sums[2] + sums[1]
            total, latent_ctx = lax.optimization_barrier((total, latent_ctx))
            total = total[:1] + swap(total[1:], "sub", 1, cores)
        else:
            for step, (low, width) in enumerate(stages):
                part = total.shape[0] >> width
                sends = [total[digit * part : (digit + 1) * part] for digit in range(1, 1 << width)]
                total = total[:part]
                for digit, send in enumerate(sends, 1):
                    total = total + swap(send, "tp", digit << low, size)
        return (latent_ctx[None], (total + own_row).astype(jnp.bfloat16)[None])

    return shards


def solution(mesh):
    in_specs = (
        P(("groups", "sub"), "tp", None, None),
        P(("groups", "sub"), "tp", None, None),
        P(("groups", "sub"), "tp"),
        P(("groups", "sub"), None),
        P(("groups", "sub"), "tp", None),
        P(),
        P("tp", None),
        P("tp", None),
        P("tp", None),
    )
    out_specs = (P(("groups", "sub"), "tp", None, None), P(("groups", "sub"), "tp", None))
    return jax.shard_map(
        make_shards(mesh.shape["tp"], mesh.shape["sub"]),
        mesh=mesh,
        in_specs=in_specs,
        out_specs=out_specs,
        check_vma=False,
    )
```

```python
import jax
import jax.numpy as jnp
from jax import lax
from jax.experimental import pallas as pl
from jax.experimental.pallas import tpu as pltpu
from jax.sharding import PartitionSpec as P

KVL = 512
MIB = 1024 * 1024

score_scale = 192.0 ** (-0.5)
norm_eps = 1e-06

VMEM = pl.BlockSpec(memory_space=pltpu.VMEM)
ANY = pl.BlockSpec(memory_space=pl.ANY)


def gather_stages(bits):
    stages, top = [], bits
    while top > 1:
        width = 1 if top % 2 == 0 else 2
        top -= width
        stages.append((top, width))
    return stages


def sum_stages(bits):
    return [(low, min(2, bits - low)) for low in range(0, bits, 2)]


def direct_offset(place, core):
    near = -place & 3
    far = place ^ (7 - (place >> 1))
    return near + core * (far - near)


def block_offset(position, stages):
    out = position * 0
    for low, width in stages:
        out = out | ((-position & ((1 << width) - 1)) << low)
        position = position >> width
    return out


def row_offset(position, stages):
    out = position * 0
    for low, width in stages[::-1]:
        out = out | ((position & ((1 << width) - 1)) << low)
        position = position >> width
    return out


def swap(x, axis, distance, size):
    return lax.ppermute(x, axis, [(i, i ^ distance) for i in range(size)])


def direct_swap(x, place, size):
    pairs = [(2 * i + core, 2 * (i ^ direct_offset(place, core)) + core) for i in range(size) for core in range(2)]
    return lax.ppermute(x, ("tp", "sub"), pairs)


def pinned(weight):
    return pltpu.with_memory_space_constraint(weight, pltpu.HBM)


def row_copy(source, first, target, sems, i):
    step = target.shape[0] // sems.shape[0]
    here = pl.multiple_of(i * step, step)
    return pltpu.make_async_copy(source.at[pl.ds(first + here, step)], target.at[pl.ds(here, step)], sems.at[i])


def start_pieces(copy):
    @pl.loop(0, copy[-1].shape[0])
    def _(i):
        row_copy(*copy, i).start()


def wait_pieces(copy):
    @pl.loop(0, copy[-1].shape[0])
    def _(i):
        row_copy(*copy, i).wait()


def pieces_of(rows):
    return 2 if rows % 32 == 0 else 1


def share_start(units, share):
    if share == units:
        return 0
    return pl.multiple_of(lax.axis_index("sub") * share, 16)


def pick_matrix(counts, device, size, slots, stages):
    bits = size.bit_length() - 1
    shape = (size, size // 2 * slots)
    slot = lax.broadcasted_iota(jnp.int32, shape, 1)
    every = lax.broadcasted_iota(jnp.int32, shape, 0)
    owner = block_offset(slot // slots, gather_stages(bits)) ^ device
    known = jnp.broadcast_to(counts, (8, size)).astype(jnp.bfloat16)
    start = jnp.dot(known, (every < owner).astype(jnp.bfloat16), preferred_element_type=jnp.float32)[:1]
    count = jnp.dot(known, (every == owner).astype(jnp.bfloat16), preferred_element_type=jnp.float32)[:1]
    place = (slot % slots)[:1].astype(jnp.float32)
    request = jnp.where(place < count, start + place, -1.0)
    row = lax.broadcasted_iota(jnp.int32, (2 * size, shape[1]), 0)
    wanted = row_offset(row % size, stages) ^ device ^ (row // size)
    return (request == wanted.astype(jnp.float32)).astype(jnp.bfloat16)


def attend(queries, cache, lengths, counts, after):
    slots, heads, _ = queries.shape
    positions = cache.shape[2]

    def body(lengths_ref, counts_ref, queries_ref, cache_ref, _, out_ref):
        lengths = lengths_ref[...]
        counts = counts_ref[...]
        here = lax.broadcasted_iota(jnp.int32, counts.shape, 1) == lax.axis_index("tp")
        live = jnp.sum(jnp.where(here, counts, 0), axis=1, keepdims=True)
        spot = lax.broadcasted_iota(jnp.int32, (heads, positions), 1)
        every = []
        for s in range(slots):
            scores = jnp.dot(queries_ref[s], cache_ref[s], preferred_element_type=jnp.float32) * score_scale
            every.append(jnp.where(spot < lengths[:, s : s + 1], scores, -jnp.inf))
        scores = jnp.concatenate(every, axis=0)
        weights = jnp.exp(scores - jnp.max(scores, axis=1, keepdims=True))
        probs = (weights / jnp.sum(weights, axis=1, keepdims=True)).astype(jnp.bfloat16)
        for s in range(slots):
            context = lax.dot_general(
                probs[s * heads : (s + 1) * heads],
                cache_ref[s, :KVL, :],
                (((1,), (1,)), ((), ())),
                preferred_element_type=jnp.float32,
            )
            out_ref[s] = jnp.where(s < live, context, 0.0).astype(jnp.bfloat16)

    return pl.pallas_call(
        body,
        out_shape=jax.ShapeDtypeStruct((slots, heads, KVL), jnp.bfloat16),
        in_specs=[VMEM] * 4 + [ANY],
        out_specs=VMEM,
        compiler_params=pltpu.CompilerParams(vmem_limit_bytes=8 * MIB),
        cost_estimate=pl.CostEstimate(
            flops=4 * slots * heads * positions * KVL,
            transcendentals=slots * heads * positions,
            bytes_accessed=2 * (queries.size + cache.size),
        ),
        name="attend",
    )(lengths, counts, queries, cache, after)


def load_rows(weight, share, after=None, counts=None, slots=0, stages=()):
    size = 0 if counts is None else counts.shape[1]
    units, width = weight.shape
    operands = [pinned(weight)]
    out_shape = [pltpu.VMEM((share, width), weight.dtype)]
    scratch = [pltpu.SemaphoreType.DMA((pieces_of(share),))]
    if counts is not None:
        operands.append(pinned(counts))
        out_shape.append(jax.ShapeDtypeStruct((2 * size, size // 2 * slots), jnp.bfloat16))
        scratch += [pltpu.VMEM((1, size), jnp.int32), pltpu.SemaphoreType.DMA]
    if after is not None:
        operands.append(after)

    def body(*refs):
        sources, refs = refs[: len(operands)], refs[len(operands) :]
        targets, (sems, *small_refs) = refs[: len(out_shape)], refs[len(out_shape) :]
        if counts is not None:
            small = pltpu.make_async_copy(sources[1], *small_refs)
            small.start()
        copy = (sources[0], share_start(units, share), targets[0], sems)
        start_pieces(copy)
        if counts is not None:
            small.wait()
            targets[1][...] = pick_matrix(small_refs[0][...], lax.axis_index("tp"), size, slots, stages)
        wait_pieces(copy)

    return pl.pallas_call(
        body,
        out_shape=out_shape,
        in_specs=[ANY] * len(operands),
        out_specs=[VMEM] * len(out_shape),
        scratch_shapes=scratch,
        compiler_params=pltpu.CompilerParams(vmem_limit_bytes=2 * MIB),
        cost_estimate=pl.CostEstimate(flops=0, transcendentals=0, bytes_accessed=4 * share * width),
        name="load_rows",
    )(*operands)


def compact(pick, blocks):
    size = pick.shape[0] // 2
    width = blocks[0].shape[1]
    column = 1024
    count = len(blocks)

    def body(*refs):
        pick_ref, block_refs, (own_ref, send_ref) = refs[0], refs[1 : 1 + count], refs[1 + count :]
        pick_now = pick_ref[...]
        for c in range(0, width, column):
            rows = [ref[:, c : c + column].astype(jnp.float32) for ref in block_refs]
            rows = rows[0] if count == 1 else jnp.concatenate(rows, axis=0)
            out = jnp.dot(pick_now, rows.astype(jnp.bfloat16), preferred_element_type=jnp.float32)
            own_ref[:, c : c + column] = out[:size].astype(jnp.bfloat16)
            send_ref[:, c : c + column] = out[size:].astype(jnp.bfloat16)

    out = jax.ShapeDtypeStruct((size, width), jnp.bfloat16)
    return pl.pallas_call(
        body,
        out_shape=(out, out),
        in_specs=[VMEM] * (1 + count),
        out_specs=(VMEM, VMEM),
        compiler_params=pltpu.CompilerParams(vmem_limit_bytes=16 * MIB),
        name="compact",
    )(pick, *blocks)


def feed_forward(gain, row_sets, gate, up, w_down):
    requests, width = row_sets[0].shape
    units = w_down.shape[0]
    share = gate.shape[0]
    set_count = len(row_sets)
    every = requests * set_count
    column = 512
    chunk = 192 if share % 192 == 0 else share

    outs = [jax.ShapeDtypeStruct((requests, width), jnp.float32)]
    if set_count == 2:
        outs.append(jax.ShapeDtypeStruct((requests, width), jnp.bfloat16))
        outs.append(jax.ShapeDtypeStruct((2, width), jnp.bfloat16))

    def body(*refs):
        gain_ref, refs = refs[0], refs[1:]
        set_refs, refs = refs[:set_count], refs[set_count:]
        gate_weight, up_weight, down_hbm, *refs = refs
        out_refs, refs = refs[: len(outs)], refs[len(outs) :]
        normed_ref, gate_ref, up_ref, hidden_ref, down_ref, down_sems = refs

        down_copy = (down_hbm, share_start(units, share), down_ref, down_sems)
        start_pieces(down_copy)

        rows = [ref[...].astype(jnp.float32) for ref in set_refs]
        rows = rows[0] if set_count == 1 else jnp.concatenate(rows, axis=0)
        inv_rms = lax.rsqrt(jnp.mean(rows * rows, axis=1, keepdims=True) + norm_eps)
        normed_ref[...] = (rows * inv_rms * gain_ref[...]).astype(jnp.bfloat16)

        for weight_ref, out_ref in ((gate_weight, gate_ref), (up_weight, up_ref)):
            for j in range(0, share, chunk):
                out_ref[j : j + chunk, :] = lax.dot_general(
                    weight_ref[j : j + chunk, :], normed_ref[...], (((1,), (1,)), ((), ())), preferred_element_type=jnp.float32
                )
        hidden = (jax.nn.silu(gate_ref[...]) * up_ref[...]).astype(jnp.bfloat16)
        place = lax.broadcasted_iota(jnp.int32, (every, every), 0)
        if set_count == 2:
            core = lax.axis_index("sub")
            other = place // requests
            holder = core ^ other
            spot = place % requests // 2
            flipped = jnp.where((spot == 0) & (holder == 1), 0, other)
            place = direct_offset(spot, holder) + ((place % 2) ^ flipped) * requests
        order = (lax.broadcasted_iota(jnp.int32, (every, every), 1) == place).astype(jnp.bfloat16)
        hidden_ref[...] = lax.dot_general(
            order, hidden, (((1,), (1,)), ((), ())), preferred_element_type=jnp.float32
        ).astype(jnp.bfloat16)

        wait_pieces(down_copy)
        for c in range(0, width, column):
            out = jnp.dot(hidden_ref[...], down_ref[:, c : c + column], preferred_element_type=jnp.float32)
            out_refs[0][:, c : c + column] = out[:requests]
            if set_count == 2:
                out_refs[1][:, c : c + column] = out[requests:].astype(jnp.bfloat16)
                farthest = jnp.where(core == 1, out[:2], out[requests : requests + 2])
                out_refs[2][:, c : c + column] = farthest.astype(jnp.bfloat16)

    return pl.pallas_call(
        body,
        out_shape=outs,
        in_specs=[VMEM] * (3 + set_count) + [ANY],
        out_specs=[VMEM] * len(outs),
        scratch_shapes=[
            pltpu.VMEM((every, width), jnp.bfloat16),
            pltpu.VMEM((share, every), jnp.float32),
            pltpu.VMEM((share, every), jnp.float32),
            pltpu.VMEM((every, share), jnp.bfloat16),
            pltpu.VMEM((share, width), jnp.bfloat16),
            pltpu.SemaphoreType.DMA((pieces_of(share),)),
        ],
        compiler_params=pltpu.CompilerParams(vmem_limit_bytes=24 * MIB),
        cost_estimate=pl.CostEstimate(
            flops=6 * every * share * width,
            transcendentals=every * share,
            bytes_accessed=6 * share * width,
        ),
        name="feed_forward",
    )(gain[None], *row_sets, gate, up, pinned(w_down))


def make_shards(size, cores):
    bits = size.bit_length() - 1

    def shards(queries, kv_cache, cache_lengths, live_counts, stream, norm_gain, w_gate, w_up, w_down):
        slots = queries.shape[1]
        units = w_gate.shape[0]
        split = cores == 2 and size == 8 and units % 32 == 0
        share = units // 2 if split else units
        stages = [(0, bits)] if split else sum_stages(bits)
        block = stream[0]
        for step, (low, width) in enumerate(gather_stages(bits)):
            blocks = [block] + [swap(block, "tp", digit << low, size) for digit in range((1 << width) - 1, 0, -1)]
            if step == 0:
                gate, pick = load_rows(w_gate, share, counts=live_counts, slots=slots, stages=stages)
            if low > 1:
                block = jnp.concatenate(blocks, axis=0)

        own, send = compact(pick, blocks)
        arrived = swap(send, "tp", 1, size)
        (up,) = load_rows(w_up, share, after=send)
        arrived, up = lax.optimization_barrier((arrived, up))
        rows = own + arrived
        row_sets = [rows, swap(rows, "sub", 1, cores)] if split else [rows]
        total, *other = feed_forward(norm_gain, row_sets, gate, up, w_down)

        cache = jnp.swapaxes(kv_cache[0], 1, 2)
        after = other[0] if split else total
        latent_ctx = attend(queries[0], cache, cache_lengths, live_counts, after)
        own_row = rows[:1].astype(jnp.float32)
        if split:
            send, far = other
            total = total + swap(send, "sub", 1, cores).astype(jnp.float32)
            far = swap(far, "tp", direct_offset(0, 1), size).astype(jnp.float32)
            sums = [
                direct_swap(total[2 * place : 2 * place + 2].astype(jnp.bfloat16), place, size).astype(jnp.float32)
                for place in (1, 2, 3)
            ]
            own = jnp.where(lax.axis_index("sub") == 0, total[:2], 0.0) + far
            total = own + sums[0] + sums[2] + sums[1]
            total, latent_ctx = lax.optimization_barrier((total, latent_ctx))
            total = total[:1] + swap(total[1:], "sub", 1, cores)
        else:
            for step, (low, width) in enumerate(stages):
                part = total.shape[0] >> width
                sends = [total[digit * part : (digit + 1) * part] for digit in range(1, 1 << width)]
                total = total[:part]
                for digit, send in enumerate(sends, 1):
                    total = total + swap(send, "tp", digit << low, size)
        return (latent_ctx[None], (total + own_row).astype(jnp.bfloat16)[None])

    return shards


def solution(mesh):
    in_specs = (
        P(("groups", "sub"), "tp", None, None),
        P(("groups", "sub"), "tp", None, None),
        P(("groups", "sub"), "tp"),
        P(("groups", "sub"), None),
        P(("groups", "sub"), "tp", None),
        P(),
        P("tp", None),
        P("tp", None),
        P("tp", None),
    )
    out_specs = (P(("groups", "sub"), "tp", None, None), P(("groups", "sub"), "tp", None))
    return jax.shard_map(
        make_shards(mesh.shape["tp"], mesh.shape["sub"]),
        mesh=mesh,
        in_specs=in_specs,
        out_specs=out_specs,
        check_vma=False,
    )
```

```python
import jax
import jax.numpy as jnp
from jax import lax
from jax.experimental import pallas as pl
from jax.experimental.pallas import tpu as pltpu
from jax.sharding import PartitionSpec as P

KVL = 512
MIB = 1024 * 1024

score_scale = 192.0 ** (-0.5)
norm_eps = 1e-06

VMEM = pl.BlockSpec(memory_space=pltpu.VMEM)
ANY = pl.BlockSpec(memory_space=pl.ANY)


def gather_stages(bits):
    stages, top = [], bits
    while top > 1:
        width = 1 if top % 2 == 0 else 2
        top -= width
        stages.append((top, width))
    return stages


def sum_stages(bits):
    return [(low, min(2, bits - low)) for low in range(0, bits, 2)]


def direct_offset(place, core):
    near = -place & 3
    far = place ^ 6
    return near + core * (far - near)


def block_offset(position, stages):
    out = position * 0
    for low, width in stages:
        out = out | ((-position & ((1 << width) - 1)) << low)
        position = position >> width
    return out


def row_offset(position, stages):
    out = position * 0
    for low, width in stages[::-1]:
        out = out | ((position & ((1 << width) - 1)) << low)
        position = position >> width
    return out


def swap(x, axis, distance, size):
    return lax.ppermute(x, axis, [(i, i ^ distance) for i in range(size)])


def direct_swap(x, place, size):
    pairs = [(2 * i + core, 2 * (i ^ direct_offset(place, core)) + core) for i in range(size) for core in range(2)]
    return lax.ppermute(x, ("tp", "sub"), pairs)


def pinned(weight):
    return pltpu.with_memory_space_constraint(weight, pltpu.HBM)


def row_copy(source, first, target, sems, i):
    step = target.shape[0] // sems.shape[0]
    here = pl.multiple_of(i * step, step)
    return pltpu.make_async_copy(source.at[pl.ds(first + here, step)], target.at[pl.ds(here, step)], sems.at[i])


def start_pieces(copy):
    @pl.loop(0, copy[-1].shape[0])
    def _(i):
        row_copy(*copy, i).start()


def wait_pieces(copy):
    @pl.loop(0, copy[-1].shape[0])
    def _(i):
        row_copy(*copy, i).wait()


def pieces_of(rows):
    return 2 if rows % 32 == 0 else 1


def share_start(units, share):
    if share == units:
        return 0
    return pl.multiple_of(lax.axis_index("sub") * share, 16)


def pick_matrix(counts, device, size, slots, stages):
    bits = size.bit_length() - 1
    shape = (size, size // 2 * slots)
    slot = lax.broadcasted_iota(jnp.int32, shape, 1)
    every = lax.broadcasted_iota(jnp.int32, shape, 0)
    owner = block_offset(slot // slots, gather_stages(bits)) ^ device
    known = jnp.broadcast_to(counts, (8, size)).astype(jnp.bfloat16)
    start = jnp.dot(known, (every < owner).astype(jnp.bfloat16), preferred_element_type=jnp.float32)[:1]
    count = jnp.dot(known, (every == owner).astype(jnp.bfloat16), preferred_element_type=jnp.float32)[:1]
    place = (slot % slots)[:1].astype(jnp.float32)
    request = jnp.where(place < count, start + place, -1.0)
    row = lax.broadcasted_iota(jnp.int32, (2 * size, shape[1]), 0)
    wanted = row_offset(row % size, stages) ^ device ^ (row // size)
    return (request == wanted.astype(jnp.float32)).astype(jnp.bfloat16)


def attend(queries, cache, lengths, counts, after):
    slots, heads, _ = queries.shape
    positions = cache.shape[2]

    def body(lengths_ref, counts_ref, queries_ref, cache_ref, _, out_ref):
        lengths = lengths_ref[...]
        counts = counts_ref[...]
        here = lax.broadcasted_iota(jnp.int32, counts.shape, 1) == lax.axis_index("tp")
        live = jnp.sum(jnp.where(here, counts, 0), axis=1, keepdims=True)
        spot = lax.broadcasted_iota(jnp.int32, (heads, positions), 1)
        every = []
        for s in range(slots):
            scores = jnp.dot(queries_ref[s], cache_ref[s], preferred_element_type=jnp.float32) * score_scale
            every.append(jnp.where(spot < lengths[:, s : s + 1], scores, -jnp.inf))
        scores = jnp.concatenate(every, axis=0)
        weights = jnp.exp(scores - jnp.max(scores, axis=1, keepdims=True))
        probs = (weights / jnp.sum(weights, axis=1, keepdims=True)).astype(jnp.bfloat16)
        for s in range(slots):
            context = lax.dot_general(
                probs[s * heads : (s + 1) * heads],
                cache_ref[s, :KVL, :],
                (((1,), (1,)), ((), ())),
                preferred_element_type=jnp.float32,
            )
            out_ref[s] = jnp.where(s < live, context, 0.0).astype(jnp.bfloat16)

    return pl.pallas_call(
        body,
        out_shape=jax.ShapeDtypeStruct((slots, heads, KVL), jnp.bfloat16),
        in_specs=[VMEM] * 4 + [ANY],
        out_specs=VMEM,
        compiler_params=pltpu.CompilerParams(vmem_limit_bytes=8 * MIB),
        cost_estimate=pl.CostEstimate(
            flops=4 * slots * heads * positions * KVL,
            transcendentals=slots * heads * positions,
            bytes_accessed=2 * (queries.size + cache.size),
        ),
        name="attend",
    )(lengths, counts, queries, cache, after)


def load_rows(weight, share, after=None, counts=None, slots=0, stages=()):
    size = 0 if counts is None else counts.shape[1]
    units, width = weight.shape
    operands = [pinned(weight)]
    out_shape = [pltpu.VMEM((share, width), weight.dtype)]
    scratch = [pltpu.SemaphoreType.DMA((pieces_of(share),))]
    if counts is not None:
        operands.append(pinned(counts))
        out_shape.append(jax.ShapeDtypeStruct((2 * size, size // 2 * slots), jnp.bfloat16))
        scratch += [pltpu.VMEM((1, size), jnp.int32), pltpu.SemaphoreType.DMA]
    if after is not None:
        operands.append(after)

    def body(*refs):
        sources, refs = refs[: len(operands)], refs[len(operands) :]
        targets, (sems, *small_refs) = refs[: len(out_shape)], refs[len(out_shape) :]
        if counts is not None:
            small = pltpu.make_async_copy(sources[1], *small_refs)
            small.start()
        copy = (sources[0], share_start(units, share), targets[0], sems)
        start_pieces(copy)
        if counts is not None:
            small.wait()
            targets[1][...] = pick_matrix(small_refs[0][...], lax.axis_index("tp"), size, slots, stages)
        wait_pieces(copy)

    return pl.pallas_call(
        body,
        out_shape=out_shape,
        in_specs=[ANY] * len(operands),
        out_specs=[VMEM] * len(out_shape),
        scratch_shapes=scratch,
        compiler_params=pltpu.CompilerParams(vmem_limit_bytes=2 * MIB),
        cost_estimate=pl.CostEstimate(flops=0, transcendentals=0, bytes_accessed=4 * share * width),
        name="load_rows",
    )(*operands)


def compact(pick, blocks):
    size = pick.shape[0] // 2
    width = blocks[0].shape[1]
    column = 1024
    count = len(blocks)

    def body(*refs):
        pick_ref, block_refs, (own_ref, send_ref) = refs[0], refs[1 : 1 + count], refs[1 + count :]
        pick_now = pick_ref[...]
        for c in range(0, width, column):
            rows = [ref[:, c : c + column].astype(jnp.float32) for ref in block_refs]
            rows = rows[0] if count == 1 else jnp.concatenate(rows, axis=0)
            out = jnp.dot(pick_now, rows.astype(jnp.bfloat16), preferred_element_type=jnp.float32)
            own_ref[:, c : c + column] = out[:size].astype(jnp.bfloat16)
            send_ref[:, c : c + column] = out[size:].astype(jnp.bfloat16)

    out = jax.ShapeDtypeStruct((size, width), jnp.bfloat16)
    return pl.pallas_call(
        body,
        out_shape=(out, out),
        in_specs=[VMEM] * (1 + count),
        out_specs=(VMEM, VMEM),
        compiler_params=pltpu.CompilerParams(vmem_limit_bytes=16 * MIB),
        name="compact",
    )(pick, *blocks)


def feed_forward(gain, row_sets, gate, up, w_down):
    requests, width = row_sets[0].shape
    units = w_down.shape[0]
    share = gate.shape[0]
    set_count = len(row_sets)
    every = requests * set_count
    column = 512
    chunk = 192 if share % 192 == 0 else share

    outs = [jax.ShapeDtypeStruct((requests, width), jnp.float32)]
    if set_count == 2:
        outs.append(jax.ShapeDtypeStruct((requests, width), jnp.bfloat16))
        outs.append(jax.ShapeDtypeStruct((2, width), jnp.bfloat16))

    def body(*refs):
        gain_ref, refs = refs[0], refs[1:]
        set_refs, refs = refs[:set_count], refs[set_count:]
        gate_weight, up_weight, down_hbm, *refs = refs
        out_refs, refs = refs[: len(outs)], refs[len(outs) :]
        scaled_ref, gate_ref, up_ref, hidden_ref, down_ref, down_sems = refs

        down_copy = (down_hbm, share_start(units, share), down_ref, down_sems)
        start_pieces(down_copy)

        rows = [ref[...].astype(jnp.float32) for ref in set_refs]
        rows = rows[0] if set_count == 1 else jnp.concatenate(rows, axis=0)
        scaled_ref[...] = (rows * gain_ref[...]).astype(jnp.bfloat16)
        inv_rms = lax.rsqrt(jnp.mean(rows * rows, axis=1, keepdims=True) + norm_eps).T

        for weight_ref, out_ref in ((gate_weight, gate_ref), (up_weight, up_ref)):
            for j in range(0, share, chunk):
                out_ref[j : j + chunk, :] = lax.dot_general(
                    weight_ref[j : j + chunk, :], scaled_ref[...], (((1,), (1,)), ((), ())), preferred_element_type=jnp.float32
                )
        hidden = (jax.nn.silu(gate_ref[...] * inv_rms) * (up_ref[...] * inv_rms)).astype(jnp.bfloat16)
        place = lax.broadcasted_iota(jnp.int32, (every, every), 0)
        if set_count == 2:
            core = lax.axis_index("sub")
            other = place // requests
            holder = core ^ other
            spot = place % requests // 2
            flipped = jnp.where((spot == 0) & (holder == 1), 0, other)
            place = direct_offset(spot, holder) + ((place % 2) ^ flipped) * requests
        order = (lax.broadcasted_iota(jnp.int32, (every, every), 1) == place).astype(jnp.bfloat16)
        hidden_ref[...] = lax.dot_general(
            order, hidden, (((1,), (1,)), ((), ())), preferred_element_type=jnp.float32
        ).astype(jnp.bfloat16)

        wait_pieces(down_copy)
        for c in range(0, width, column):
            out = jnp.dot(hidden_ref[...], down_ref[:, c : c + column], preferred_element_type=jnp.float32)
            out_refs[0][:, c : c + column] = out[:requests]
            if set_count == 2:
                out_refs[1][:, c : c + column] = out[requests:].astype(jnp.bfloat16)
                far = jnp.where(core == 1, out[:2], out[requests : requests + 2])
                out_refs[2][:, c : c + column] = far.astype(jnp.bfloat16)

    return pl.pallas_call(
        body,
        out_shape=outs,
        in_specs=[VMEM] * (3 + set_count) + [ANY],
        out_specs=[VMEM] * len(outs),
        scratch_shapes=[
            pltpu.VMEM((every, width), jnp.bfloat16),
            pltpu.VMEM((share, every), jnp.float32),
            pltpu.VMEM((share, every), jnp.float32),
            pltpu.VMEM((every, share), jnp.bfloat16),
            pltpu.VMEM((share, width), jnp.bfloat16),
            pltpu.SemaphoreType.DMA((pieces_of(share),)),
        ],
        compiler_params=pltpu.CompilerParams(vmem_limit_bytes=24 * MIB),
        cost_estimate=pl.CostEstimate(
            flops=6 * every * share * width,
            transcendentals=every * share,
            bytes_accessed=6 * share * width,
        ),
        name="feed_forward",
    )(gain[None], *row_sets, gate, up, pinned(w_down))


def make_shards(size, cores):
    bits = size.bit_length() - 1

    def shards(queries, kv_cache, cache_lengths, live_counts, stream, norm_gain, w_gate, w_up, w_down):
        slots = queries.shape[1]
        units = w_gate.shape[0]
        split = cores == 2 and size == 8 and units % 32 == 0
        share = units // 2 if split else units
        stages = [(0, bits)] if split else sum_stages(bits)
        block = stream[0]
        for step, (low, width) in enumerate(gather_stages(bits)):
            blocks = [block] + [swap(block, "tp", digit << low, size) for digit in range((1 << width) - 1, 0, -1)]
            if step == 0:
                gate, pick = load_rows(w_gate, share, counts=live_counts, slots=slots, stages=stages)
            if low > 1:
                block = jnp.concatenate(blocks, axis=0)

        own, send = compact(pick, blocks)
        arrived = swap(send, "tp", 1, size)
        (up,) = load_rows(w_up, share, after=send)
        arrived, up = lax.optimization_barrier((arrived, up))
        rows = own + arrived
        row_sets = [rows, swap(rows, "sub", 1, cores)] if split else [rows]
        total, *other = feed_forward(norm_gain, row_sets, gate, up, w_down)

        cache = jnp.swapaxes(kv_cache[0], 1, 2)
        after = other[0] if split else total
        latent_ctx = attend(queries[0], cache, cache_lengths, live_counts, after)
        own_row = rows[:1].astype(jnp.float32)
        if split:
            send, far = other
            total = total + swap(send, "sub", 1, cores).astype(jnp.float32)
            far = swap(far, "tp", direct_offset(0, 1), size).astype(jnp.float32)
            sums = [
                direct_swap(total[2 * place : 2 * place + 2].astype(jnp.bfloat16), place, size).astype(jnp.float32)
                for place in (1, 2, 3)
            ]
            own = jnp.where(lax.axis_index("sub") == 0, total[:2], 0.0) + far
            total = own + sums[0] + sums[2] + sums[1]
            total, latent_ctx = lax.optimization_barrier((total, latent_ctx))
            total = total[:1] + swap(total[1:], "sub", 1, cores)
        else:
            for step, (low, width) in enumerate(stages):
                part = total.shape[0] >> width
                sends = [total[digit * part : (digit + 1) * part] for digit in range(1, 1 << width)]
                total = total[:part]
                for digit, send in enumerate(sends, 1):
                    total = total + swap(send, "tp", digit << low, size)
        return (latent_ctx[None], (total + own_row).astype(jnp.bfloat16)[None])

    return shards


def solution(mesh):
    in_specs = (
        P(("groups", "sub"), "tp", None, None),
        P(("groups", "sub"), "tp", None, None),
        P(("groups", "sub"), "tp"),
        P(("groups", "sub"), None),
        P(("groups", "sub"), "tp", None),
        P(),
        P("tp", None),
        P("tp", None),
        P("tp", None),
    )
    out_specs = (P(("groups", "sub"), "tp", None, None), P(("groups", "sub"), "tp", None))
    return jax.shard_map(
        make_shards(mesh.shape["tp"], mesh.shape["sub"]),
        mesh=mesh,
        in_specs=in_specs,
        out_specs=out_specs,
        check_vma=False,
    )
```

```python
import jax
import jax.numpy as jnp
from jax import lax
from jax.experimental import pallas as pl
from jax.experimental.pallas import tpu as pltpu
from jax.sharding import PartitionSpec as P

KVL = 512
MIB = 1024 * 1024

score_scale = 192.0 ** (-0.5)
norm_eps = 1e-06

VMEM = pl.BlockSpec(memory_space=pltpu.VMEM)
ANY = pl.BlockSpec(memory_space=pl.ANY)


def gather_stages(bits):
    stages, top = [], bits
    while top > 1:
        width = 1 if top % 2 == 0 else 2
        top -= width
        stages.append((top, width))
    return stages


def sum_stages(bits):
    return [(low, min(2, bits - low)) for low in range(0, bits, 2)]


def direct_offset(place, core):
    near = -place & 3
    far = place ^ 6
    return near + core * (far - near)


def block_offset(position, stages):
    out = position * 0
    for low, width in stages:
        out = out | ((-position & ((1 << width) - 1)) << low)
        position = position >> width
    return out


def row_offset(position, stages):
    out = position * 0
    for low, width in stages[::-1]:
        out = out | ((position & ((1 << width) - 1)) << low)
        position = position >> width
    return out


def swap(x, axis, distance, size):
    return lax.ppermute(x, axis, [(i, i ^ distance) for i in range(size)])


def direct_swap(x, place, size):
    pairs = [(2 * i + core, 2 * (i ^ direct_offset(place, core)) + core) for i in range(size) for core in range(2)]
    return lax.ppermute(x, ("tp", "sub"), pairs)


def pinned(weight):
    return pltpu.with_memory_space_constraint(weight, pltpu.HBM)


def row_copy(source, first, target, sems, i):
    step = target.shape[0] // sems.shape[0]
    here = pl.multiple_of(i * step, step)
    return pltpu.make_async_copy(source.at[pl.ds(first + here, step)], target.at[pl.ds(here, step)], sems.at[i])


def start_pieces(copy):
    @pl.loop(0, copy[-1].shape[0])
    def _(i):
        row_copy(*copy, i).start()


def wait_pieces(copy):
    @pl.loop(0, copy[-1].shape[0])
    def _(i):
        row_copy(*copy, i).wait()


def pieces_of(rows):
    return 2 if rows % 32 == 0 else 1


def share_start(units, share):
    if share == units:
        return 0
    return pl.multiple_of(lax.axis_index("sub") * share, 16)


def pick_matrix(counts, device, size, slots, stages):
    bits = size.bit_length() - 1
    shape = (size, size // 2 * slots)
    slot = lax.broadcasted_iota(jnp.int32, shape, 1)
    every = lax.broadcasted_iota(jnp.int32, shape, 0)
    owner = block_offset(slot // slots, gather_stages(bits)) ^ device
    known = jnp.broadcast_to(counts, (8, size)).astype(jnp.bfloat16)
    start = jnp.dot(known, (every < owner).astype(jnp.bfloat16), preferred_element_type=jnp.float32)[:1]
    count = jnp.dot(known, (every == owner).astype(jnp.bfloat16), preferred_element_type=jnp.float32)[:1]
    place = (slot % slots)[:1].astype(jnp.float32)
    request = jnp.where(place < count, start + place, -1.0)
    row = lax.broadcasted_iota(jnp.int32, (2 * size, shape[1]), 0)
    wanted = row_offset(row % size, stages) ^ device ^ (row // size)
    return (request == wanted.astype(jnp.float32)).astype(jnp.bfloat16)


def attend(queries, cache, lengths, counts, after):
    slots, heads, _ = queries.shape
    positions = cache.shape[2]

    def body(lengths_ref, counts_ref, queries_ref, cache_ref, _, out_ref):
        lengths = lengths_ref[...]
        counts = counts_ref[...]
        here = lax.broadcasted_iota(jnp.int32, counts.shape, 1) == lax.axis_index("tp")
        live = jnp.sum(jnp.where(here, counts, 0), axis=1, keepdims=True)
        spot = lax.broadcasted_iota(jnp.int32, (heads, positions), 1)
        every = []
        for s in range(slots):
            scores = jnp.dot(queries_ref[s], cache_ref[s], preferred_element_type=jnp.float32) * score_scale
            every.append(jnp.where(spot < lengths[:, s : s + 1], scores, -jnp.inf))
        scores = jnp.concatenate(every, axis=0)
        weights = jnp.exp(scores - jnp.max(scores, axis=1, keepdims=True))
        probs = (weights / jnp.sum(weights, axis=1, keepdims=True)).astype(jnp.bfloat16)
        for s in range(slots):
            context = lax.dot_general(
                probs[s * heads : (s + 1) * heads],
                cache_ref[s, :KVL, :],
                (((1,), (1,)), ((), ())),
                preferred_element_type=jnp.float32,
            )
            out_ref[s] = jnp.where(s < live, context, 0.0).astype(jnp.bfloat16)

    return pl.pallas_call(
        body,
        out_shape=jax.ShapeDtypeStruct((slots, heads, KVL), jnp.bfloat16),
        in_specs=[VMEM] * 4 + [ANY],
        out_specs=VMEM,
        compiler_params=pltpu.CompilerParams(vmem_limit_bytes=8 * MIB),
        cost_estimate=pl.CostEstimate(
            flops=4 * slots * heads * positions * KVL,
            transcendentals=slots * heads * positions,
            bytes_accessed=2 * (queries.size + cache.size),
        ),
        name="attend",
    )(lengths, counts, queries, cache, after)


def load_rows(weight, share, after=None, counts=None, slots=0, stages=()):
    size = 0 if counts is None else counts.shape[1]
    units, width = weight.shape
    operands = [pinned(weight)]
    out_shape = [pltpu.VMEM((share, width), weight.dtype)]
    scratch = [pltpu.SemaphoreType.DMA((pieces_of(share),))]
    if counts is not None:
        operands.append(pinned(counts))
        out_shape.append(jax.ShapeDtypeStruct((2 * size, size // 2 * slots), jnp.bfloat16))
        scratch += [pltpu.VMEM((1, size), jnp.int32), pltpu.SemaphoreType.DMA]
    if after is not None:
        operands.append(after)

    def body(*refs):
        sources, refs = refs[: len(operands)], refs[len(operands) :]
        targets, (sems, *small_refs) = refs[: len(out_shape)], refs[len(out_shape) :]
        if counts is not None:
            small = pltpu.make_async_copy(sources[1], *small_refs)
            small.start()
        copy = (sources[0], share_start(units, share), targets[0], sems)
        start_pieces(copy)
        if counts is not None:
            small.wait()
            targets[1][...] = pick_matrix(small_refs[0][...], lax.axis_index("tp"), size, slots, stages)
        wait_pieces(copy)

    return pl.pallas_call(
        body,
        out_shape=out_shape,
        in_specs=[ANY] * len(operands),
        out_specs=[VMEM] * len(out_shape),
        scratch_shapes=scratch,
        compiler_params=pltpu.CompilerParams(vmem_limit_bytes=2 * MIB),
        cost_estimate=pl.CostEstimate(flops=0, transcendentals=0, bytes_accessed=4 * share * width),
        name="load_rows",
    )(*operands)


def compact(pick, blocks):
    size = pick.shape[0] // 2
    width = blocks[0].shape[1]
    column = 1024
    count = len(blocks)

    def body(*refs):
        pick_ref, block_refs, (own_ref, send_ref) = refs[0], refs[1 : 1 + count], refs[1 + count :]
        pick_now = pick_ref[...]
        for c in range(0, width, column):
            rows = [ref[:, c : c + column].astype(jnp.float32) for ref in block_refs]
            rows = rows[0] if count == 1 else jnp.concatenate(rows, axis=0)
            out = jnp.dot(pick_now, rows.astype(jnp.bfloat16), preferred_element_type=jnp.float32)
            own_ref[:, c : c + column] = out[:size].astype(jnp.bfloat16)
            send_ref[:, c : c + column] = out[size:].astype(jnp.bfloat16)

    out = jax.ShapeDtypeStruct((size, width), jnp.bfloat16)
    return pl.pallas_call(
        body,
        out_shape=(out, out),
        in_specs=[VMEM] * (1 + count),
        out_specs=(VMEM, VMEM),
        compiler_params=pltpu.CompilerParams(vmem_limit_bytes=16 * MIB),
        name="compact",
    )(pick, *blocks)


def feed_forward(gain, row_sets, gate, up, w_down):
    requests, width = row_sets[0].shape
    units = w_down.shape[0]
    share = gate.shape[0]
    set_count = len(row_sets)
    every = requests * set_count
    column = 512
    chunk = 192 if share % 192 == 0 else share

    outs = [jax.ShapeDtypeStruct((requests, width), jnp.float32)]
    if set_count == 2:
        outs.append(jax.ShapeDtypeStruct((requests, width), jnp.bfloat16))
        outs.append(jax.ShapeDtypeStruct((2, width), jnp.bfloat16))

    def body(*refs):
        gain_ref, refs = refs[0], refs[1:]
        set_refs, refs = refs[:set_count], refs[set_count:]
        gate_weight, up_weight, down_hbm, *refs = refs
        out_refs, refs = refs[: len(outs)], refs[len(outs) :]
        normed_ref, gate_ref, up_ref, hidden_ref, down_ref, down_sems = refs

        down_copy = (down_hbm, share_start(units, share), down_ref, down_sems)
        start_pieces(down_copy)

        rows = [ref[...].astype(jnp.float32) for ref in set_refs]
        rows = rows[0] if set_count == 1 else jnp.concatenate(rows, axis=0)
        inv_rms = lax.rsqrt(jnp.mean(rows * rows, axis=1, keepdims=True) + norm_eps)
        normed_ref[...] = (rows * inv_rms * gain_ref[...]).astype(jnp.bfloat16)

        for weight_ref, out_ref in ((gate_weight, gate_ref), (up_weight, up_ref)):
            for j in range(0, share, chunk):
                out_ref[j : j + chunk, :] = lax.dot_general(
                    weight_ref[j : j + chunk, :], normed_ref[...], (((1,), (1,)), ((), ())), preferred_element_type=jnp.float32
                )
        hidden = (jax.nn.silu(gate_ref[...]) * up_ref[...]).astype(jnp.bfloat16)
        place = lax.broadcasted_iota(jnp.int32, (every, every), 0)
        if set_count == 2:
            core = lax.axis_index("sub")
            other = place // requests
            holder = core ^ other
            spot = place % requests // 2
            flipped = jnp.where((spot == 0) & (holder == 1), 0, other)
            place = direct_offset(spot, holder) + ((place % 2) ^ flipped) * requests
        order = (lax.broadcasted_iota(jnp.int32, (every, every), 1) == place).astype(jnp.bfloat16)
        hidden_ref[...] = lax.dot_general(
            order, hidden, (((1,), (1,)), ((), ())), preferred_element_type=jnp.float32
        ).astype(jnp.bfloat16)

        wait_pieces(down_copy)
        for c in range(0, width, column):
            out = jnp.dot(hidden_ref[...], down_ref[:, c : c + column], preferred_element_type=jnp.float32)
            out_refs[0][:, c : c + column] = out[:requests]
            if set_count == 2:
                out_refs[1][:, c : c + column] = out[requests:].astype(jnp.bfloat16)
                far = jnp.where(core == 1, out[:2], out[requests : requests + 2])
                out_refs[2][:, c : c + column] = far.astype(jnp.bfloat16)

    return pl.pallas_call(
        body,
        out_shape=outs,
        in_specs=[VMEM] * (3 + set_count) + [ANY],
        out_specs=[VMEM] * len(outs),
        scratch_shapes=[
            pltpu.VMEM((every, width), jnp.bfloat16),
            pltpu.VMEM((share, every), jnp.float32),
            pltpu.VMEM((share, every), jnp.float32),
            pltpu.VMEM((every, share), jnp.bfloat16),
            pltpu.VMEM((share, width), jnp.bfloat16),
            pltpu.SemaphoreType.DMA((pieces_of(share),)),
        ],
        compiler_params=pltpu.CompilerParams(vmem_limit_bytes=24 * MIB),
        cost_estimate=pl.CostEstimate(
            flops=6 * every * share * width,
            transcendentals=every * share,
            bytes_accessed=6 * share * width,
        ),
        name="feed_forward",
    )(gain[None], *row_sets, gate, up, pinned(w_down))


def make_shards(size, cores):
    bits = size.bit_length() - 1

    def shards(queries, kv_cache, cache_lengths, live_counts, stream, norm_gain, w_gate, w_up, w_down):
        slots = queries.shape[1]
        units = w_gate.shape[0]
        split = cores == 2 and size == 8 and units % 32 == 0
        share = units // 2 if split else units
        stages = [(0, bits)] if split else sum_stages(bits)
        block = stream[0]
        for step, (low, width) in enumerate(gather_stages(bits)):
            blocks = [block] + [swap(block, "tp", digit << low, size) for digit in range((1 << width) - 1, 0, -1)]
            if step == 0:
                gate, pick = load_rows(w_gate, share, counts=live_counts, slots=slots, stages=stages)
            if low > 1:
                block = jnp.concatenate(blocks, axis=0)

        own, send = compact(pick, blocks)
        arrived = swap(send, "tp", 1, size)
        (up,) = load_rows(w_up, share, after=send)
        arrived, up = lax.optimization_barrier((arrived, up))
        rows = own + arrived
        row_sets = [rows, swap(rows, "sub", 1, cores)] if split else [rows]
        total, *other = feed_forward(norm_gain, row_sets, gate, up, w_down)

        cache = jnp.swapaxes(kv_cache[0], 1, 2)
        after = other[0] if split else total
        latent_ctx = attend(queries[0], cache, cache_lengths, live_counts, after)
        own_row = rows[:1].astype(jnp.float32)
        if split:
            send, far = other
            total = total + swap(send, "sub", 1, cores).astype(jnp.float32)
            far = swap(far, "tp", direct_offset(0, 1), size).astype(jnp.float32)
            sums = [
                direct_swap(total[2 * place : 2 * place + 2].astype(jnp.bfloat16), place, size).astype(jnp.float32)
                for place in (1, 2, 3)
            ]
            own = jnp.where(lax.axis_index("sub") == 0, total[:2], 0.0) + far
            total = own + sums[0] + sums[2] + sums[1]
            total, latent_ctx = lax.optimization_barrier((total, latent_ctx))
            total = total[:1] + swap(total[1:], "sub", 1, cores)
        else:
            for step, (low, width) in enumerate(stages):
                part = total.shape[0] >> width
                sends = [total[digit * part : (digit + 1) * part] for digit in range(1, 1 << width)]
                total = total[:part]
                for digit, send in enumerate(sends, 1):
                    total = total + swap(send, "tp", digit << low, size)
        return (latent_ctx[None], (total + own_row).astype(jnp.bfloat16)[None])

    return shards


def solution(mesh):
    in_specs = (
        P(("groups", "sub"), "tp", None, None),
        P(("groups", "sub"), "tp", None, None),
        P(("groups", "sub"), "tp"),
        P(("groups", "sub"), None),
        P(("groups", "sub"), "tp", None),
        P(),
        P("tp", None),
        P("tp", None),
        P("tp", None),
    )
    out_specs = (P(("groups", "sub"), "tp", None, None), P(("groups", "sub"), "tp", None))
    return jax.shard_map(
        make_shards(mesh.shape["tp"], mesh.shape["sub"]),
        mesh=mesh,
        in_specs=in_specs,
        out_specs=out_specs,
        check_vma=False,
    )
```

```python
import jax
import jax.numpy as jnp
from jax import lax
from jax.experimental import pallas as pl
from jax.experimental.pallas import tpu as pltpu
from jax.sharding import PartitionSpec as P

KVL = 512
MIB = 1024 * 1024

score_scale = 192.0 ** (-0.5)
norm_eps = 1e-06

VMEM = pl.BlockSpec(memory_space=pltpu.VMEM)
ANY = pl.BlockSpec(memory_space=pl.ANY)


def gather_stages(bits):
    stages, top = [], bits
    while top > 1:
        width = 1 if top % 2 == 0 else 2
        top -= width
        stages.append((top, width))
    return stages


def sum_stages(bits):
    return [(low, min(2, bits - low)) for low in range(0, bits, 2)]


def direct_offset(place, core):
    near = -place & 3
    far = place ^ 6
    return near + core * (far - near)


def block_offset(position, stages):
    out = position * 0
    for low, width in stages:
        out = out | ((-position & ((1 << width) - 1)) << low)
        position = position >> width
    return out


def row_offset(position, stages):
    out = position * 0
    for low, width in stages[::-1]:
        out = out | ((position & ((1 << width) - 1)) << low)
        position = position >> width
    return out


def swap(x, axis, distance, size):
    return lax.ppermute(x, axis, [(i, i ^ distance) for i in range(size)])


def direct_swap(x, place, size):
    pairs = [(2 * i + core, 2 * (i ^ direct_offset(place, core)) + core) for i in range(size) for core in range(2)]
    return lax.ppermute(x, ("tp", "sub"), pairs)


def pinned(weight):
    return pltpu.with_memory_space_constraint(weight, pltpu.HBM)


def row_copy(source, first, target, sems, i):
    step = target.shape[0] // sems.shape[0]
    here = pl.multiple_of(i * step, step)
    return pltpu.make_async_copy(source.at[pl.ds(first + here, step)], target.at[pl.ds(here, step)], sems.at[i])


def start_pieces(copy):
    @pl.loop(0, copy[-1].shape[0])
    def _(i):
        row_copy(*copy, i).start()


def wait_pieces(copy):
    @pl.loop(0, copy[-1].shape[0])
    def _(i):
        row_copy(*copy, i).wait()


def pieces_of(rows):
    return 2 if rows % 32 == 0 else 1


def share_start(units, share):
    if share == units:
        return 0
    return pl.multiple_of(lax.axis_index("sub") * share, 16)


def pick_matrix(counts, device, size, slots, stages):
    bits = size.bit_length() - 1
    shape = (size, size // 2 * slots)
    slot = lax.broadcasted_iota(jnp.int32, shape, 1)
    every = lax.broadcasted_iota(jnp.int32, shape, 0)
    owner = block_offset(slot // slots, gather_stages(bits)) ^ device
    known = jnp.broadcast_to(counts, (8, size)).astype(jnp.bfloat16)
    start = jnp.dot(known, (every < owner).astype(jnp.bfloat16), preferred_element_type=jnp.float32)[:1]
    count = jnp.dot(known, (every == owner).astype(jnp.bfloat16), preferred_element_type=jnp.float32)[:1]
    place = (slot % slots)[:1].astype(jnp.float32)
    request = jnp.where(place < count, start + place, -1.0)
    row = lax.broadcasted_iota(jnp.int32, (2 * size, shape[1]), 0)
    wanted = row_offset(row % size, stages) ^ device ^ (row // size)
    return (request == wanted.astype(jnp.float32)).astype(jnp.bfloat16)


def attend(queries, cache, lengths, counts, after):
    slots, heads, _ = queries.shape
    positions = cache.shape[2]

    def body(lengths_ref, counts_ref, queries_ref, cache_ref, _, out_ref):
        lengths = lengths_ref[...]
        counts = counts_ref[...]
        here = lax.broadcasted_iota(jnp.int32, counts.shape, 1) == lax.axis_index("tp")
        live = jnp.sum(jnp.where(here, counts, 0), axis=1, keepdims=True)
        spot = lax.broadcasted_iota(jnp.int32, (heads, positions), 1)
        every = []
        for s in range(slots):
            scores = jnp.dot(queries_ref[s], cache_ref[s], preferred_element_type=jnp.float32) * score_scale
            every.append(jnp.where(spot < lengths[:, s : s + 1], scores, -jnp.inf))
        scores = jnp.concatenate(every, axis=0)
        weights = jnp.exp(scores - jnp.max(scores, axis=1, keepdims=True))
        probs = (weights / jnp.sum(weights, axis=1, keepdims=True)).astype(jnp.bfloat16)
        for s in range(slots):
            context = lax.dot_general(
                probs[s * heads : (s + 1) * heads],
                cache_ref[s, :KVL, :],
                (((1,), (1,)), ((), ())),
                preferred_element_type=jnp.float32,
            )
            out_ref[s] = jnp.where(s < live, context, 0.0).astype(jnp.bfloat16)

    return pl.pallas_call(
        body,
        out_shape=jax.ShapeDtypeStruct((slots, heads, KVL), jnp.bfloat16),
        in_specs=[VMEM] * 4 + [ANY],
        out_specs=VMEM,
        compiler_params=pltpu.CompilerParams(vmem_limit_bytes=8 * MIB),
        cost_estimate=pl.CostEstimate(
            flops=4 * slots * heads * positions * KVL,
            transcendentals=slots * heads * positions,
            bytes_accessed=2 * (queries.size + cache.size),
        ),
        name="attend",
    )(lengths, counts, queries, cache, after)


def load_rows(weight, share, after=None, counts=None, slots=0, stages=()):
    size = 0 if counts is None else counts.shape[1]
    units, width = weight.shape
    operands = [pinned(weight)]
    out_shape = [pltpu.VMEM((share, width), weight.dtype)]
    scratch = [pltpu.SemaphoreType.DMA((pieces_of(share),))]
    if counts is not None:
        operands.append(pinned(counts))
        out_shape.append(jax.ShapeDtypeStruct((2 * size, size // 2 * slots), jnp.bfloat16))
        scratch += [pltpu.VMEM((1, size), jnp.int32), pltpu.SemaphoreType.DMA]
    if after is not None:
        operands.append(after)

    def body(*refs):
        sources, refs = refs[: len(operands)], refs[len(operands) :]
        targets, (sems, *small_refs) = refs[: len(out_shape)], refs[len(out_shape) :]
        if counts is not None:
            small = pltpu.make_async_copy(sources[1], *small_refs)
            small.start()
        copy = (sources[0], share_start(units, share), targets[0], sems)
        start_pieces(copy)
        if counts is not None:
            small.wait()
            targets[1][...] = pick_matrix(small_refs[0][...], lax.axis_index("tp"), size, slots, stages)
        wait_pieces(copy)

    return pl.pallas_call(
        body,
        out_shape=out_shape,
        in_specs=[ANY] * len(operands),
        out_specs=[VMEM] * len(out_shape),
        scratch_shapes=scratch,
        compiler_params=pltpu.CompilerParams(vmem_limit_bytes=2 * MIB),
        cost_estimate=pl.CostEstimate(flops=0, transcendentals=0, bytes_accessed=4 * share * width),
        name="load_rows",
    )(*operands)


def compact(pick, blocks):
    size = pick.shape[0] // 2
    width = blocks[0].shape[1]
    column = 1024
    count = len(blocks)

    def body(*refs):
        pick_ref, block_refs, (own_ref, send_ref) = refs[0], refs[1 : 1 + count], refs[1 + count :]
        pick_now = pick_ref[...]
        for c in range(0, width, column):
            rows = [ref[:, c : c + column].astype(jnp.float32) for ref in block_refs]
            rows = rows[0] if count == 1 else jnp.concatenate(rows, axis=0)
            out = jnp.dot(pick_now, rows.astype(jnp.bfloat16), preferred_element_type=jnp.float32)
            own_ref[:, c : c + column] = out[:size].astype(jnp.bfloat16)
            send_ref[:, c : c + column] = out[size:].astype(jnp.bfloat16)

    out = jax.ShapeDtypeStruct((size, width), jnp.bfloat16)
    return pl.pallas_call(
        body,
        out_shape=(out, out),
        in_specs=[VMEM] * (1 + count),
        out_specs=(VMEM, VMEM),
        compiler_params=pltpu.CompilerParams(vmem_limit_bytes=16 * MIB),
        name="compact",
    )(pick, *blocks)


def normalize(rows, gain):
    inv_rms = lax.rsqrt(jnp.mean(rows * rows, axis=1, keepdims=True) + norm_eps)
    return (rows * inv_rms * gain).astype(jnp.bfloat16)


def normalized(rows, gain):
    def body(rows_ref, gain_ref, out_ref):
        out_ref[...] = normalize(rows_ref[...].astype(jnp.float32), gain_ref[...])

    return pl.pallas_call(
        body,
        out_shape=jax.ShapeDtypeStruct(rows.shape, jnp.bfloat16),
        in_specs=[VMEM] * 2,
        out_specs=VMEM,
        compiler_params=pltpu.CompilerParams(vmem_limit_bytes=16 * MIB),
        name="normalized",
    )(rows, gain[None])


def feed_forward(gain, row_sets, gate, up, w_down):
    requests, width = row_sets[0].shape
    units = w_down.shape[0]
    share = gate.shape[0]
    set_count = len(row_sets)
    every = requests * set_count
    column = 512
    chunk = 192 if share % 192 == 0 else share

    outs = [jax.ShapeDtypeStruct((requests, width), jnp.float32)]
    if set_count == 2:
        outs.append(jax.ShapeDtypeStruct((requests, width), jnp.bfloat16))
        outs.append(jax.ShapeDtypeStruct((2, width), jnp.bfloat16))

    def body(*refs):
        gain_ref, refs = refs[0], refs[1:]
        set_refs, refs = refs[:set_count], refs[set_count:]
        gate_weight, up_weight, down_hbm, *refs = refs
        out_refs, refs = refs[: len(outs)], refs[len(outs) :]
        normed_ref, gate_ref, up_ref, hidden_ref, down_ref, down_sems = refs

        down_copy = (down_hbm, share_start(units, share), down_ref, down_sems)
        start_pieces(down_copy)

        rows = [set_refs[0][...].astype(jnp.float32)]
        for ref in set_refs[1:]:
            rows.append(normalize(ref[...].astype(jnp.float32), gain_ref[...]).astype(jnp.float32))
        rows = rows[0] if set_count == 1 else jnp.concatenate(rows, axis=0)
        normed_ref[...] = rows.astype(jnp.bfloat16)

        for weight_ref, out_ref in ((gate_weight, gate_ref), (up_weight, up_ref)):
            for j in range(0, share, chunk):
                out_ref[j : j + chunk, :] = lax.dot_general(
                    weight_ref[j : j + chunk, :], normed_ref[...], (((1,), (1,)), ((), ())), preferred_element_type=jnp.float32
                )
        hidden = (jax.nn.silu(gate_ref[...]) * up_ref[...]).astype(jnp.bfloat16)
        place = lax.broadcasted_iota(jnp.int32, (every, every), 0)
        if set_count == 2:
            core = lax.axis_index("sub")
            other = place // requests
            holder = core ^ other
            spot = place % requests // 2
            flipped = jnp.where((spot == 0) & (holder == 1), 0, other)
            place = direct_offset(spot, holder) + ((place % 2) ^ flipped) * requests
        order = (lax.broadcasted_iota(jnp.int32, (every, every), 1) == place).astype(jnp.bfloat16)
        hidden_ref[...] = lax.dot_general(
            order, hidden, (((1,), (1,)), ((), ())), preferred_element_type=jnp.float32
        ).astype(jnp.bfloat16)

        wait_pieces(down_copy)
        for c in range(0, width, column):
            out = jnp.dot(hidden_ref[...], down_ref[:, c : c + column], preferred_element_type=jnp.float32)
            out_refs[0][:, c : c + column] = out[:requests]
            if set_count == 2:
                out_refs[1][:, c : c + column] = out[requests:].astype(jnp.bfloat16)
                far = jnp.where(core == 1, out[:2], out[requests : requests + 2])
                out_refs[2][:, c : c + column] = far.astype(jnp.bfloat16)

    return pl.pallas_call(
        body,
        out_shape=outs,
        in_specs=[VMEM] * (3 + set_count) + [ANY],
        out_specs=[VMEM] * len(outs),
        scratch_shapes=[
            pltpu.VMEM((every, width), jnp.bfloat16),
            pltpu.VMEM((share, every), jnp.float32),
            pltpu.VMEM((share, every), jnp.float32),
            pltpu.VMEM((every, share), jnp.bfloat16),
            pltpu.VMEM((share, width), jnp.bfloat16),
            pltpu.SemaphoreType.DMA((pieces_of(share),)),
        ],
        compiler_params=pltpu.CompilerParams(vmem_limit_bytes=24 * MIB),
        cost_estimate=pl.CostEstimate(
            flops=6 * every * share * width,
            transcendentals=every * share,
            bytes_accessed=6 * share * width,
        ),
        name="feed_forward",
    )(gain[None], *row_sets, gate, up, pinned(w_down))


def make_shards(size, cores):
    bits = size.bit_length() - 1

    def shards(queries, kv_cache, cache_lengths, live_counts, stream, norm_gain, w_gate, w_up, w_down):
        slots = queries.shape[1]
        units = w_gate.shape[0]
        split = cores == 2 and size == 8 and units % 32 == 0
        share = units // 2 if split else units
        stages = [(0, bits)] if split else sum_stages(bits)
        block = stream[0]
        for step, (low, width) in enumerate(gather_stages(bits)):
            blocks = [block] + [swap(block, "tp", digit << low, size) for digit in range((1 << width) - 1, 0, -1)]
            if step == 0:
                gate, pick = load_rows(w_gate, share, counts=live_counts, slots=slots, stages=stages)
            if low > 1:
                block = jnp.concatenate(blocks, axis=0)

        own, send = compact(pick, blocks)
        arrived = swap(send, "tp", 1, size)
        (up,) = load_rows(w_up, share, after=send)
        arrived, up = lax.optimization_barrier((arrived, up))
        rows = own + arrived
        row_sets = [normalized(rows, norm_gain)]
        if split:
            row_sets.append(swap(rows, "sub", 1, cores))
        total, *other = feed_forward(norm_gain, row_sets, gate, up, w_down)

        cache = jnp.swapaxes(kv_cache[0], 1, 2)
        after = other[0] if split else total
        latent_ctx = attend(queries[0], cache, cache_lengths, live_counts, after)
        own_row = rows[:1].astype(jnp.float32)
        if split:
            send, far = other
            total = total + swap(send, "sub", 1, cores).astype(jnp.float32)
            far = swap(far, "tp", direct_offset(0, 1), size).astype(jnp.float32)
            sums = [
                direct_swap(total[2 * place : 2 * place + 2].astype(jnp.bfloat16), place, size).astype(jnp.float32)
                for place in (1, 2, 3)
            ]
            own = jnp.where(lax.axis_index("sub") == 0, total[:2], 0.0) + far
            total = own + sums[0] + sums[2] + sums[1]
            total, latent_ctx = lax.optimization_barrier((total, latent_ctx))
            total = total[:1] + swap(total[1:], "sub", 1, cores)
        else:
            for step, (low, width) in enumerate(stages):
                part = total.shape[0] >> width
                sends = [total[digit * part : (digit + 1) * part] for digit in range(1, 1 << width)]
                total = total[:part]
                for digit, send in enumerate(sends, 1):
                    total = total + swap(send, "tp", digit << low, size)
        return (latent_ctx[None], (total + own_row).astype(jnp.bfloat16)[None])

    return shards


def solution(mesh):
    in_specs = (
        P(("groups", "sub"), "tp", None, None),
        P(("groups", "sub"), "tp", None, None),
        P(("groups", "sub"), "tp"),
        P(("groups", "sub"), None),
        P(("groups", "sub"), "tp", None),
        P(),
        P("tp", None),
        P("tp", None),
        P("tp", None),
    )
    out_specs = (P(("groups", "sub"), "tp", None, None), P(("groups", "sub"), "tp", None))
    return jax.shard_map(
        make_shards(mesh.shape["tp"], mesh.shape["sub"]),
        mesh=mesh,
        in_specs=in_specs,
        out_specs=out_specs,
        check_vma=False,
    )
```

```python
import jax
import jax.numpy as jnp
from jax import lax
from jax.experimental import pallas as pl
from jax.experimental.pallas import tpu as pltpu
from jax.sharding import PartitionSpec as P

KVL = 512
MIB = 1024 * 1024

score_scale = 192.0 ** (-0.5)
norm_eps = 1e-06

VMEM = pl.BlockSpec(memory_space=pltpu.VMEM)
ANY = pl.BlockSpec(memory_space=pl.ANY)


def gather_stages(bits):
    stages, top = [], bits
    while top > 1:
        width = 1 if top % 2 == 0 else 2
        top -= width
        stages.append((top, width))
    return stages


def sum_stages(bits):
    return [(low, min(2, bits - low)) for low in range(0, bits, 2)]


def direct_offset(place, core):
    near = -place & 3
    far = place ^ 6
    return near + core * (far - near)


def block_offset(position, stages):
    out = position * 0
    for low, width in stages:
        out = out | ((-position & ((1 << width) - 1)) << low)
        position = position >> width
    return out


def row_offset(position, stages):
    out = position * 0
    for low, width in stages[::-1]:
        out = out | ((position & ((1 << width) - 1)) << low)
        position = position >> width
    return out


def swap(x, axis, distance, size):
    return lax.ppermute(x, axis, [(i, i ^ distance) for i in range(size)])


def direct_swap(x, place, size):
    pairs = [(2 * i + core, 2 * (i ^ direct_offset(place, core)) + core) for i in range(size) for core in range(2)]
    return lax.ppermute(x, ("tp", "sub"), pairs)


def pinned(weight):
    return pltpu.with_memory_space_constraint(weight, pltpu.HBM)


def row_copy(source, first, target, sems, i):
    step = target.shape[0] // sems.shape[0]
    here = pl.multiple_of(i * step, step)
    return pltpu.make_async_copy(source.at[pl.ds(first + here, step)], target.at[pl.ds(here, step)], sems.at[i])


def start_pieces(copy):
    @pl.loop(0, copy[-1].shape[0])
    def _(i):
        row_copy(*copy, i).start()


def wait_pieces(copy):
    @pl.loop(0, copy[-1].shape[0])
    def _(i):
        row_copy(*copy, i).wait()


def pieces_of(rows):
    return 2 if rows % 32 == 0 else 1


def share_start(units, share):
    if share == units:
        return 0
    return pl.multiple_of(lax.axis_index("sub") * share, 16)


def pick_matrix(counts, device, size, slots, stages):
    bits = size.bit_length() - 1
    shape = (size, size // 2 * slots)
    slot = lax.broadcasted_iota(jnp.int32, shape, 1)
    every = lax.broadcasted_iota(jnp.int32, shape, 0)
    owner = block_offset(slot // slots, gather_stages(bits)) ^ device
    known = jnp.broadcast_to(counts, (8, size)).astype(jnp.bfloat16)
    start = jnp.dot(known, (every < owner).astype(jnp.bfloat16), preferred_element_type=jnp.float32)[:1]
    count = jnp.dot(known, (every == owner).astype(jnp.bfloat16), preferred_element_type=jnp.float32)[:1]
    place = (slot % slots)[:1].astype(jnp.float32)
    request = jnp.where(place < count, start + place, -1.0)
    row = lax.broadcasted_iota(jnp.int32, (2 * size, shape[1]), 0)
    wanted = row_offset(row % size, stages) ^ device ^ (row // size)
    return (request == wanted.astype(jnp.float32)).astype(jnp.bfloat16)


def attend(queries, cache, lengths, counts, after):
    slots, heads, _ = queries.shape
    positions = cache.shape[2]

    def body(lengths_ref, counts_ref, queries_ref, cache_ref, _, out_ref):
        lengths = lengths_ref[...]
        counts = counts_ref[...]
        here = lax.broadcasted_iota(jnp.int32, counts.shape, 1) == lax.axis_index("tp")
        live = jnp.sum(jnp.where(here, counts, 0), axis=1, keepdims=True)
        spot = lax.broadcasted_iota(jnp.int32, (heads, positions), 1)
        every = []
        for s in range(slots):
            scores = jnp.dot(queries_ref[s], cache_ref[s], preferred_element_type=jnp.float32) * score_scale
            every.append(jnp.where(spot < lengths[:, s : s + 1], scores, -jnp.inf))
        scores = jnp.concatenate(every, axis=0)
        weights = jnp.exp(scores - jnp.max(scores, axis=1, keepdims=True))
        probs = (weights / jnp.sum(weights, axis=1, keepdims=True)).astype(jnp.bfloat16)
        for s in range(slots):
            context = lax.dot_general(
                probs[s * heads : (s + 1) * heads],
                cache_ref[s, :KVL, :],
                (((1,), (1,)), ((), ())),
                preferred_element_type=jnp.float32,
            )
            out_ref[s] = jnp.where(s < live, context, 0.0).astype(jnp.bfloat16)

    return pl.pallas_call(
        body,
        out_shape=jax.ShapeDtypeStruct((slots, heads, KVL), jnp.bfloat16),
        in_specs=[VMEM] * 4 + [ANY],
        out_specs=VMEM,
        compiler_params=pltpu.CompilerParams(vmem_limit_bytes=8 * MIB),
        cost_estimate=pl.CostEstimate(
            flops=4 * slots * heads * positions * KVL,
            transcendentals=slots * heads * positions,
            bytes_accessed=2 * (queries.size + cache.size),
        ),
        name="attend",
    )(lengths, counts, queries, cache, after)


def load_rows(weight, share, after=None, counts=None, slots=0, stages=()):
    size = 0 if counts is None else counts.shape[1]
    units, width = weight.shape
    operands = [pinned(weight)]
    out_shape = [pltpu.VMEM((share, width), weight.dtype)]
    scratch = [pltpu.SemaphoreType.DMA((pieces_of(share),))]
    if counts is not None:
        operands.append(pinned(counts))
        out_shape.append(jax.ShapeDtypeStruct((2 * size, size // 2 * slots), jnp.bfloat16))
        scratch += [pltpu.VMEM((1, size), jnp.int32), pltpu.SemaphoreType.DMA]
    if after is not None:
        operands.append(after)

    def body(*refs):
        sources, refs = refs[: len(operands)], refs[len(operands) :]
        targets, (sems, *small_refs) = refs[: len(out_shape)], refs[len(out_shape) :]
        if counts is not None:
            small = pltpu.make_async_copy(sources[1], *small_refs)
            small.start()
        copy = (sources[0], share_start(units, share), targets[0], sems)
        start_pieces(copy)
        if counts is not None:
            small.wait()
            targets[1][...] = pick_matrix(small_refs[0][...], lax.axis_index("tp"), size, slots, stages)
        wait_pieces(copy)

    return pl.pallas_call(
        body,
        out_shape=out_shape,
        in_specs=[ANY] * len(operands),
        out_specs=[VMEM] * len(out_shape),
        scratch_shapes=scratch,
        compiler_params=pltpu.CompilerParams(vmem_limit_bytes=2 * MIB),
        cost_estimate=pl.CostEstimate(flops=0, transcendentals=0, bytes_accessed=4 * share * width),
        name="load_rows",
    )(*operands)


def compact(pick, blocks):
    size = pick.shape[0] // 2
    width = blocks[0].shape[1]
    column = 1024
    count = len(blocks)

    def body(*refs):
        pick_ref, block_refs, (own_ref, send_ref) = refs[0], refs[1 : 1 + count], refs[1 + count :]
        pick_now = pick_ref[...]
        for c in range(0, width, column):
            rows = [ref[:, c : c + column].astype(jnp.float32) for ref in block_refs]
            rows = rows[0] if count == 1 else jnp.concatenate(rows, axis=0)
            out = jnp.dot(pick_now, rows.astype(jnp.bfloat16), preferred_element_type=jnp.float32)
            own_ref[:, c : c + column] = out[:size].astype(jnp.bfloat16)
            send_ref[:, c : c + column] = out[size:].astype(jnp.bfloat16)

    out = jax.ShapeDtypeStruct((size, width), jnp.bfloat16)
    return pl.pallas_call(
        body,
        out_shape=(out, out),
        in_specs=[VMEM] * (1 + count),
        out_specs=(VMEM, VMEM),
        compiler_params=pltpu.CompilerParams(vmem_limit_bytes=16 * MIB),
        name="compact",
    )(pick, *blocks)


def normalize(rows, gain):
    inv_rms = lax.rsqrt(jnp.mean(rows * rows, axis=1, keepdims=True) + norm_eps)
    return (rows * inv_rms * gain).astype(jnp.bfloat16)


def normalized(rows, gain):
    def body(rows_ref, gain_ref, out_ref):
        out_ref[...] = normalize(rows_ref[...].astype(jnp.float32), gain_ref[...])

    return pl.pallas_call(
        body,
        out_shape=jax.ShapeDtypeStruct(rows.shape, jnp.bfloat16),
        in_specs=[VMEM] * 2,
        out_specs=VMEM,
        compiler_params=pltpu.CompilerParams(vmem_limit_bytes=16 * MIB),
        name="normalized",
    )(rows, gain[None])


def feed_forward(gain, row_sets, gate, up, w_down):
    requests, width = row_sets[0].shape
    units = w_down.shape[0]
    share = gate.shape[0]
    set_count = len(row_sets)
    every = requests * set_count
    column = 512
    chunk = 192 if share % 192 == 0 else share

    outs = [jax.ShapeDtypeStruct((requests, width), jnp.float32)]
    if set_count == 2:
        outs.append(jax.ShapeDtypeStruct((requests, width), jnp.bfloat16))
        outs.append(jax.ShapeDtypeStruct((2, width), jnp.bfloat16))

    def body(*refs):
        gain_ref, refs = refs[0], refs[1:]
        set_refs, refs = refs[:set_count], refs[set_count:]
        gate_weight, up_weight, down_hbm, *refs = refs
        out_refs, refs = refs[: len(outs)], refs[len(outs) :]
        normed_ref, gate_ref, up_ref, hidden_ref, down_ref, down_sems = refs

        down_copy = (down_hbm, share_start(units, share), down_ref, down_sems)
        start_pieces(down_copy)

        rows = [set_refs[0][...].astype(jnp.float32)]
        for ref in set_refs[1:]:
            rows.append(normalize(ref[...].astype(jnp.float32), gain_ref[...]).astype(jnp.float32))
        rows = rows[0] if set_count == 1 else jnp.concatenate(rows, axis=0)
        normed_ref[...] = rows.astype(jnp.bfloat16)

        for weight_ref, out_ref in ((gate_weight, gate_ref), (up_weight, up_ref)):
            for j in range(0, share, chunk):
                out_ref[j : j + chunk, :] = lax.dot_general(
                    weight_ref[j : j + chunk, :], normed_ref[...], (((1,), (1,)), ((), ())), preferred_element_type=jnp.float32
                )
        wait_pieces(down_copy)

        hidden = (jax.nn.silu(gate_ref[...]) * up_ref[...]).astype(jnp.bfloat16)
        place = lax.broadcasted_iota(jnp.int32, (every, every), 0)
        if set_count == 2:
            core = lax.axis_index("sub")
            other = place // requests
            holder = core ^ other
            spot = place % requests // 2
            flipped = jnp.where((spot == 0) & (holder == 1), 0, other)
            place = direct_offset(spot, holder) + ((place % 2) ^ flipped) * requests
        order = (lax.broadcasted_iota(jnp.int32, (every, every), 1) == place).astype(jnp.bfloat16)
        hidden_ref[...] = lax.dot_general(
            order, hidden, (((1,), (1,)), ((), ())), preferred_element_type=jnp.float32
        ).astype(jnp.bfloat16)
        for c in range(0, width, column):
            out = jnp.dot(hidden_ref[...], down_ref[:, c : c + column], preferred_element_type=jnp.float32)
            out_refs[0][:, c : c + column] = out[:requests]
            if set_count == 2:
                out_refs[1][:, c : c + column] = out[requests:].astype(jnp.bfloat16)
                far = jnp.where(core == 1, out[:2], out[requests : requests + 2])
                out_refs[2][:, c : c + column] = far.astype(jnp.bfloat16)

    return pl.pallas_call(
        body,
        out_shape=outs,
        in_specs=[VMEM] * (3 + set_count) + [ANY],
        out_specs=[VMEM] * len(outs),
        scratch_shapes=[
            pltpu.VMEM((every, width), jnp.bfloat16),
            pltpu.VMEM((share, every), jnp.float32),
            pltpu.VMEM((share, every), jnp.float32),
            pltpu.VMEM((every, share), jnp.bfloat16),
            pltpu.VMEM((share, width), jnp.bfloat16),
            pltpu.SemaphoreType.DMA((pieces_of(share),)),
        ],
        compiler_params=pltpu.CompilerParams(vmem_limit_bytes=24 * MIB),
        cost_estimate=pl.CostEstimate(
            flops=6 * every * share * width,
            transcendentals=every * share,
            bytes_accessed=6 * share * width,
        ),
        name="feed_forward",
    )(gain[None], *row_sets, gate, up, pinned(w_down))


def make_shards(size, cores):
    bits = size.bit_length() - 1

    def shards(queries, kv_cache, cache_lengths, live_counts, stream, norm_gain, w_gate, w_up, w_down):
        slots = queries.shape[1]
        units = w_gate.shape[0]
        split = cores == 2 and size == 8 and units % 32 == 0
        share = units // 2 if split else units
        stages = [(0, bits)] if split else sum_stages(bits)
        block = stream[0]
        for step, (low, width) in enumerate(gather_stages(bits)):
            blocks = [block] + [swap(block, "tp", digit << low, size) for digit in range((1 << width) - 1, 0, -1)]
            if step == 0:
                gate, pick = load_rows(w_gate, share, counts=live_counts, slots=slots, stages=stages)
            if low > 1:
                block = jnp.concatenate(blocks, axis=0)

        own, send = compact(pick, blocks)
        arrived = swap(send, "tp", 1, size)
        (up,) = load_rows(w_up, share, after=send)
        arrived, up = lax.optimization_barrier((arrived, up))
        rows = own + arrived
        row_sets = [normalized(rows, norm_gain)]
        if split:
            row_sets.append(swap(rows, "sub", 1, cores))
        total, *other = feed_forward(norm_gain, row_sets, gate, up, w_down)

        cache = jnp.swapaxes(kv_cache[0], 1, 2)
        after = other[0] if split else total
        latent_ctx = attend(queries[0], cache, cache_lengths, live_counts, after)
        own_row = rows[:1].astype(jnp.float32)
        if split:
            send, far = other
            total = total + swap(send, "sub", 1, cores).astype(jnp.float32)
            far = swap(far, "tp", direct_offset(0, 1), size).astype(jnp.float32)
            sums = [
                direct_swap(total[2 * place : 2 * place + 2].astype(jnp.bfloat16), place, size).astype(jnp.float32)
                for place in (1, 2, 3)
            ]
            own = jnp.where(lax.axis_index("sub") == 0, total[:2], 0.0) + far
            total = own + sums[0] + sums[2] + sums[1]
            total, latent_ctx = lax.optimization_barrier((total, latent_ctx))
            total = total[:1] + swap(total[1:], "sub", 1, cores)
        else:
            for step, (low, width) in enumerate(stages):
                part = total.shape[0] >> width
                sends = [total[digit * part : (digit + 1) * part] for digit in range(1, 1 << width)]
                total = total[:part]
                for digit, send in enumerate(sends, 1):
                    total = total + swap(send, "tp", digit << low, size)
        return (latent_ctx[None], (total + own_row).astype(jnp.bfloat16)[None])

    return shards


def solution(mesh):
    in_specs = (
        P(("groups", "sub"), "tp", None, None),
        P(("groups", "sub"), "tp", None, None),
        P(("groups", "sub"), "tp"),
        P(("groups", "sub"), None),
        P(("groups", "sub"), "tp", None),
        P(),
        P("tp", None),
        P("tp", None),
        P("tp", None),
    )
    out_specs = (P(("groups", "sub"), "tp", None, None), P(("groups", "sub"), "tp", None))
    return jax.shard_map(
        make_shards(mesh.shape["tp"], mesh.shape["sub"]),
        mesh=mesh,
        in_specs=in_specs,
        out_specs=out_specs,
        check_vma=False,
    )
```
